32 devices in a mesh: replica: 8 (over y, x, core), group: 4 (over z).
Axes of the slice: x: 2, y: 2, z: 4, core: 2. Of those that a mesh axis runs over, the one named last changes fastest.
Arguments:
- tokens: bfloat16 [8, 1024, 2048], P('replica', 'group'), may hold values from -6 to 6
- cotangent: bfloat16 [8, 1024, 2048], P('replica', 'group'), may hold values from -6 to 6
- doc_start: int32 [8, 1024], P('replica', 'group'), may hold values from 0 to 1023, as said below
- norm_gain: bfloat16 [2048], P('group'), may hold values from 0.099609375 to 1.8984375
- qkv_weight: bfloat16 [2048, 6144], P('group'), may hold values from -0.125 to 0.125
- conv_weight: bfloat16 [6144, 4], P('group'), may hold values from -3 to 3
- beta_weight: bfloat16 [2048, 16], P('group'), may hold values from -0.125 to 0.125
- head_gain: bfloat16 [128], replicated, may hold values from 0.099609375 to 1.8984375
- out_weight: bfloat16 [2048, 2048], P('group'), may hold values from -0.125 to 0.125
- ffn_gain: bfloat16 [2048], P('group'), may hold values from 0.099609375 to 1.8984375
- gate_up_weight: bfloat16 [2048, 11264], P('group'), may hold values from -0.125 to 0.125
- down_weight: bfloat16 [5632, 2048], P('group'), may hold values from -0.078125 to 0.078125
Outputs:
- output: bfloat16 [8, 1024, 2048], P('replica', 'group')
- input_grad: float32 [8, 1024, 2048], P('replica', 'group')
- norm_gain_grad: float32 [2048], P('group')
- qkv_grad: float32 [2048, 6144], P('group')
- conv_grad: float32 [6144, 4], P('group')
- beta_grad: float32 [2048, 16], P('group')
- head_gain_grad: float32 [128], replicated
- out_grad: float32 [2048, 2048], P('group')
- ffn_gain_grad: float32 [2048], P('group')
- gate_up_grad: float32 [2048, 11264], P('group')
- down_grad: float32 [5632, 2048], P('group')
The draws below stay inside these ranges and needn't reach their ends.
Inputs may be any that keep to these rules, and one draw needn't show every extreme that they name: doc_start never falls along a sequence and at each position equals that position or the previous token's value; in each aligned pair of sequences (rows 2k and 2k + 1) one, drawn from the seed, is a single document, and in the other the last token starts a document of its own.
All inputs are finite; a program needn't handle non-finite values.
Results may differ from the reference program's by a relative error of at most 0.02.
Values may be sent and summed in bfloat16 or wider, within the bound.
No kernel may reach another device: no remote copies, remote signals or barrier semaphores. Data moves between devices by JAX's collectives and lax.ppermute only.
A program may use at most 512 MiB of HBM per device.

```python
import math
from functools import partial
import jax
import jax.numpy as jnp
from jax import lax

D = 2048
HEADS = 16
HEAD_DIM = 128
FF = 5632
CONV = 4
STRETCH = 64
LEN = 1024
SEQS = 8


def draw_doc_start(key, part):
    key = jax.random.fold_in(key, 7)
    key_rate, key_hits, key_whole = jax.random.split(key, 3)
    rate_table = jnp.array([8, 32, 128, 512], jnp.int32)
    rate_pick = jax.random.randint(key_rate, (SEQS,), 0, 4)
    seq_rate = jnp.sum(jnp.where(rate_pick[:, None] == jnp.arange(4, dtype=jnp.int32)[None, :], rate_table[None, :], 0), axis=1)
    start_hits = jax.random.randint(key_hits, (SEQS, LEN), 0, 1 << 20) % seq_rate[:, None] == 0
    whole_pick = jax.random.randint(key_whole, (SEQS // 2,), 0, 2)
    seq_index = jnp.arange(SEQS, dtype=jnp.int32)
    single_doc = seq_index % 2 == jnp.repeat(whole_pick, 2)
    positions = jnp.arange(LEN, dtype=jnp.int32)
    start_hits = start_hits | (positions[None, :] == LEN - 1)
    doc_starts = start_hits & (positions[None, :] > 0) & jnp.logical_not(single_doc)[:, None]
    return lax.cummax(jnp.where(doc_starts, positions[None, :], 0), axis=1).astype(jnp.int32)


def levels(key, extent, cuts, least, top_value):
    loudness = 1.0
    for dim, parts in cuts:
        steps = jax.random.uniform(jax.random.fold_in(jax.random.fold_in(key, 6), dim), (parts,), jnp.float32, least / len(cuts), top_value / len(cuts))
        loudness = loudness * jnp.repeat(jnp.exp(steps), extent[dim] // parts).reshape((-1,) + (1,) * (len(extent) - 1 - dim))
    return loudness


def scatter_about(key, dims, scale, bound, cuts=(), kind=jnp.bfloat16):
    drawn = jax.random.normal(key, dims, jnp.float32) * scale
    if len(cuts) > 0:
        drawn = levels(key, dims, cuts, -0.22, 0.18) * drawn
    return jnp.clip(drawn, min=-bound, max=bound).astype(kind)


def setup_inputs(seed: int = 0) -> dict:
    splits = jax.random.split(jax.random.key(seed), 13)
    tokens = scatter_about(splits[0], (SEQS, LEN, D), 1.0, 6.0, ((0, 8), (1, 4)))
    cotangent = scatter_about(splits[1], (SEQS, LEN, D), 1.0, 6.0, ((0, 8), (1, 4)))
    doc_start = draw_doc_start(jax.random.fold_in(splits[12], 71), 0)
    norm_gain = jnp.clip(1.0 + 0.18 * jax.random.normal(splits[3], (D,), jnp.float32), 0.099609375, 1.8984375).astype(jnp.bfloat16)
    qkv_weight = scatter_about(splits[4], (D, 3 * D), D ** -0.5, 0.125, ((0, 4),))
    conv_weight = scatter_about(splits[5], (3 * D, CONV), 0.5, 3.0, ((0, 4),))
    beta_weight = scatter_about(splits[6], (D, HEADS), D ** -0.5, 0.125, ((0, 4),))
    head_gain = jnp.clip(1.0 + 0.18 * jax.random.normal(splits[7], (HEAD_DIM,), jnp.float32), 0.099609375, 1.8984375).astype(jnp.bfloat16)
    out_weight = scatter_about(splits[8], (D, D), D ** -0.5, 0.125, ((0, 4),))
    ffn_gain = jnp.clip(1.0 + 0.18 * jax.random.normal(splits[9], (D,), jnp.float32), 0.099609375, 1.8984375).astype(jnp.bfloat16)
    gate_up_weight = scatter_about(splits[10], (D, 2 * FF), D ** -0.5, 0.125, ((0, 4),))
    down_weight = scatter_about(splits[11], (FF, D), FF ** -0.5, 0.078125, ((0, 4),))
    return {"tokens": tokens, "cotangent": cotangent, "doc_start": doc_start, "norm_gain": norm_gain, "qkv_weight": qkv_weight, "conv_weight": conv_weight, "beta_weight": beta_weight, "head_gain": head_gain, "out_weight": out_weight, "ffn_gain": ffn_gain, "gate_up_weight": gate_up_weight, "down_weight": down_weight}


EPS = 1e-06
HIGH = lax.Precision.HIGHEST

@jax.custom_vjp
def low(v):
    return lax.optimization_barrier(v.astype(jnp.bfloat16)).astype(jnp.float32)

@jax.custom_vjp
def low_back(v):
    return v

def low_keep(v):
    return (low(v), None)

def low_pass(kept, grad):
    return (grad,)

def back_keep(v):
    return (v, None)

def back_low(kept, grad):
    return (low(grad),)
low.defvjp(low_keep, low_pass)
low_back.defvjp(back_keep, back_low)

def norm_rows(values, gain):
    return values * lax.rsqrt(lax.optimization_barrier(jnp.mean(values * values, axis=-1, keepdims=True)) + EPS) * gain

def unit_rows(values):
    return values * lax.rsqrt(lax.optimization_barrier(jnp.sum(values * values, axis=-1, keepdims=True)) + EPS)

def stretch_step(carry_state, queries, key_rows, value_rows, strength, documents, first_pos):
    span_size = queries.shape[1]
    positions = first_pos + jnp.arange(span_size, dtype=jnp.int32)
    causal = positions[:, None] >= positions[None, :]
    same_doc = (documents[:, :, None] <= positions[None, None, :]) & causal[None]
    strict = same_doc & (positions[:, None] > positions[None, :])[None]
    carried = (documents < first_pos).astype(jnp.float32)
    rates = jnp.swapaxes(strength, 1, 2)[..., None]
    key_gram = jnp.einsum('bihe,bjhe->bhij', key_rows, key_rows, precision=HIGH)
    coupling = key_gram * rates * strict[:, None].astype(jnp.float32)
    key_state = jnp.einsum('bihe,bhef->bhif', key_rows, carry_state, precision=HIGH)
    target = rates * (jnp.swapaxes(value_rows, 1, 2) - key_state * carried[:, None, :, None])
    identity = jnp.eye(span_size, dtype=jnp.float32)
    update = jax.scipy.linalg.solve_triangular(identity + coupling, target, lower=True, unit_diagonal=True)
    scores = jnp.einsum('bihe,bjhe->bhij', queries, key_rows, precision=HIGH) * same_doc[:, None].astype(jnp.float32)
    result_rows = jnp.einsum('bhij,bhjf->bihf', scores, update, precision=HIGH)
    result_rows = result_rows + jnp.einsum('bihe,bhef->bihf', queries, carry_state, precision=HIGH) * carried[:, :, None, None]
    last_row = same_doc[:, -1, :].astype(jnp.float32)
    next_state = carry_state * carried[:, -1][:, None, None, None]
    next_state = next_state + jnp.einsum('bjhe,bhjf->bhef', key_rows * last_row[:, :, None, None], update, precision=HIGH)
    return (next_state, result_rows)

def run_stretches(carry_state, queries, key_rows, value_rows, strength, documents, start_pos):
    batch_size = queries.shape[0]
    length = queries.shape[1]
    blocks = length // STRETCH

    def to_blocks(values):
        return jnp.moveaxis(values.reshape((batch_size, blocks, STRETCH) + values.shape[2:]), 1, 0)

    def block_step(state_now, block_item):
        block_index, query_block, key_block, value_block, rate_block, doc_block = block_item
        return stretch_step(state_now, query_block, key_block, value_block, rate_block, doc_block, start_pos + block_index * STRETCH)
    final_state, block_outs = lax.scan(jax.checkpoint(block_step), carry_state, (jnp.arange(blocks, dtype=jnp.int32), to_blocks(queries), to_blocks(key_rows), to_blocks(value_rows), to_blocks(strength), to_blocks(documents)))
    return (jnp.moveaxis(block_outs, 0, 1).reshape(queries.shape), final_state)

def layer(inputs, norm_gain, qkv_weight, conv_weight, beta_weight, head_gain, out_weight, ffn_gain, gate_up_weight, down_weight, documents):
    batch_size = inputs.shape[0]
    length = inputs.shape[1]
    normed_in = low(norm_rows(inputs, norm_gain))
    projected = low_back(low(jnp.einsum('bld,de->ble', normed_in, qkv_weight, precision=HIGH)))
    padded = jnp.pad(projected, ((0, 0), (CONV - 1, 0), (0, 0)))
    positions = jnp.arange(length, dtype=jnp.int32)
    mixed = jnp.zeros(projected.shape, jnp.float32)
    for tap_index in range(CONV):
        tap_valid = (positions[None, :] - (CONV - 1) + tap_index >= documents).astype(jnp.float32)
        mixed = mixed + padded[:, tap_index:tap_index + length] * conv_weight[:, tap_index] * tap_valid[..., None]
    activity = jax.nn.silu(mixed)
    shape_heads = (batch_size, length, HEADS, HEAD_DIM)
    queries = low(unit_rows(activity[..., :D].reshape(shape_heads)) * HEAD_DIM ** (-0.5))
    key_rows = low(unit_rows(activity[..., D:2 * D].reshape(shape_heads)))
    value_rows = low(activity[..., 2 * D:].reshape(shape_heads))
    strength = jax.nn.sigmoid(jnp.einsum('bld,dh->blh', normed_in, beta_weight, precision=HIGH))
    zero_state = jnp.zeros((batch_size, HEADS, HEAD_DIM, HEAD_DIM), jnp.float32)
    head_out, final_state = run_stretches(zero_state, queries, key_rows, value_rows, strength, documents, 0)
    normed = low(norm_rows(head_out, head_gain)).reshape(batch_size, length, D)
    branch = low_back(jnp.einsum('bld,de->ble', normed, out_weight, precision=HIGH))
    middle = inputs + branch
    normed_mid = low(norm_rows(middle, ffn_gain))
    gate_up = low_back(jnp.einsum('bld,df->blf', normed_mid, gate_up_weight, precision=HIGH))
    hidden = low(jax.nn.silu(gate_up[..., :FF]) * gate_up[..., FF:])
    return middle + low_back(jnp.einsum('blf,fd->bld', hidden, down_weight, precision=HIGH))

def reference(tokens, cotangent, doc_start, norm_gain, qkv_weight, conv_weight, beta_weight, head_gain, out_weight, ffn_gain, gate_up_weight, down_weight):
    weights = tuple((weight.astype(jnp.float32) for weight in (norm_gain, qkv_weight, conv_weight, beta_weight, head_gain, out_weight, ffn_gain, gate_up_weight, down_weight)))
    per_group = math.gcd(SEQS, max(1, 4096 // LEN))
    groups = SEQS // per_group
    token_groups = tokens.astype(jnp.float32).reshape(groups, per_group, LEN, D)
    cotan_groups = cotangent.astype(jnp.float32).reshape(groups, per_group, LEN, D)
    doc_groups = doc_start.reshape(groups, per_group, LEN)

    def one_group(totals, loop_item):
        token_block, cotan_block, doc_block = loop_item
        result, pullback = jax.vjp(partial(layer, documents=doc_block), token_block, *weights)
        grads = pullback(cotan_block)
        return (tuple((total_sum + grad_part for total_sum, grad_part in zip(totals, grads[1:]))), (result, grads[0]))
    init = tuple((jnp.zeros_like(weight) for weight in weights))
    totals, (results, input_grads) = lax.scan(one_group, init, (token_groups, cotan_groups, doc_groups))
    output = results.reshape(SEQS, LEN, D).astype(jnp.bfloat16)
    input_grad = input_grads.reshape(SEQS, LEN, D)
    return (output, input_grad, totals[0], totals[1], totals[2], totals[3], totals[4], totals[5], totals[6], totals[7], totals[8])
```

```python
import functools

import jax
import jax.numpy as jnp
from jax import lax
from jax.experimental import pallas as pl
from jax.experimental.pallas import tpu as pltpu
from jax.sharding import PartitionSpec as P

D = 2048
HEADS = 16
HD = 128
FF = 5632
CONV = 4
EPS = 1e-06
RIM = 16
TP = 4
HT = HEADS // TP
DT = D // TP
FT = FF // TP
SCALE = HD**-0.5
VMEM = 56 * 1024 * 1024

BF = jnp.bfloat16
F32 = jnp.float32


def swap(x, bits):
    n = lax.axis_size("replica")
    return lax.ppermute(x, "replica", [(i, i ^ bits) for i in range(n)])


def plane_swap(x, j):
    return swap(x, 2 * j)


def core_swap(x):
    return swap(x, 1)


def far_sum(x):
    x = x.astype(F32)
    bits = 8
    while bits < lax.axis_size("replica"):
        x = x + swap(x.astype(BF), bits).astype(F32)
        bits *= 2
    return x


def z_shift(x, by):
    n = lax.axis_size("group")
    return lax.ppermute(x, "group", [(i, i + by) for i in range(n) if 0 <= i + by < n])


def z_turn(x, by):
    n = lax.axis_size("group")
    return lax.ppermute(x, "group", [(i, (i + by) % n) for i in range(n)])


def plane_copies(x):
    a, b = plane_swap(x, 1), plane_swap(x, 2)
    h = x.shape[0] // 32 * 16 if x.shape[0] >= 32 else x.shape[0] // 2
    d = jnp.concatenate([plane_swap(a[:h], 2), plane_swap(b[h:], 1)], axis=0)
    return [x, a, b, d]


def plane_sum(parts):
    got = [plane_swap(parts[j].astype(BF), j) for j in (1, 2, 3)]
    return parts[0].astype(F32) + got[0].astype(F32) + got[1].astype(F32) + got[2].astype(F32)


def plane_trade(parts):
    return [parts[0]] + [plane_swap(parts[j], j) for j in (1, 2, 3)]


def place(pieces, count, axis=0):
    shape = list(pieces[0][1].shape)
    shape.insert(axis, count)
    buf = jnp.zeros(shape, pieces[0][1].dtype)
    for index, piece in pieces:
        buf = lax.dynamic_update_index_in_dim(buf, piece, index, axis)
    return buf


def pick(x, index, axis=0):
    return lax.dynamic_index_in_dim(x, index, axis, keepdims=False)


def dot(a, b, dims=((1,), (0,))):
    return lax.dot_general(a, b, (dims, ((), ())), preferred_element_type=F32)


NT = ((1,), (1,))
TN = ((0,), (0,))


def dot3(a, b):
    ah, bh = a.astype(BF), b.astype(BF)
    al, bl = (a - ah.astype(F32)).astype(BF), (b - bh.astype(F32)).astype(BF)
    return dot(ah, bh) + (dot(ah, bl) + dot(al, bh))


def iotas(rows, cols):
    return (
        lax.broadcasted_iota(jnp.int32, (rows, cols), 0),
        lax.broadcasted_iota(jnp.int32, (rows, cols), 1),
    )


def unit_lower_inverse(a):
    n = a.shape[0]
    base = 16
    ri, ci = iotas(n, n)
    same = (ri // base) == (ci // base)
    compact = jnp.sum(jnp.where(same, a, 0.0).reshape(n // base, base, n), axis=0)
    lane = lax.broadcasted_iota(jnp.int32, (base, n), 1) % base
    rows = lax.broadcasted_iota(jnp.int32, (base, n), 0)
    spread = jnp.concatenate(
        [jnp.where(lane == j, compact, 0.0) for j in range(base)], axis=0
    )
    ones = same.astype(BF)
    hi = spread.astype(BF)
    lo = (spread - hi.astype(F32)).astype(BF)
    wide = dot(hi, ones) + dot(lo, ones)
    x = (lane == rows).astype(F32)
    for j in range(base - 1):
        x = x - wide[j * base : (j + 1) * base] * x[j : j + 1]
    full = jnp.where(same, jnp.concatenate([x] * (n // base), axis=0), 0.0)
    size = base
    while size < n:
        part = (
            ((ri // (2 * size)) == (ci // (2 * size)))
            & ((ri // size) % 2 == 1)
            & ((ci // size) % 2 == 0)
        )
        full = full - dot3(full, dot3(jnp.where(part, a, 0.0), full))
        size *= 2
    return full


def conv_rows(ext, taps, doc, length):
    pos = lax.broadcasted_iota(jnp.int32, (length, 1), 0)
    total = None
    for i in range(CONV):
        valid = (pos - (CONV - 1) + i >= doc).astype(F32)
        first = RIM - (CONV - 1) + i
        term = ext[first : first + length] * taps[i : i + 1] * valid
        total = term if total is None else total + term
    return total


def masks(doc, length):
    ri, ci = iotas(length, length)
    same = (doc <= ci) & (ri >= ci)
    return same.astype(F32), (same & (ri > ci)).astype(F32)


def ends(doc, length):
    last = doc[length - 1 : length]
    pos = lax.broadcasted_iota(jnp.int32, (length, 1), 0)
    return (pos >= last).astype(F32), (last < 0).astype(F32), (doc < 0).astype(F32)


def front_kernel(q_ref, taps_ref, doc_ref, rate_ref, qo, ko, vo, t_ref, u0_ref, w_ref, m_ref, b_ref):
    length = doc_ref.shape[1]
    doc = doc_ref[0]
    same, strict = masks(doc, length)
    tail, keep, carried = ends(doc, length)
    eye = (iotas(HD, HD)[0] == iotas(HD, HD)[1]).astype(F32)
    for h in range(HT):
        lanes = slice(h * HD, (h + 1) * HD)
        acts = []
        for part in range(3):
            cols = slice(part * DT + h * HD, part * DT + (h + 1) * HD)
            mixed = conv_rows(q_ref[0, :, cols].astype(F32), taps_ref[part, :, lanes], doc, length)
            acts.append(mixed * jax.nn.sigmoid(mixed))
        qa, ka, va = acts
        q = (qa * (lax.rsqrt(jnp.sum(qa * qa, axis=-1, keepdims=True) + EPS) * SCALE)).astype(BF)
        k = (ka * lax.rsqrt(jnp.sum(ka * ka, axis=-1, keepdims=True) + EPS)).astype(BF)
        v = va.astype(BF)
        rate = rate_ref[0, :, h : h + 1]
        inv = unit_lower_inverse(dot(k, k, NT) * (strict * rate)).astype(BF)
        kf = k.astype(F32)
        u0 = dot(inv, (v.astype(F32) * rate).astype(BF))
        w = dot(inv, (kf * (rate * carried)).astype(BF)).astype(BF)
        kl = (kf * tail).astype(BF)
        m_ref[0, h] = eye * keep - dot(kl, w, TN)
        b_ref[0, h] = dot(kl, u0.astype(BF), TN)
        qo[0, :, lanes] = q
        ko[0, :, lanes] = k
        vo[0, :, lanes] = v
        t_ref[0, h] = inv
        u0_ref[0, :, lanes] = u0
        w_ref[0, :, lanes] = w


def out_kernel(q_ref, k_ref, u0_ref, w_ref, s_ref, doc_ref, gain_ref, n_ref, o_ref, u_ref):
    length = doc_ref.shape[1]
    doc = doc_ref[0]
    same, _ = masks(doc, length)
    carried = (doc < 0).astype(F32)
    gain = gain_ref[...]
    for h in range(HT):
        lanes = slice(h * HD, (h + 1) * HD)
        q, k, state = q_ref[0, :, lanes], k_ref[0, :, lanes], s_ref[0, h]
        u = (u0_ref[0, :, lanes] - dot(w_ref[0, :, lanes], state)).astype(BF)
        scores = (dot(q, k, NT) * same).astype(BF)
        o = dot(scores, u) + dot(q, state) * carried
        r = lax.rsqrt(jnp.mean(o * o, axis=-1, keepdims=True) + EPS)
        n_ref[0, :, lanes] = (o * r * gain).astype(BF)
        o_ref[0, :, lanes] = o
        u_ref[0, :, lanes] = u


def back_kernel(
    dn_ref, o_ref, gain_ref, q_ref, k_ref, t_ref, rate_ref, doc_ref, g_ref, y_ref, z_ref, l_ref, hg_ref
):
    length = doc_ref.shape[1]
    doc = doc_ref[0]
    same, _ = masks(doc, length)
    tail, _, carried = ends(doc, length)
    gain = gain_ref[...]

    @pl.when(pl.program_id(0) == 0)
    def _():
        hg_ref[...] = jnp.zeros_like(hg_ref)

    total = jnp.zeros((1, HD), F32)
    for h in range(HT):
        lanes = slice(h * HD, (h + 1) * HD)
        o, dy = o_ref[0, :, lanes], dn_ref[0, :, lanes].astype(F32)
        r = lax.rsqrt(jnp.mean(o * o, axis=-1, keepdims=True) + EPS)
        total = total + jnp.sum(o * r * dy, axis=0, keepdims=True)
        gy = gain * dy
        gf = r * gy - o * (r * r * r * jnp.mean(o * gy, axis=-1, keepdims=True))
        g = gf.astype(BF)
        q, k = q_ref[0, :, lanes], k_ref[0, :, lanes]
        inv = t_ref[0, h]
        scores = (dot(q, k, NT) * same).astype(BF)
        kf = k.astype(F32)
        y = dot(inv, dot(scores, g, TN).astype(BF), TN)
        z_ref[0, :, lanes] = dot(inv, (kf * tail).astype(BF), TN).astype(BF)
        rate = rate_ref[0, :, h : h + 1]
        l_ref[0, h] = dot((q.astype(F32) * carried).astype(BF), g, TN) - dot(
            (kf * (rate * carried)).astype(BF), y.astype(BF), TN
        )
        g_ref[0, :, lanes] = g
        y_ref[0, :, lanes] = y
    hg_ref[0:1] += total


def unit_back(act, dy, scale):
    r = lax.rsqrt(jnp.sum(act * act, axis=-1, keepdims=True) + EPS)
    inner = jnp.sum(act * dy, axis=-1, keepdims=True)
    return (r * scale) * dy - act * (r * r * r * scale * inner)


def grad_kernel(
    p_ref, taps_ref, doc_ref, rate_ref, q_ref, k_ref, v_ref, s_ref, u_ref, g_ref, y_ref, z_ref, a_ref,
    gp_ref, gl_ref, cg_ref,
):
    length = doc_ref.shape[1]
    doc = doc_ref[0]
    same, strict = masks(doc, length)
    tail, _, carried = ends(doc, length)
    pos = lax.broadcasted_iota(jnp.int32, (length, 1), 0)

    @pl.when(pl.program_id(0) == 0)
    def _():
        cg_ref[...] = jnp.zeros_like(cg_ref)

    logits = []
    for h in range(HT):
        lanes = slice(h * HD, (h + 1) * HD)
        q, k, v = q_ref[0, :, lanes], k_ref[0, :, lanes], v_ref[0, :, lanes]
        state, u, g, adj = s_ref[0, h], u_ref[0, :, lanes], g_ref[0, :, lanes], a_ref[0, h]
        rate = rate_ref[0, :, h : h + 1]
        yf = y_ref[0, :, lanes] + dot(z_ref[0, :, lanes], adj)
        y = yf.astype(BF)
        dv = rate * yf
        d1 = dot(y, u, NT) * strict
        gram = dot(k, k, NT)
        e = v.astype(F32) - dot(k, state) * carried
        drate = jnp.sum(yf * e, axis=-1, keepdims=True) - jnp.sum(d1 * gram, axis=-1, keepdims=True)
        dgram = (d1 * (-rate)).astype(BF)
        dscore = (dot(g, u, NT) * same).astype(BF)
        dq = dot(dscore, k) + dot(g, state, NT) * carried
        dk = dot(dscore, q, TN) + dot(dgram, k) + dot(dgram, k, TN)
        dk = dk - dot(y, state, NT) * (rate * carried) + dot(u, adj, NT) * tail
        logits.append(drate * rate * (1.0 - rate))
        for part, grad in enumerate((dq, dk, dv)):
            cols = slice(part * DT + h * HD, part * DT + (h + 1) * HD)
            ext = p_ref[0, :, cols].astype(F32)
            taps = taps_ref[part, :, lanes]
            mixed = conv_rows(ext, taps, doc, length)
            s = jax.nn.sigmoid(mixed)
            if part < 2:
                grad = unit_back(mixed * s, grad, SCALE if part == 0 else 1.0)
            gm = grad * (s * (1.0 + mixed * (1.0 - s)))
            total = jnp.zeros((length + RIM, HD), F32)
            for i in range(CONV):
                valid = (pos - (CONV - 1) + i >= doc).astype(F32)
                gv = gm * valid
                first = RIM - (CONV - 1) + i
                cg_ref[part, i : i + 1, lanes] += jnp.sum(
                    gv * ext[first : first + length], axis=0, keepdims=True
                )
                gv = gv * taps[i : i + 1]
                pads = [jnp.zeros((first, HD), F32), gv]
                if RIM - first > 0:
                    pads.append(jnp.zeros((RIM - first, HD), F32))
                total = total + jnp.concatenate(pads, axis=0)
            gp_ref[0, :, cols] = total.astype(BF)
    gl_ref[0] = jnp.concatenate(logits, axis=1)


def block(shape, fixed=False):
    zeros = (0,) * len(shape)
    if fixed:
        return pl.BlockSpec(tuple(shape), lambda i: zeros)
    return pl.BlockSpec((1,) + tuple(shape[1:]), lambda i: (i,) + zeros[1:])


def call(kernel, ins, fixed_ins, outs, fixed_outs=(), flops=0):
    count = ins[0].shape[0]
    size = sum(x.size * x.dtype.itemsize for x in ins)
    for shape, dtype in outs:
        n = 1
        for extent in shape:
            n *= extent
        size += n * jnp.dtype(dtype).itemsize
    return pl.pallas_call(
        kernel,
        grid=(count,),
        in_specs=[block(x.shape, i in fixed_ins) for i, x in enumerate(ins)],
        out_specs=[block(s, i in fixed_outs) for i, (s, _) in enumerate(outs)],
        out_shape=[jax.ShapeDtypeStruct(s, d) for s, d in outs],
        compiler_params=pltpu.CompilerParams(vmem_limit_bytes=VMEM),
        cost_estimate=pl.CostEstimate(flops=flops, bytes_accessed=size, transcendentals=0),
    )(*ins)


def norm_back(x, gain, dy):
    r = lax.rsqrt(jnp.mean(x * x, axis=-1, keepdims=True) + EPS)
    gy = gain * dy
    dx = r * gy - x * (r * r * r * jnp.mean(x * gy, axis=-1, keepdims=True))
    return dx, jnp.sum((x * r * dy).reshape(-1, x.shape[-1]), axis=0)


def norm_rows(x, gain):
    return (x * lax.rsqrt(jnp.mean(x * x, axis=-1, keepdims=True) + EPS) * gain).astype(BF)


def mm(a, b, dims=((1,), (0,))):
    return lax.dot_general(a, b, (dims, ((), ())), preferred_element_type=F32)


def body(
    tokens,
    cotangent,
    doc_start,
    norm_gain,
    qkv_weight,
    conv_weight,
    beta_weight,
    head_gain,
    out_weight,
    ffn_gain,
    gate_up_weight,
    down_weight,
):
    groups = lax.axis_size("group")
    r = lax.axis_index("replica") % 8
    g = lax.axis_index("group")
    c, t = r % 2, r // 2
    batch, length, _ = tokens.shape
    rows = batch * length
    seqs = TP * batch
    ext_len = length + RIM
    shard = D // groups
    half = shard // 2
    ff_shard = FF // groups
    col = D // 8

    def z_pieces(x):
        return [(g, x)] + [((g - s) % groups, z_turn(x, s)) for s in range(1, groups)]

    gain_in = place(z_pieces(norm_gain.reshape(1, shard)), groups).reshape(D).astype(F32)
    small = jnp.concatenate(
        [ffn_gain.reshape(-1), beta_weight.reshape(-1), conv_weight.reshape(-1)]
    ).reshape(-1, 128)
    small = place(z_pieces(small), groups).reshape(groups, -1)
    gain_mid = small[:, :shard].reshape(D).astype(F32)
    beta_full = small[:, shard : shard * (1 + HEADS)].reshape(D, HEADS)
    conv_full = small[:, shard * (1 + HEADS) :].reshape(3, TP, DT, CONV)
    beta_t = lax.dynamic_slice(beta_full, (0, t * HT), (D, HT))
    taps = jnp.swapaxes(pick(conv_full, t, 1), 1, 2).astype(F32)
    gain_head = head_gain.astype(F32).reshape(1, HD)

    rim = z_shift(tokens[:, length - RIM :], 1)
    inputs = tokens.astype(F32)
    ext = jnp.concatenate([rim, tokens], axis=1).astype(F32)
    normed_ext = norm_rows(ext, gain_in)
    normed_all = jnp.concatenate(plane_copies(normed_ext.reshape(batch * ext_len, D)), axis=0)
    doc_rel = doc_start - g * length
    docs = jnp.concatenate(
        [doc_rel] + [plane_swap(doc_rel, j) for j in (1, 2, 3)], axis=0
    ).reshape(seqs, length, 1)

    piece = jnp.concatenate(
        [lax.dynamic_slice(qkv_weight, (c * half, j * D + t * DT), (half, DT)) for j in range(3)], axis=1
    )
    qkv = jnp.zeros((groups, 2, half, 3 * DT), BF)
    for index, part in z_pieces(piece):
        qkv = lax.dynamic_update_slice(qkv, part[None, None], (index, c, 0, 0))
        qkv = lax.dynamic_update_slice(qkv, core_swap(part)[None, None], (index, 1 - c, 0, 0))
    qkv = qkv.reshape(D, 3 * DT)

    projected = mm(normed_all, qkv).astype(BF).reshape(seqs, ext_len, 3 * DT)
    logits = mm(normed_all, beta_t).reshape(seqs, ext_len, HT)[:, RIM:]
    rates = jax.nn.sigmoid(logits)

    piece = lax.dynamic_slice(down_weight, (0, r * col), (ff_shard, col))
    piece = lax.all_gather(piece, "group", axis=0, tiled=True).reshape(TP, FT, col)
    got = plane_trade([pick(piece, t ^ j) for j in range(TP)])
    other = core_swap(jnp.stack(got))
    down = place(
        [((t ^ j) * 2 + c, got[j]) for j in range(TP)]
        + [((t ^ j) * 2 + 1 - c, other[j]) for j in range(TP)],
        8,
    )
    down = jnp.swapaxes(down, 0, 1).reshape(FT, D)

    piece = jnp.concatenate(
        [
            lax.dynamic_slice(gate_up_weight, (c * half, j * FF + t * FT), (half, FT))
            for j in range(2)
        ],
        axis=1,
    )
    piece = lax.all_gather(piece, "group", axis=0)
    gate_up_w = place([(c, piece), (1 - c, core_swap(piece))], 2, 1).reshape(D, 2 * FT)

    piece = lax.dynamic_slice(out_weight, (r * (shard // 8), 0), (shard // 8, D))
    piece = place(z_pieces(piece), groups)
    got = plane_copies(piece)
    other = core_swap(jnp.stack(got))
    out_w = place(
        [((t ^ j) * 2 + c, got[j]) for j in range(TP)]
        + [((t ^ j) * 2 + 1 - c, other[j]) for j in range(TP)],
        8,
        1,
    ).reshape(TP, DT, D)
    out_rel = jnp.concatenate([pick(out_w, t ^ j) for j in range(TP)], axis=0)

    cot = cotangent.reshape(rows, D)
    cot_all = jnp.concatenate(plane_copies(cot), axis=0)

    wide = (seqs, length, DT)
    square = (seqs, HT, HD, HD)
    queries, key_rows, value_rows, inverse, u0, w, move, free = call(
        front_kernel,
        [projected, taps, docs, rates],
        (1,),
        [
            (wide, BF),
            (wide, BF),
            (wide, BF),
            ((seqs, HT, length, length), BF),
            (wide, F32),
            (wide, BF),
            (square, F32),
            (square, F32),
        ],
        flops=seqs * HT * length * length * (24 * 2 * length + 3 * 2 * HD),
    )
    state = jnp.zeros(square, BF)
    for _ in range(groups - 1):
        leaving = (
            jnp.einsum("shij,shjk->shik", move.astype(BF), state, preferred_element_type=F32) + free
        )
        state = z_shift(leaving.astype(BF), 1)
    normed, head_out, update = call(
        out_kernel,
        [queries, key_rows, u0, w, state, docs, gain_head],
        (6,),
        [(wide, BF), (wide, F32), (wide, BF)],
        flops=seqs * HT * length * 2 * HD * (2 * length + 2 * HD),
    )
    got = plane_trade([normed[j * batch : (j + 1) * batch].reshape(rows, DT) for j in range(TP)])
    normed_rel = jnp.concatenate(got, axis=1)
    normed_abs = jnp.swapaxes(place([(t ^ j, got[j]) for j in range(TP)], TP), 0, 1).reshape(rows, D)
    middle = inputs.reshape(rows, D) + mm(normed_rel, out_rel)
    normed_mid = norm_rows(middle, gain_mid)
    mid_all = jnp.concatenate(plane_copies(normed_mid), axis=0)

    gate_up = mm(mid_all, gate_up_w)
    grad_hidden = mm(cot_all, down, NT)
    gate, up = gate_up[:, :FT], gate_up[:, FT:]
    sg = jax.nn.sigmoid(gate)
    hidden = (gate * sg * up).astype(BF)
    grad_gate_up = jnp.concatenate(
        [
            (grad_hidden * up * (sg * (1.0 + gate * (1.0 - sg)))).astype(BF),
            (grad_hidden * gate * sg).astype(BF),
        ],
        axis=1,
    )
    mid_part = mm(grad_gate_up, gate_up_w, NT).astype(BF).reshape(TP, rows, D)
    grad_mid = plane_sum([mid_part[j] for j in range(TP)])
    out_part = mm(hidden, down).astype(BF).reshape(TP, rows, D)
    output = (middle + plane_sum([out_part[j] for j in range(TP)])).astype(BF)

    dx, ffn_gain_part = norm_back(middle, gain_mid, grad_mid)
    grad_middle = cot.astype(F32) + dx
    branch = grad_middle.astype(BF)
    dnormed = mm(branch, out_rel, NT).astype(BF)
    got = plane_trade([dnormed[:, j * DT : (j + 1) * DT] for j in range(TP)])
    dnormed = jnp.concatenate(got, axis=0).reshape(wide)

    grad_out, y0, z, local, head_part = call(
        back_kernel,
        [dnormed, head_out, gain_head, queries, key_rows, inverse, rates, docs],
        (2,),
        [(wide, BF), (wide, F32), (wide, BF), (square, F32), ((8, HD), F32)],
        (4,),
        flops=seqs * HT * length * 2 * HD * (4 * length + 2 * HD),
    )
    later = jnp.zeros(square, BF)
    for _ in range(groups - 1):
        leaving = (
            jnp.einsum("shji,shjk->shik", move.astype(BF), later, preferred_element_type=F32) + local
        )
        later = z_shift(leaving.astype(BF), -1)
    grad_proj, grad_logit, conv_part = call(
        grad_kernel,
        [
            projected, taps, docs, rates, queries, key_rows, value_rows, state, update, grad_out, y0, z, later,
        ],
        (1,),
        [((seqs, ext_len, 3 * DT), BF), ((seqs, length, HT), F32), ((3, CONV, DT), F32)],
        (2,),
        flops=seqs * HT * length * 2 * HD * (7 * length + 5 * HD),
    )
    grad_proj = grad_proj.reshape(seqs * ext_len, 3 * DT)

    logit_ext = jnp.pad(grad_logit, ((0, 0), (RIM, 0), (0, 0))).reshape(seqs * ext_len, HT).astype(BF)
    in_part = mm(grad_proj, qkv, NT) + mm(logit_ext, beta_t, NT)
    in_part = in_part.astype(BF).reshape(TP, batch, ext_len, D)
    grad_in = plane_sum([in_part[j] for j in range(TP)])
    back_rim = z_shift(grad_in[:, :RIM].astype(BF), -1).astype(F32)
    grad_in = grad_in[:, RIM:]
    grad_in = jnp.concatenate(
        [grad_in[:, : length - RIM], grad_in[:, length - RIM :] + back_rim], axis=1
    )
    dx, norm_gain_part = norm_back(inputs, gain_in, grad_in)
    input_grad = grad_middle.reshape(batch, length, D) + dx

    def two_halves(left, right):
        parts = left.reshape(-1, groups, 2, half)
        away = mm(pick(parts, 1 - c, 2).reshape(-1, groups * half), right, TN).astype(BF)
        mine = mm(pick(parts, c, 2).reshape(-1, groups * half), right, TN)
        return (mine + core_swap(away).astype(F32)).astype(BF).reshape(groups, half, -1)

    def columns(x, core):
        parts = x.reshape(-1, TP, 2, col)
        return jnp.concatenate([pick(pick(parts, t ^ j, 1), core, 1) for j in range(TP)], axis=1)

    def two_columns(left, right):
        away = mm(left, columns(right, 1 - c), TN).astype(BF)
        mine = mm(left, columns(right, c), TN)
        return (mine + core_swap(away).astype(F32)).astype(BF)

    def spread(x):
        got = plane_copies(x)
        mine = jnp.stack(got)
        other = core_swap(mine)
        return place(
            [((t ^ j) * 2 + c, got[j]) for j in range(TP)]
            + [((t ^ j) * 2 + 1 - c, other[j]) for j in range(TP)],
            8,
        )

    gate_sum = two_halves(mid_all, grad_gate_up)
    gate_sum = far_sum(lax.psum_scatter(gate_sum, "group", scatter_dimension=0)).astype(BF)
    gate_sum = spread(gate_sum).reshape(TP, 2, half, 2, FT)
    gate_up_grad = gate_sum.transpose(1, 2, 3, 0, 4).reshape(shard, 2 * FF).astype(F32)

    down_sum = two_columns(hidden, cot_all)
    got = plane_trade([down_sum[:, j * col : (j + 1) * col] for j in range(TP)])
    down_sum = place([(t ^ j, got[j]) for j in range(TP)], TP).reshape(groups, ff_shard, col)
    down_sum = far_sum(lax.psum_scatter(down_sum, "group", scatter_dimension=0)).astype(BF)
    down_grad = jnp.swapaxes(spread(down_sum), 0, 1).reshape(ff_shard, D).astype(F32)

    out_sum = two_columns(normed_abs, branch)
    out_sum = plane_sum([out_sum[:, j * col : (j + 1) * col] for j in range(TP)]).astype(BF)

    def z_sum(x):
        total = pick(x, g).astype(F32)
        for s in range(1, groups):
            total = total + z_turn(pick(x, (g + s) % groups), s).astype(F32)
        return total

    out_sum = far_sum(z_sum(out_sum.reshape(groups, shard, col))).astype(BF)
    out_grad = jnp.swapaxes(spread(out_sum), 0, 1).reshape(shard, D).astype(F32)

    qkv_sum = far_sum(z_sum(two_halves(normed_all, grad_proj))).astype(BF)
    qkv_sum = spread(qkv_sum).reshape(TP, 2, half, 3, DT)
    qkv_grad = qkv_sum.transpose(1, 2, 3, 0, 4).reshape(shard, 3 * D).astype(F32)

    beta_part = mm(normed_all, logit_ext, TN)
    beta_all = lax.dynamic_update_slice(jnp.zeros((D, HEADS), F32), beta_part, (0, t * HT))
    conv_all = place([(t, jnp.swapaxes(conv_part, 1, 2))], TP, 1)
    pack = jnp.concatenate(
        [
            norm_gain_part.reshape(groups, -1),
            ffn_gain_part.reshape(groups, -1),
            jnp.broadcast_to(head_part[:1], (groups, HD)),
            beta_all.reshape(groups, -1),
            conv_all.reshape(groups, -1),
        ],
        axis=1,
    ).reshape(groups, -1, 128)
    total = far_sum(z_sum(pack))
    total = total + core_swap(total)
    total = total + plane_swap(total, 1)
    total = (total + plane_swap(total, 2)).reshape(-1)
    sizes = [shard, shard, HD, shard * HEADS, 3 * D // groups * CONV]
    at = [0]
    for size in sizes:
        at.append(at[-1] + size)
    norm_gain_grad, ffn_gain_grad, head_gain_grad, beta_grad, conv_grad = [
        total[at[i] : at[i + 1]] for i in range(5)
    ]
    return (
        output.reshape(batch, length, D),
        input_grad,
        norm_gain_grad,
        qkv_grad,
        conv_grad.reshape(-1, CONV),
        beta_grad.reshape(-1, HEADS),
        head_gain_grad,
        out_grad,
        ffn_gain_grad,
        gate_up_grad,
        down_grad,
    )


def solution(mesh):
    rows = P("replica", "group", None)
    shard = P("group", None)
    return jax.shard_map(
        body,
        mesh=mesh,
        in_specs=(
            rows, rows, P("replica", "group"), P("group"), shard, shard, shard, P(), shard, P("group"), shard, shard,
        ),
        out_specs=(
            rows, rows, P("group"), shard, shard, shard, P(), shard, P("group"), shard, shard,
        ),
        check_vma=False,
    )
```

```python
import functools

import jax
import jax.numpy as jnp
from jax import lax
from jax.experimental import pallas as pl
from jax.experimental.pallas import tpu as pltpu
from jax.sharding import PartitionSpec as P

D = 2048
HEADS = 16
HD = 128
FF = 5632
CONV = 4
EPS = 1e-06
RIM = 16
TP = 4
HT = HEADS // TP
DT = D // TP
FT = FF // TP
SCALE = HD**-0.5
VMEM = 56 * 1024 * 1024

BF = jnp.bfloat16
F32 = jnp.float32


def swap(x, bits):
    n = lax.axis_size("replica")
    return lax.ppermute(x, "replica", [(i, i ^ bits) for i in range(n)])


def plane_swap(x, j):
    return swap(x, 2 * j)


def core_swap(x):
    return swap(x, 1)


def far_sum(x):
    x = x.astype(F32)
    bits = 8
    while bits < lax.axis_size("replica"):
        x = x + swap(x.astype(BF), bits).astype(F32)
        bits *= 2
    return x


def z_shift(x, by):
    n = lax.axis_size("group")
    return lax.ppermute(x, "group", [(i, i + by) for i in range(n) if 0 <= i + by < n])


def z_turn(x, by):
    n = lax.axis_size("group")
    return lax.ppermute(x, "group", [(i, (i + by) % n) for i in range(n)])


def plane_copies(x):
    a, b = plane_swap(x, 1), plane_swap(x, 2)
    h = split_at(x.shape[0])
    return [x, a, b, plane_swap(a[:h], 2), plane_swap(b[h:], 1)]


def plane_parts(parts):
    own, x, y, d = parts
    h = split_at(own.shape[0])
    via_x, via_y = plane_swap(d[:h], 1), plane_swap(d[h:], 2)
    y = jnp.concatenate([(y[:h].astype(F32) + via_x.astype(F32)).astype(BF), y[h:]], axis=0)
    x = jnp.concatenate([x[:h], (x[h:].astype(F32) + via_y.astype(F32)).astype(BF)], axis=0)
    return [own, plane_swap(x, 1), plane_swap(y, 2)]


def plane_sum(parts):
    own, x, y = plane_parts([p.astype(BF) for p in parts])
    return parts[0].astype(F32) + x.astype(F32) + y.astype(F32)


def after(x, *others):
    return lax.optimization_barrier((x, *others))[0]


def plane_trade(parts):
    return [parts[0]] + [plane_swap(parts[j], j) for j in (1, 2, 3)]


def place(pieces, count, axis=0):
    shape = list(pieces[0][1].shape)
    shape.insert(axis, count)
    buf = jnp.zeros(shape, pieces[0][1].dtype)
    for index, piece in pieces:
        buf = lax.dynamic_update_index_in_dim(buf, piece, index, axis)
    return buf


def pick(x, index, axis=0):
    return lax.dynamic_index_in_dim(x, index, axis, keepdims=False)


def dot(a, b, dims=((1,), (0,))):
    return lax.dot_general(a, b, (dims, ((), ())), preferred_element_type=F32)


NT = ((1,), (1,))
TN = ((0,), (0,))


def iotas(rows, cols):
    return (
        lax.broadcasted_iota(jnp.int32, (rows, cols), 0),
        lax.broadcasted_iota(jnp.int32, (rows, cols), 1),
    )


def unit_lower_inverses(mats):
    n = mats[0].shape[0]
    base, tile = 16, 128
    ri, ci = iotas(n, n)
    lane = lax.broadcasted_iota(jnp.int32, (base, tile), 1) % base
    rows = lax.broadcasted_iota(jnp.int32, (base, tile), 0)
    picks = [lane == j for j in range(base)]
    rt, ct = iotas(tile, tile)
    same = (rt // base) == (ct // base)
    ones = same.astype(BF)
    zero = jnp.zeros((), BF)
    lows = [a.astype(BF) for a in mats]
    spans = [slice(at, at + tile) for at in range(0, n, tile)]
    blocks = [(m, span) for m in range(len(mats)) for span in spans]
    wides = []
    for m, span in blocks:
        part = jnp.where(same, mats[m][span, span], 0.0)
        compact = jnp.sum(part.reshape(tile // base, base, tile), axis=0).astype(BF)
        spread = jnp.concatenate([jnp.where(p, compact, zero) for p in picks], axis=0)
        wides.append(dot(spread, ones))
    xs = [(lane == rows).astype(F32)] * len(blocks)
    for j in range(base - 1):
        xs = [x - w[j * base : (j + 1) * base] * x[j : j + 1] for x, w in zip(xs, wides)]
    fulls = [jnp.where(same, jnp.concatenate([x] * (tile // base), axis=0), 0.0) for x in xs]
    size = base
    while size < tile:
        part = (
            ((rt // (2 * size)) == (ct // (2 * size)))
            & ((rt // size) % 2 == 1)
            & ((ct // size) % 2 == 0)
        )
        halves = [full.astype(BF) for full in fulls]
        inner = [
            dot(jnp.where(part, lows[m][span, span], zero), h).astype(BF)
            for (m, span), h in zip(blocks, halves)
        ]
        fulls = [full - dot(h, i) for full, h, i in zip(fulls, halves, inner)]
        size *= 2
    fulls = [full.astype(BF) for full in fulls]
    if n == tile:
        return fulls
    inner = [dot(low[tile:, :tile], fulls[2 * m]).astype(BF) for m, low in enumerate(lows)]
    corners = [-dot(fulls[2 * m + 1], i) for m, i in enumerate(inner)]
    blank = jnp.zeros((tile, tile), BF)
    return [
        jnp.concatenate(
            [
                jnp.concatenate([fulls[2 * m], blank], axis=1),
                jnp.concatenate([corner.astype(BF), fulls[2 * m + 1]], axis=1),
            ],
            axis=0,
        )
        for m, corner in enumerate(corners)
    ]


def tap_masks(doc, length):
    pos = lax.broadcasted_iota(jnp.int32, (length, 1), 0)
    return [
        jnp.broadcast_to((pos - (CONV - 1) + i >= doc).astype(F32), (length, HD)) for i in range(CONV - 1)
    ]


def conv_rows(ext, taps, kept, length):
    total = ext[RIM : RIM + length] * taps[CONV - 1 : CONV]
    for i in range(CONV - 1):
        first = RIM - (CONV - 1) + i
        total = total + ext[first : first + length] * taps[i : i + 1] * kept[i]
    return total


def masks(doc, length):
    ri, ci = iotas(length, length)
    same = (doc <= ci) & (ri >= ci)
    return same.astype(F32), (same & (ri > ci)).astype(F32)


def ends(doc, length):
    last = doc[length - 1 : length]
    pos = lax.broadcasted_iota(jnp.int32, (length, 1), 0)
    return (pos >= last).astype(F32), (last < 0).astype(F32), (doc < 0).astype(F32)


def row_starts(n):
    return (0, n, 2 * n, 3 * n, 3 * n + split_at(n))


def row_copies(srcs, dst, sem):
    starts = row_starts(srcs[0].shape[0])
    return [
        pltpu.make_async_copy(src, dst.at[pl.ds(starts[i], src.shape[0])], sem.at[i])
        for i, src in enumerate(srcs)
    ]


def front_kernel(groups, *refs):
    idx_ref, xs, ws = refs[0], refs[1:6], refs[6 : 6 + 2 * groups]
    (
        beta_ref, taps_ref, doc_ref, qo, ko, vo, t_ref, u0_ref, wo_ref, m_ref, b_ref, p_ref, rate_ref,
        all_ref, w_ref, x_sem, w_sem,
    ) = refs[6 + 2 * groups :]
    length = doc_ref.shape[1]
    half = ws[0].shape[0]
    step = pl.program_id(0)

    @pl.when(step == 0)
    def _():
        copies = row_copies(xs, all_ref, x_sem)
        for cc in range(2):
            for s in range(groups):
                at = (cc * groups + (idx_ref[2] + groups - s) % groups) * half
                copies.append(
                    pltpu.make_async_copy(
                        ws[cc * groups + s],
                        w_ref.at[pl.ds(pl.multiple_of(at, 128), half)],
                        w_sem.at[cc * groups + s],
                    )
                )
        for copy in copies:
            copy.start()
        for copy in copies:
            copy.wait()

    rows = length + RIM
    here = pl.ds(pl.multiple_of(step * rows, 16), rows)
    doc = doc_ref[0]
    same, strict = masks(doc, length)
    tail, keep, carried = ends(doc, length)
    eye = (iotas(HD, HD)[0] == iotas(HD, HD)[1]).astype(F32)

    @pl.loop(0, 3 * DT // 256)
    def _(i):
        cols = pl.ds(pl.multiple_of(i * 256, 256), 256)
        p_ref[0, :, cols] = dot(all_ref[here], w_ref[:, cols]).astype(BF)

    own = pl.ds(pl.multiple_of(step * rows + RIM, 16), length)
    rates = jax.nn.sigmoid(dot(all_ref[own], beta_ref[...]))
    rate_ref[0] = rates
    kept = tap_masks(doc, length)
    wide = (length, HD)
    tail, carried = jnp.broadcast_to(tail, wide), jnp.broadcast_to(carried, wide)
    head_rates = [jnp.broadcast_to(rates[:, h : h + 1], wide) for h in range(HT)]
    lanes = [slice(h * HD, (h + 1) * HD) for h in range(HT)]
    mats = []
    for h in range(HT):
        acts = []
        for part in range(3):
            cols = slice(part * DT + h * HD, part * DT + (h + 1) * HD)
            mixed = conv_rows(p_ref[0, :, cols].astype(F32), taps_ref[part, :, lanes[h]], kept, length)
            acts.append(mixed * jax.nn.sigmoid(mixed))
        qa, ka, va = acts
        q = (qa * (lax.rsqrt(jnp.sum(qa * qa, axis=-1, keepdims=True) + EPS) * SCALE)).astype(BF)
        k = (ka * lax.rsqrt(jnp.sum(ka * ka, axis=-1, keepdims=True) + EPS)).astype(BF)
        qo[0, :, lanes[h]] = q
        ko[0, :, lanes[h]] = k
        vo[0, :, lanes[h]] = va.astype(BF)
        mats.append(dot(k, k, NT) * (strict * rates[:, h : h + 1]))
    invs = unit_lower_inverses(mats)
    for h in range(HT):
        inv, rate = invs[h], head_rates[h]
        kf = ko[0, :, lanes[h]].astype(F32)
        u0 = dot(inv, (vo[0, :, lanes[h]].astype(F32) * rate).astype(BF))
        w = dot(inv, (kf * (rate * carried)).astype(BF)).astype(BF)
        kl = (kf * tail).astype(BF)
        m_ref[0, h] = (eye * keep - dot(kl, w, TN)).astype(BF)
        b_ref[0, h] = dot(kl, u0.astype(BF), TN)
        t_ref[0, h] = inv
        u0_ref[0, :, lanes[h]] = u0
        wo_ref[0, :, lanes[h]] = w


def out_kernel(gain_ref, q_ref, k_ref, u0_ref, w_ref, s_ref, doc_ref, n_ref, o_ref, u_ref):
    length = doc_ref.shape[1]
    doc = doc_ref[0]
    same, _ = masks(doc, length)
    carried = (doc < 0).astype(F32)
    gain = gain_ref[...]
    for h in range(HT):
        lanes = slice(h * HD, (h + 1) * HD)
        q, k, state = q_ref[0, :, lanes], k_ref[0, :, lanes], s_ref[0, h]
        u = (u0_ref[0, :, lanes] - dot(w_ref[0, :, lanes], state)).astype(BF)
        scores = (dot(q, k, NT) * same).astype(BF)
        o = dot(scores, u) + dot(q, state) * carried
        r = lax.rsqrt(jnp.mean(o * o, axis=-1, keepdims=True) + EPS)
        n_ref[0, :, lanes] = (o * r * gain).astype(BF)
        o_ref[0, :, lanes] = o
        u_ref[0, :, lanes] = u


def back_kernel(
    gain_ref, dn_ref, o_ref, q_ref, k_ref, t_ref, rate_ref, doc_ref, g_ref, y_ref, z_ref, l_ref, hg_ref
):
    length = doc_ref.shape[1]
    doc = doc_ref[0]
    same, _ = masks(doc, length)
    tail, _, carried = ends(doc, length)
    gain = gain_ref[...]

    @pl.when(pl.program_id(0) == 0)
    def _():
        hg_ref[...] = jnp.zeros_like(hg_ref)

    total = jnp.zeros((1, HD), F32)
    for h in range(HT):
        lanes = slice(h * HD, (h + 1) * HD)
        o, dy = o_ref[0, :, lanes], dn_ref[0, :, lanes].astype(F32)
        r = lax.rsqrt(jnp.mean(o * o, axis=-1, keepdims=True) + EPS)
        total = total + jnp.sum(o * r * dy, axis=0, keepdims=True)
        gy = gain * dy
        gf = r * gy - o * (r * r * r * jnp.mean(o * gy, axis=-1, keepdims=True))
        g = gf.astype(BF)
        q, k = q_ref[0, :, lanes], k_ref[0, :, lanes]
        inv = t_ref[0, h]
        scores = (dot(q, k, NT) * same).astype(BF)
        kf = k.astype(F32)
        y = dot(inv, dot(scores, g, TN).astype(BF), TN)
        z_ref[0, :, lanes] = dot(inv, (kf * tail).astype(BF), TN).astype(BF)
        rate = rate_ref[0, :, h : h + 1]
        l_ref[0, h] = dot((q.astype(F32) * carried).astype(BF), g, TN) - dot(
            (kf * (rate * carried)).astype(BF), y.astype(BF), TN
        )
        g_ref[0, :, lanes] = g
        y_ref[0, :, lanes] = y
    hg_ref[0:1] += total


def unit_back(act, dy, scale):
    r = lax.rsqrt(jnp.sum(act * act, axis=-1, keepdims=True) + EPS)
    inner = jnp.sum(act * dy, axis=-1, keepdims=True)
    return (r * scale) * dy - act * (r * r * r * scale * inner)


def grad_kernel(
    taps_ref, w_ref, beta_ref, p_ref, doc_ref, rate_ref, q_ref, k_ref, v_ref, s_ref, u_ref, g_ref, y_ref,
    z_ref, a_ref, gp_ref, gl_ref, in_ref, cg_ref,
):
    length = doc_ref.shape[1]
    doc = doc_ref[0]
    same, strict = masks(doc, length)
    tail, _, carried = ends(doc, length)

    @pl.when(pl.program_id(0) == 0)
    def _():
        cg_ref[...] = jnp.zeros_like(cg_ref)

    logits = []
    kept = tap_masks(doc, length)
    tail, carried = jnp.broadcast_to(tail, (length, HD)), jnp.broadcast_to(carried, (length, HD))
    for h in range(HT):
        lanes = slice(h * HD, (h + 1) * HD)
        q, k, v = q_ref[0, :, lanes], k_ref[0, :, lanes], v_ref[0, :, lanes]
        state, u, g, adj = s_ref[0, h], u_ref[0, :, lanes], g_ref[0, :, lanes], a_ref[0, h]
        rate = rate_ref[0, :, h : h + 1]
        yf = y_ref[0, :, lanes] + dot(z_ref[0, :, lanes], adj)
        y = yf.astype(BF)
        dv = rate * yf
        d1 = dot(y, u, NT) * strict
        gram = dot(k, k, NT)
        e = v.astype(F32) - dot(k, state) * carried
        drate = jnp.sum(yf * e, axis=-1, keepdims=True) - jnp.sum(d1 * gram, axis=-1, keepdims=True)
        dgram = (d1 * (-rate)).astype(BF)
        dscore = (dot(g, u, NT) * same).astype(BF)
        dq = dot(dscore, k) + dot(g, state, NT) * carried
        dk = dot(dscore, q, TN) + dot(dgram, k) + dot(dgram, k, TN)
        dk = dk - dot(y, state, NT) * (rate * carried) + dot(u, adj, NT) * tail
        logits.append(drate * rate * (1.0 - rate))
        for part, grad in enumerate((dq, dk, dv)):
            cols = slice(part * DT + h * HD, part * DT + (h + 1) * HD)
            ext = p_ref[0, :, cols].astype(F32)
            taps = taps_ref[part, :, lanes]
            mixed = conv_rows(ext, taps, kept, length)
            s = jax.nn.sigmoid(mixed)
            if part < 2:
                grad = unit_back(mixed * s, grad, SCALE if part == 0 else 1.0)
            gm = grad * (s * (1.0 + mixed * (1.0 - s)))
            total = jnp.zeros((length + RIM, HD), F32)
            for i in range(CONV):
                gv = gm * kept[i] if i < CONV - 1 else gm
                first = RIM - (CONV - 1) + i
                cg_ref[part, i : i + 1, lanes] += jnp.sum(
                    gv * ext[first : first + length], axis=0, keepdims=True
                )
                gv = gv * taps[i : i + 1]
                pads = [jnp.zeros((first, HD), F32), gv]
                if RIM - first > 0:
                    pads.append(jnp.zeros((RIM - first, HD), F32))
                total = total + jnp.concatenate(pads, axis=0)
            gp_ref[0, :, cols] = total.astype(BF)
    lane = lax.broadcasted_iota(jnp.int32, (length, HD), 1)
    wide = jnp.zeros((length, HD), F32)
    for h in range(HT):
        wide = jnp.where(lane == h, logits[h], wide)
    gl_ref[0, :RIM] = jnp.zeros((RIM, HD), BF)
    gl_ref[0, RIM:] = wide.astype(BF)

    @pl.loop(0, D // 256)
    def _(i):
        span = pl.ds(pl.multiple_of(i * 256, 256), 256)
        total = dot(gp_ref[0], w_ref[span], NT) + dot(gl_ref[0], beta_ref[span], NT)
        in_ref[0, :, span] = total.astype(BF)


def to_rel(x, c, groups):
    half = D // groups // 2
    out = []
    for cc in range(2):
        for i in range(groups):
            at = i * 2 * half
            one, two = x[:, at : at + half], x[:, at + half : at + 2 * half]
            out.append(jnp.where(c == 0, one, two) if cc == 0 else jnp.where(c == 0, two, one))
    return jnp.concatenate(out, axis=1)


def from_rel(x, c, groups):
    half = D // groups // 2
    out = []
    for i in range(groups):
        one, two = x[:, i * half : (i + 1) * half], x[:, (groups + i) * half : (groups + i + 1) * half]
        out += [jnp.where(c == 0, one, two), jnp.where(c == 0, two, one)]
    return jnp.concatenate(out, axis=1)


def norm_kernel(groups, idx_ref, rim_ref, x_ref, gain_ref, n_ref):
    c = idx_ref[0]
    for src, span in ((rim_ref, slice(0, RIM)), (x_ref, slice(RIM, RIM + x_ref.shape[0]))):
        x = src[...].astype(F32)
        r = lax.rsqrt(jnp.mean(x * x, axis=-1, keepdims=True) + EPS)
        n_ref[span] = to_rel(x * r * gain_ref[...], c, groups).astype(BF)


def mid_kernel(groups, idx_ref, n0, n1, n2, n3, w_ref, x_ref, gain_ref, mid_ref, n_ref):
    c = idx_ref[0]
    heads = (n0, n1, n2, n3)

    @pl.loop(0, D // 256)
    def _(i):
        span = pl.ds(pl.multiple_of(i * 256, 256), 256)
        total = x_ref[:, span].astype(F32)
        for j in range(TP):
            total = total + dot(heads[j][...], w_ref[j * DT : (j + 1) * DT, span])
        mid_ref[:, span] = total

    x = mid_ref[...]
    r = lax.rsqrt(jnp.mean(x * x, axis=-1, keepdims=True) + EPS)
    n_ref[...] = to_rel(x * r * gain_ref[...], c, groups).astype(BF)


def norm_back_rows(groups, c, parts, x, gain):
    dy = parts[0].astype(F32)
    for part in parts[1:]:
        dy = dy + part.astype(F32)
    dy = from_rel(dy, c, groups)
    r = lax.rsqrt(jnp.mean(x * x, axis=-1, keepdims=True) + EPS)
    gy = gain * dy
    dx = r * gy - x * (r * r * r * jnp.mean(x * gy, axis=-1, keepdims=True))
    return dx, jnp.sum(x * r * dy, axis=0, keepdims=True)


def mid_back_kernel(
    groups, idx_ref, p0, p1, p2, x_ref, cot_ref, gain_ref, w_ref, gm_ref, away_ref, mine_ref, d0, d1, d2, d3,
    gg_ref, br_ref,
):
    parts = [p[...] for p in (p0, p1, p2)]
    dx, gain_part = norm_back_rows(groups, idx_ref[0], parts, x_ref[...], gain_ref[...])
    grad = cot_ref[...].astype(F32) + dx
    gm_ref[...] = grad
    br_ref[...] = grad.astype(BF)
    gg_ref[...] = gain_part
    col = D // 8
    for j in range(TP):
        for cc, ref in ((1, away_ref), (0, mine_ref)):
            at = (jnp.bitwise_xor(idx_ref[1], j) * 2 + jnp.bitwise_xor(idx_ref[0], cc)) * col
            ref[:, j * col : (j + 1) * col] = br_ref[:, pl.ds(pl.multiple_of(at, 128), col)]
    for j, d_ref in enumerate((d0, d1, d2, d3)):

        @pl.loop(0, DT // 256)
        def _(i):
            at = pl.multiple_of(i * 256, 256)
            d_ref[:, pl.ds(at, 256)] = dot(br_ref[...], w_ref[pl.ds(j * DT + at, 256)], NT).astype(BF)


def in_back_kernel(groups, idx_ref, p0, p1, p2, x_ref, base_ref, gain_ref, out_ref, gg_ref):
    parts = [p[...] for p in (p0, p1, p2)]
    dx, gain_part = norm_back_rows(groups, idx_ref[0], parts, x_ref[...].astype(F32), gain_ref[...])
    out_ref[...] = base_ref[...] + dx
    gg_ref[...] = gain_part


def ffn_kernel(*refs):
    idx_ref, xs, cs, gus, downs = refs[0], refs[1:6], refs[6:11], refs[11:13], refs[13:21]
    hid_ref, gg_ref, part_ref, away_ref, mine_ref, x_ref, d_ref, c_ref, w_ref = refs[22:31]
    x_sem, c_sem, w_sem, d_sem = refs[31:]
    length = hid_ref.shape[1]
    c, t = idx_ref[0], idx_ref[1]
    step = pl.program_id(0)
    depth = gus[0].shape[0]
    col = downs[0].shape[1]

    def x_copies():
        return row_copies(xs, x_ref, x_sem)

    def c_copies():
        return row_copies(cs, c_ref, c_sem)

    def w_copies():
        return [
            pltpu.make_async_copy(gus[i], w_ref.at[pl.ds(i * depth, depth)], w_sem.at[i]) for i in range(2)
        ]

    def d_copies():
        out = []
        for cc in range(2):
            for j in range(TP):
                at = (jnp.bitwise_xor(t, j) * 2 + jnp.bitwise_xor(c, cc)) * col
                n = cc * TP + j
                out.append(
                    pltpu.make_async_copy(
                        downs[n], d_ref.at[:, pl.ds(pl.multiple_of(at, 128), col)], d_sem.at[n]
                    )
                )
        return out

    @pl.when(step == 0)
    def _():
        first = w_copies() + x_copies()
        for copy in first + c_copies() + d_copies():
            copy.start()
        for copy in first:
            copy.wait()

    here = pl.ds(pl.multiple_of(step * length, 16), length)

    def hidden_tile(at, width):
        cols = pl.ds(at, width)
        ups = pl.ds(pl.multiple_of(FT + at, 128), width)
        x = x_ref[here]
        gate, up = dot(x, w_ref[:, cols]), dot(x, w_ref[:, ups])
        grad = dot(c_ref[here], d_ref[cols], NT)
        sg = jax.nn.sigmoid(gate)
        act = gate * sg
        hid_ref[0, :, cols] = (act * up).astype(BF)
        gg_ref[0, :, cols] = (grad * up * (sg * (1.0 + gate * (1.0 - sg)))).astype(BF)
        gg_ref[0, :, ups] = (grad * act).astype(BF)

    @pl.when(step == 0)
    def _():
        for copy in c_copies() + d_copies():
            copy.wait()

    tiles = FT // 256

    @pl.loop(0, tiles)
    def _(i):
        hidden_tile(pl.multiple_of(i * 256, 256), 256)

    if FT % 256:
        hidden_tile(tiles * 256, FT % 256)

    @pl.loop(0, D // 256)
    def _(i):
        span = pl.ds(pl.multiple_of(i * 256, 256), 256)
        part_ref[0, :, span] = dot(gg_ref[0], w_ref[span], NT).astype(BF)

    for j in range(TP):
        for cc, ref in ((1, away_ref), (0, mine_ref)):
            at = (jnp.bitwise_xor(t, j) * 2 + jnp.bitwise_xor(c, cc)) * col
            ref[0, :, j * col : (j + 1) * col] = c_ref[here, pl.ds(pl.multiple_of(at, 128), col)]


def whole_call(kernel, idx, ins, outs, us=5, scratch=()):
    return pl.pallas_call(
        kernel,
        in_specs=[pl.BlockSpec(memory_space=pltpu.SMEM)]
        + [pl.BlockSpec(memory_space=pltpu.VMEM)] * len(ins),
        out_specs=[pl.BlockSpec(memory_space=pltpu.VMEM)] * len(outs),
        out_shape=[jax.ShapeDtypeStruct(s, d) for s, d in outs],
        scratch_shapes=list(scratch),
        compiler_params=pltpu.CompilerParams(vmem_limit_bytes=VMEM),
        cost_estimate=cost(us),
    )(idx, *ins)


def assemble(idx, pieces, plan, shape, us=5):
    count = len(plan([0, 0, 0]))

    def kernel(idx_ref, *refs):
        srcs, out, sem = refs[: len(pieces)], refs[-2], refs[-1]
        copies = [
            pltpu.make_async_copy(srcs[p].at[src], out.at[dst], sem.at[n])
            for n, (p, src, dst) in enumerate(plan(idx_ref))
        ]
        for copy in copies:
            copy.start()
        for copy in copies:
            copy.wait()

    dtype = pieces[0].dtype
    return pl.pallas_call(
        kernel,
        in_specs=[pl.BlockSpec(memory_space=pltpu.SMEM)] + [pl.BlockSpec(memory_space=pl.ANY)] * len(pieces),
        out_specs=pl.BlockSpec(memory_space=pltpu.VMEM),
        out_shape=jax.ShapeDtypeStruct(shape, dtype),
        scratch_shapes=[pltpu.SemaphoreType.DMA((count,))],
        compiler_params=pltpu.CompilerParams(vmem_limit_bytes=VMEM),
        cost_estimate=cost(us),
    )(idx, *pieces)


def split_at(rows):
    return rows // 32 * 16


def chunk_of(rows, cap):
    best = 16
    for q in range(16, cap + 1, 16):
        if rows % q == 0:
            best = q
    return best


def join_kernel(groups, idx_ref, g0, g1, g2, g3, out_ref):
    t = idx_ref[1]
    got = (g0, g1, g2, g3)
    shard, ff_shard = D // groups, FF // groups
    for i in range(groups):
        span = slice(i * shard, (i + 1) * shard)
        total = got[0][span].astype(F32)
        for x in got[1:]:
            total = total + x[span].astype(F32)
        out_ref[i, :shard] = total.astype(BF)
    per = groups // TP
    for j in range(TP):
        chip = jnp.bitwise_xor(t, j)
        for i in range(per):
            out_ref[chip * per + i, shard:] = got[j][D + i * ff_shard : D + (i + 1) * ff_shard]


def spread_first(x):
    return [x, plane_swap(x, 1), plane_swap(x, 2)]


def spread_pieces(first):
    x, a, b = first
    h = split_at(x.shape[0])
    mine = [x, a, b, plane_swap(a[:h], 2), plane_swap(b[h:], 1)]
    return mine + [core_swap(p) for p in mine]


def spread_out(idx, first, parts, heights=None):
    pieces = first if len(first) == 10 else spread_pieces(first)
    rows, cols = pieces[0].shape
    h = split_at(rows)
    width = cols // parts if parts else cols
    outs = []
    start = 0
    for height in heights or (rows,):
        edges = [start, start + height] + ([h] if start < h < start + height else [])
        q = 16
        for n in range(16, (64 if parts else 256) + 1, 16):
            if all((e - start) % n == 0 for e in edges) and start % n == 0 and h % n == 0:
                q = n
        outs.append(spread_part(idx, pieces, parts, width, start, height, h, q))
        start += height
    return outs


def gather_eight(x):
    n = lax.axis_size("replica")
    blocks = [list(range(i, i + 8)) for i in range(0, n, 8)]
    return lax.all_gather(x, "replica", axis=0, axis_index_groups=blocks if n > 8 else None)


def spread_abs(x, parts, start, height):
    _, rows, cols = x.shape
    width = cols // parts if parts else cols
    q = 16
    for n in range(16, (64 if parts else 128) + 1, 16):
        if height % n == 0 and start % n == 0:
            q = n
    base = start // q

    def kernel(x_ref, out):
        for r in range(8):
            chip, core = r // 2, r % 2
            if parts:
                for p in range(parts):
                    at = (p * TP + chip) * width
                    out[core, :, at : at + width] = x_ref[r, :, p * width : (p + 1) * width].astype(F32)
            else:
                out[:, r * width : (r + 1) * width] = x_ref[r].astype(F32)

    if parts:
        shape, out_spec = (2, height, TP * cols), pl.BlockSpec((2, q, TP * cols), lambda i: (0, i, 0))
    else:
        shape, out_spec = (height, 8 * cols), pl.BlockSpec((q, 8 * cols), lambda i: (i, 0))
    out = pl.pallas_call(
        kernel,
        grid=(height // q,),
        in_specs=[pl.BlockSpec((8, q, cols), lambda i: (0, i + base, 0))],
        out_specs=out_spec,
        out_shape=jax.ShapeDtypeStruct(shape, F32),
        compiler_params=pltpu.CompilerParams(vmem_limit_bytes=VMEM),
        cost_estimate=cost(height * cols * 16e-6),
    )(x)
    return out.reshape(-1, out.shape[-1])


def spread_part(idx, pieces, parts, width, start, height, h, q):
    cols = pieces[0].shape[1]
    rows = pieces[0].shape[0]
    cut, base = h // q, start // q

    def kernel(idx_ref, *refs):
        srcs, out = refs[:-1], refs[-1]
        c, t = idx_ref[0], idx_ref[1]
        i = pl.program_id(0) + base
        for cc in range(2):
            core = jnp.bitwise_xor(c, cc)

            def put(j, value):
                chip = jnp.bitwise_xor(t, j)
                if parts:
                    for p in range(parts):
                        at = pl.multiple_of((p * TP + chip) * width, 128)
                        out[core, :, pl.ds(at, width)] = value[:, p * width : (p + 1) * width].astype(F32)
                else:
                    at = pl.multiple_of((chip * 2 + core) * width, 128)
                    out[:, pl.ds(at, width)] = value.astype(F32)

            for j in range(3):
                put(j, srcs[5 * cc + j][...])

            @pl.when(i < cut)
            def _():
                put(3, srcs[5 * cc + 3][...])

            @pl.when(i >= cut)
            def _():
                put(3, srcs[5 * cc + 4][...])

    most = (rows - h) // q - 1
    full = pl.BlockSpec((q, cols), lambda i: (i + base, 0))
    low = pl.BlockSpec((q, cols), lambda i: (jnp.minimum(i + base, cut - 1), 0))
    high = pl.BlockSpec((q, cols), lambda i: (jnp.clip(i + base - cut, 0, most), 0))
    if parts:
        shape, out_spec = (2, height, TP * cols), pl.BlockSpec((2, q, TP * cols), lambda i: (0, i, 0))
    else:
        shape, out_spec = (height, 8 * cols), pl.BlockSpec((q, 8 * cols), lambda i: (i, 0))
    out = pl.pallas_call(
        kernel,
        grid=(height // q,),
        in_specs=[pl.BlockSpec(memory_space=pltpu.SMEM)] + [full, full, full, low, high] * 2,
        out_specs=out_spec,
        out_shape=jax.ShapeDtypeStruct(shape, F32),
        compiler_params=pltpu.CompilerParams(vmem_limit_bytes=VMEM),
        cost_estimate=cost(0.05),
    )(idx, *pieces)
    return out.reshape(-1, out.shape[-1])


def cost(us):
    return pl.CostEstimate(flops=int(us * 1.1e9), bytes_accessed=0, transcendentals=0)


def block(shape, fixed=False):
    zeros = (0,) * len(shape)
    if fixed:
        return pl.BlockSpec(tuple(shape), lambda i: zeros, pipeline_mode=pl.Buffered(1))
    return pl.BlockSpec((1,) + tuple(shape[1:]), lambda i: (i,) + zeros[1:])


def call(kernel, ins, fixed_ins, outs, fixed_outs=(), us=10, extra=(), scratch=(), held_outs=()):
    count = ins[-1].shape[0]
    out_specs = []
    for i, (shape, _) in enumerate(outs):
        zeros = (0,) * len(shape)
        if i in held_outs:
            spec = pl.BlockSpec(shape, lambda i, z=zeros: z, pipeline_mode=pl.Buffered(1))
        elif i in fixed_outs:
            spec = pl.BlockSpec(shape, lambda i, z=zeros: z)
        else:
            spec = block(shape)
        out_specs.append(spec)
    lead = [pl.BlockSpec(memory_space=pltpu.SMEM)] + [pl.BlockSpec(memory_space=pl.ANY)] * (len(extra) - 1)
    return pl.pallas_call(
        kernel,
        grid=(count,),
        in_specs=(lead if extra else []) + [block(x.shape, i in fixed_ins) for i, x in enumerate(ins)],
        out_specs=out_specs,
        out_shape=[jax.ShapeDtypeStruct(s, d) for s, d in outs],
        scratch_shapes=list(scratch),
        compiler_params=pltpu.CompilerParams(vmem_limit_bytes=VMEM),
        cost_estimate=cost(us),
    )(*extra, *ins)


def mm(a, b, dims=((1,), (0,))):
    return lax.dot_general(a, b, (dims, ((), ())), preferred_element_type=F32)


def body(
    tokens,
    cotangent,
    doc_start,
    norm_gain,
    qkv_weight,
    conv_weight,
    beta_weight,
    head_gain,
    out_weight,
    ffn_gain,
    gate_up_weight,
    down_weight,
):
    groups = lax.axis_size("group")
    r = lax.axis_index("replica") % 8
    g = lax.axis_index("group")
    c, t = r % 2, r // 2
    idx = jnp.stack([c, t, g]).astype(jnp.int32)
    _, length, _ = tokens.shape
    seqs = TP
    ext_len = length + RIM
    shard = D // groups
    half = shard // 2
    ff_shard = FF // groups
    col = D // 8
    tokens = tokens.reshape(length, D)
    cot = cotangent.reshape(length, D)

    def z_pieces(x):
        return [x] + [z_turn(x, s) for s in range(1, groups)]

    def z_abs(x):
        pieces = z_pieces(x)
        return place([((g - s) % groups, piece) for s, piece in enumerate(pieces)], groups)

    def rel(x):
        x = x.reshape(x.shape[:-1] + (groups, 2, half))
        x = jnp.where(c == 0, x, jnp.flip(x, -2))
        return jnp.swapaxes(x, -3, -2).reshape(x.shape[:-3] + (D,))

    def unrel(x):
        x = jnp.swapaxes(x.reshape(x.shape[:-1] + (2, groups, half)), -3, -2)
        x = jnp.where(c == 0, x, jnp.flip(x, -2))
        return x.reshape(x.shape[:-3] + (D,))

    small = jnp.concatenate(
        [
            beta_weight.T,
            jnp.swapaxes(conv_weight.reshape(3, shard, CONV), 1, 2).reshape(3 * CONV, shard),
            ffn_gain.reshape(1, shard),
            norm_gain.reshape(1, shard),
            jnp.zeros((2, shard), BF),
        ],
        axis=0,
    )
    rim = z_shift(tokens[length - RIM :], 1)
    small = z_abs(small)
    gain_in = small[:, HEADS + 3 * CONV + 1].reshape(1, D).astype(F32)
    gain_mid = small[:, HEADS + 3 * CONV].reshape(1, D).astype(F32)
    beta_full = jnp.swapaxes(small[:, :HEADS], 0, 1).reshape(HEADS, D)
    beta_t = jnp.pad(rel(lax.dynamic_slice(beta_full, (t * HT, 0), (HT, D))).T, ((0, 0), (0, HD - HT)))
    conv_full = small[:, HEADS : HEADS + 3 * CONV].reshape(groups * 3, CONV, shard)
    conv_full = jnp.swapaxes(conv_full, 0, 1).reshape(CONV, 3, TP, DT)
    taps = jnp.swapaxes(pick(conv_full, t, 2), 0, 1).astype(F32)
    gain_head = head_gain.astype(F32).reshape(1, HD)
    doc_rel = doc_start.reshape(1, length) - g * length
    docs = jnp.concatenate(
        [doc_rel] + [plane_swap(doc_rel, j) for j in (1, 2, 3)], axis=0
    ).reshape(seqs, length, 1)
    cot_x, cot_y = plane_swap(cot, 1), plane_swap(cot, 2)
    qkv_weight, small, rim = lax.optimization_barrier((qkv_weight, small, rim))

    (normed_ext,) = whole_call(
        functools.partial(norm_kernel, groups), idx, [rim, tokens, gain_in], [((ext_len, D), BF)]
    )
    normed_pieces = plane_copies(normed_ext)

    piece = jnp.concatenate(
        [lax.dynamic_slice(qkv_weight, (c * half, j * D + t * DT), (half, DT)) for j in range(3)], axis=1
    )
    qkv_pieces = z_pieces(piece)
    qkv_late = qkv_pieces
    qkv_pieces = qkv_pieces + [core_swap(p) for p in qkv_pieces]

    h = split_at(length)
    cot_pieces = [cot, cot_x, cot_y, plane_swap(cot_x[:h], 2), plane_swap(cot_y[h:], 1)]

    piece = jnp.concatenate(
        [
            lax.dynamic_slice(out_weight, (0, r * col), (shard, col)),
            lax.dynamic_slice(down_weight, (0, r * col), (ff_shard, col)),
        ],
        axis=0,
    )
    both = lax.all_gather(after(piece, *qkv_late), "group", axis=0)

    normed_pieces[0] = after(normed_pieces[0], *cot_pieces[:3])

    wide = (seqs, length, DT)
    square = (seqs, HT, HD, HD)
    (
        queries, key_rows, value_rows, inverse, u0, w, move, free, projected, rates, normed_all, qkv,
    ) = call(
        functools.partial(front_kernel, groups),
        [beta_t, taps, docs],
        (0, 1),
        [
            (wide, BF),
            (wide, BF),
            (wide, BF),
            ((seqs, HT, length, length), BF),
            (wide, F32),
            (wide, BF),
            (square, BF),
            (square, F32),
            ((seqs, ext_len, 3 * DT), BF),
            ((seqs, length, HD), F32),
            ((seqs * ext_len, D), BF),
            ((D, 3 * DT), BF),
        ],
        us=40,
        extra=[idx, *normed_pieces, *qkv_pieces],
        scratch=[pltpu.SemaphoreType.DMA((5,)), pltpu.SemaphoreType.DMA((2 * groups,))],
        held_outs=(10, 11),
    )
    piece = jnp.concatenate(
        [
            lax.dynamic_slice(gate_up_weight, (c * half, j * FF + t * FT), (half, FT))
            for j in range(2)
        ],
        axis=1,
    )
    gate_up = lax.all_gather(after(piece, free), "group", axis=0, tiled=True)

    state = jnp.zeros(square, BF)
    for hop in range(groups - 1):
        leaving = jnp.einsum("shij,shjk->shik", move, state, preferred_element_type=F32) + free
        if hop == groups - 2:
            leaving = after(leaving, *downs, *outs)
        state = z_shift(leaving.astype(BF), 1)
        if hop == 0:
            both = after(both, free)
            part = both[:, shard:].reshape(TP, FT, col)
            downs = plane_trade([pick(part, t ^ j) for j in range(TP)])
            outs = both[:, :shard].reshape(D, col)
            outs = plane_copies(outs)
    outs = outs + [core_swap(p) for p in outs]
    downs = downs + [core_swap(p) for p in downs]
    normed, head_out, update = call(
        out_kernel,
        [gain_head, queries, key_rows, u0, w, state, docs],
        (0,),
        [(wide, BF), (wide, F32), (wide, BF)],
        us=6,
    )

    def plan(ref):
        moves = []
        for cc in range(2):
            for j in range(TP):
                at = ((ref[1] ^ j) * 2 + (ref[0] ^ cc)) * col
                for b in range(TP):
                    n, first = (j, b) if j < 3 else ((3, b) if b < 2 else (4, b - 2))
                    moves.append(
                        (
                            5 * cc + n,
                            pl.ds(first * DT, DT),
                            (
                                pl.ds(pl.multiple_of((ref[1] ^ b) * DT, DT), DT),
                                pl.ds(pl.multiple_of(at, 128), col),
                            ),
                        )
                    )
        return moves

    out_w = assemble(idx, outs, plan, (D, D))

    heads = plane_trade([normed[j] for j in range(TP)])
    middle, normed_mid = whole_call(
        functools.partial(mid_kernel, groups),
        idx,
        heads + [out_w, tokens, gain_mid],
        [((length, D), F32), ((length, D), BF)],
        us=10,
    )
    mid_pieces = plane_copies(normed_mid)
    gate_ups = [gate_up, core_swap(after(gate_up, mid_pieces[1], mid_pieces[2]))]

    hidden, grad_gate_up, mid_part, cot_away, cot_mine, mid_all, down = call(
        ffn_kernel,
        [docs],
        (),
        [
            ((seqs, length, FT), BF),
            ((seqs, length, 2 * FT), BF),
            ((seqs, length, D), BF),
            ((seqs, length, D // 2), BF),
            ((seqs, length, D // 2), BF),
            ((seqs * length, D), BF),
            ((FT, D), BF),
        ],
        us=45,
        extra=[idx, *mid_pieces, *cot_pieces, *gate_ups, *downs],
        scratch=[pltpu.VMEM((seqs * length, D), BF), pltpu.VMEM((D, 2 * FT), BF)]
        + [pltpu.SemaphoreType.DMA((n,)) for n in (5, 5, 2, 8)],
        held_outs=(5, 6),
    )
    hidden = hidden.reshape(-1, FT)
    grad_gate_up = grad_gate_up.reshape(-1, 2 * FT)
    def two_halves(left, right):
        away = mm(left[:, groups * half :], right, TN).astype(BF)
        mine = mm(left[:, : groups * half], right, TN)
        return (mine + core_swap(away).astype(F32)).astype(BF).reshape(groups, half, -1)

    def two_columns(left, away, mine):
        away = mm(left, away, TN).astype(BF)
        mine = mm(left, mine, TN)
        return (mine + core_swap(away).astype(F32)).astype(BF)

    def z_sum(x, *others):
        total = pick(x, g).astype(F32)
        for s in range(1, groups):
            total = total + after(z_turn(pick(x, (g + s) % groups), s), *others).astype(F32)
        return total

    parts = plane_parts([mid_part[j] for j in range(TP)])
    gate_sums = [two_halves(mid_all, grad_gate_up[:, i * FT : (i + 1) * FT]) for i in range(2)]
    down_sum = two_columns(hidden, cot_away.reshape(-1, D // 2), cot_mine.reshape(-1, D // 2))
    first_sum = far_sum(lax.psum_scatter(gate_sums[0], "group", scatter_dimension=0)).astype(BF)
    parts, second_sum, down_sum = lax.optimization_barrier((parts, gate_sums[1], down_sum))
    second_sum = far_sum(lax.psum_scatter(second_sum, "group", scatter_dimension=0)).astype(BF)
    grad_middle, branch_away, branch_mine, *dheads, ffn_gain_part = whole_call(
        functools.partial(mid_back_kernel, groups),
        idx,
        parts + [middle.reshape(length, D), cot, gain_mid, out_w],
        [((length, D), F32)]
        + [((length, D // 2), BF)] * 2
        + [((length, DT), BF)] * TP
        + [((1, D), F32)],
        us=13,
        scratch=[pltpu.VMEM((length, D), BF)],
    )
    dnormed = jnp.stack(plane_trade(dheads))

    normed_abs = jnp.swapaxes(
        place([(t ^ j, heads[j]) for j in range(TP)], TP), 0, 1
    ).reshape(length, D)
    out_sum = two_columns(normed_abs, branch_away, branch_mine)
    both = [
        jnp.concatenate([x[:, j * col : (j + 1) * col] for x in (out_sum, down_sum)], axis=0)
        for j in range(TP)
    ]
    dnormed = after(dnormed, first_sum, *both)
    both = plane_trade(both)

    grad_out, y0, z, local, head_part = call(
        back_kernel,
        [gain_head, dnormed, head_out, queries, key_rows, inverse, rates, docs],
        (0,),
        [(wide, BF), (wide, F32), (wide, BF), (square, F32), ((8, HD), F32)],
        (4,),
        us=12,
    )

    out_part = mm(hidden, down).astype(BF).reshape(TP, length, D)

    later = jnp.zeros(square, BF)
    for hop in range(groups - 1):
        leaving = jnp.einsum("shji,shjk->shik", move, later, preferred_element_type=F32) + local
        if hop == 1:
            leaving = after(leaving, out_part)
        later = z_shift(leaving.astype(BF), -1)

    (both_sum,) = whole_call(
        functools.partial(join_kernel, groups), idx, both, [((groups, shard + ff_shard, col), BF)]
    )
    later = after(later, both_sum, second_sum)
    gate_sum = jnp.concatenate([first_sum, second_sum], axis=1)
    both_sum = lax.psum_scatter(both_sum, "group", scatter_dimension=0)
    gate_pieces = spread_first(gate_sum)
    grad_proj, grad_logit, in_part, conv_part = call(
        grad_kernel,
        [
            taps, qkv, beta_t, projected, docs, rates, queries, key_rows, value_rows, state, update, grad_out,
            y0, z, later,
        ],
        (0, 1, 2),
        [
            ((seqs, ext_len, 3 * DT), BF),
            ((seqs, ext_len, HD), BF),
            ((seqs, ext_len, D), BF),
            ((3, CONV, DT), F32),
        ],
        (3,),
        us=44,
    )
    qkv_sum = two_halves(normed_all, grad_proj.reshape(-1, 3 * DT))
    gate_pieces = spread_pieces([after(p, qkv_sum) for p in gate_pieces])
    rim = z_shift(in_part[:, :RIM], -1)
    in_part = after(in_part[:, RIM:], qkv_sum)
    qkv_sum = z_sum(qkv_sum)
    ends_in = (in_part[:, length - RIM :].astype(F32) + rim.astype(F32)).astype(BF)
    in_part = jnp.concatenate([in_part[:, : length - RIM], ends_in], axis=1)
    parts = plane_parts([in_part[j] for j in range(TP)])
    parts[0] = after(parts[0], qkv_sum)
    input_grad, norm_gain_part = whole_call(
        functools.partial(in_back_kernel, groups),
        idx,
        parts + [tokens, grad_middle, gain_in],
        [((length, D), F32), ((1, D), F32)],
        us=0.05,
    )
    output = (middle + plane_sum([out_part[j] for j in range(TP)])).astype(BF)

    beta_part = mm(grad_logit.reshape(-1, HD), normed_all, TN)[:HT]
    beta_all = lax.dynamic_update_slice(jnp.zeros((HEADS, D), F32), unrel(beta_part), (t * HT, 0))
    conv_all = lax.dynamic_update_slice(
        jnp.zeros((CONV, 3, TP, DT), F32), jnp.swapaxes(conv_part, 0, 1)[:, :, None], (0, 0, t, 0)
    )
    conv_all = jnp.swapaxes(conv_all.reshape(CONV, groups * 3, shard), 0, 1)
    pack = jnp.concatenate(
        [
            jnp.swapaxes(beta_all.reshape(HEADS, groups, shard), 0, 1),
            conv_all.reshape(groups, 3 * CONV, shard),
            norm_gain_part.reshape(groups, 1, shard),
            ffn_gain_part.reshape(groups, 1, shard),
            jnp.broadcast_to(jnp.pad(head_part[:1], ((0, 0), (0, shard - HD))), (groups, 1, shard)),
            jnp.zeros((groups, 1, shard), F32),
        ],
        axis=1,
    )
    pack = pack + core_swap(pack)
    pack = pack + plane_swap(pack, 1)
    pack = pack + plane_swap(pack, 2)

    (gate_up_grad,) = spread_out(idx, gate_pieces, 2)

    total = far_sum(z_sum(after(pack, qkv_sum)))
    both_pieces = [after(p, qkv_sum) for p in spread_first(far_sum(both_sum).astype(BF))]
    qkv_pieces = [after(p, gate_up_grad, output) for p in spread_first(far_sum(qkv_sum).astype(BF))]
    qkv_pieces = spread_pieces(qkv_pieces)
    out_grad, down_grad = spread_out(idx, both_pieces, 0, (shard, ff_shard))
    qkv_pieces[0] = after(qkv_pieces[0], total, out_grad, down_grad)
    (qkv_grad,) = spread_out(idx, qkv_pieces, 3)
    beta_grad = total[:HEADS].T
    conv_grad = jnp.swapaxes(total[HEADS : HEADS + 3 * CONV].reshape(3, CONV, shard), 1, 2)
    at = HEADS + 3 * CONV
    return (
        output.reshape(1, length, D),
        input_grad.reshape(1, length, D),
        total[at],
        qkv_grad,
        conv_grad.reshape(-1, CONV),
        beta_grad,
        total[at + 2, :HD],
        out_grad,
        total[at + 1],
        gate_up_grad,
        down_grad,
    )


def solution(mesh):
    rows = P("replica", "group", None)
    shard = P("group", None)
    return jax.shard_map(
        body,
        mesh=mesh,
        in_specs=(
            rows, rows, P("replica", "group"), P("group"), shard, shard, shard, P(), shard, P("group"), shard, shard,
        ),
        out_specs=(
            rows, rows, P("group"), shard, shard, shard, P(), shard, P("group"), shard, shard,
        ),
        check_vma=False,
    )
```

```python
import functools

import jax
import jax.numpy as jnp
from jax import lax
from jax.experimental import pallas as pl
from jax.experimental.pallas import tpu as pltpu
from jax.sharding import PartitionSpec as P

D = 2048
HEADS = 16
HD = 128
FF = 5632
CONV = 4
EPS = 1e-06
RIM = 16
TP = 4
HT = HEADS // TP
DT = D // TP
FT = FF // TP
SCALE = HD**-0.5
VMEM = 56 * 1024 * 1024

BF = jnp.bfloat16
F32 = jnp.float32


def swap(x, bits):
    n = lax.axis_size("replica")
    return lax.ppermute(x, "replica", [(i, i ^ bits) for i in range(n)])


def plane_swap(x, j):
    return swap(x, 2 * j)


def core_swap(x):
    return swap(x, 1)


def far_sum(x):
    x = x.astype(F32)
    bits = 8
    while bits < lax.axis_size("replica"):
        x = x + swap(x.astype(BF), bits).astype(F32)
        bits *= 2
    return x


def z_shift(x, by):
    n = lax.axis_size("group")
    return lax.ppermute(x, "group", [(i, i + by) for i in range(n) if 0 <= i + by < n])


def z_turn(x, by):
    n = lax.axis_size("group")
    return lax.ppermute(x, "group", [(i, (i + by) % n) for i in range(n)])


def plane_copies(x):
    a, b = plane_swap(x, 1), plane_swap(x, 2)
    h = split_at(x.shape[0])
    return [x, a, b, plane_swap(a[:h], 2), plane_swap(b[h:], 1)]


def plane_parts(parts):
    own, x, y, d = parts
    h = split_at(own.shape[0])
    via_x, via_y = plane_swap(d[:h], 1), plane_swap(d[h:], 2)
    y = jnp.concatenate([(y[:h].astype(F32) + via_x.astype(F32)).astype(BF), y[h:]], axis=0)
    x = jnp.concatenate([x[:h], (x[h:].astype(F32) + via_y.astype(F32)).astype(BF)], axis=0)
    return [own, plane_swap(x, 1), plane_swap(y, 2)]


def plane_sum(parts):
    own, x, y = plane_parts([p.astype(BF) for p in parts])
    return parts[0].astype(F32) + x.astype(F32) + y.astype(F32)


def after(x, *others):
    return lax.optimization_barrier((x, *others))[0]


def plane_trade(parts):
    return [parts[0]] + [plane_swap(parts[j], j) for j in (1, 2, 3)]


def place(pieces, count, axis=0):
    shape = list(pieces[0][1].shape)
    shape.insert(axis, count)
    buf = jnp.zeros(shape, pieces[0][1].dtype)
    for index, piece in pieces:
        buf = lax.dynamic_update_index_in_dim(buf, piece, index, axis)
    return buf


def pick(x, index, axis=0):
    return lax.dynamic_index_in_dim(x, index, axis, keepdims=False)


def dot(a, b, dims=((1,), (0,))):
    return lax.dot_general(a, b, (dims, ((), ())), preferred_element_type=F32)


NT = ((1,), (1,))
TN = ((0,), (0,))


def iotas(rows, cols):
    return (
        lax.broadcasted_iota(jnp.int32, (rows, cols), 0),
        lax.broadcasted_iota(jnp.int32, (rows, cols), 1),
    )


def unit_lower_inverses(mats):
    n = mats[0].shape[0]
    base, tile = 16, 128
    ri, ci = iotas(n, n)
    lane = lax.broadcasted_iota(jnp.int32, (base, tile), 1) % base
    rows = lax.broadcasted_iota(jnp.int32, (base, tile), 0)
    picks = [lane == j for j in range(base)]
    rt, ct = iotas(tile, tile)
    same = (rt // base) == (ct // base)
    ones = same.astype(BF)
    zero = jnp.zeros((), BF)
    lows = [a.astype(BF) for a in mats]
    spans = [slice(at, at + tile) for at in range(0, n, tile)]
    blocks = [(m, span) for m in range(len(mats)) for span in spans]
    wides = []
    for m, span in blocks:
        part = jnp.where(same, mats[m][span, span], 0.0)
        compact = jnp.sum(part.reshape(tile // base, base, tile), axis=0).astype(BF)
        spread = jnp.concatenate([jnp.where(p, compact, zero) for p in picks], axis=0)
        wides.append(dot(spread, ones))
    xs = [(lane == rows).astype(F32)] * len(blocks)
    for j in range(base - 1):
        xs = [x - w[j * base : (j + 1) * base] * x[j : j + 1] for x, w in zip(xs, wides)]
    fulls = [jnp.where(same, jnp.concatenate([x] * (tile // base), axis=0), 0.0) for x in xs]
    size = base
    while size < tile:
        part = (
            ((rt // (2 * size)) == (ct // (2 * size)))
            & ((rt // size) % 2 == 1)
            & ((ct // size) % 2 == 0)
        )
        halves = [full.astype(BF) for full in fulls]
        inner = [
            dot(jnp.where(part, lows[m][span, span], zero), h).astype(BF)
            for (m, span), h in zip(blocks, halves)
        ]
        fulls = [full - dot(h, i) for full, h, i in zip(fulls, halves, inner)]
        size *= 2
    fulls = [full.astype(BF) for full in fulls]
    if n == tile:
        return fulls
    inner = [dot(low[tile:, :tile], fulls[2 * m]).astype(BF) for m, low in enumerate(lows)]
    corners = [-dot(fulls[2 * m + 1], i) for m, i in enumerate(inner)]
    blank = jnp.zeros((tile, tile), BF)
    return [
        jnp.concatenate(
            [
                jnp.concatenate([fulls[2 * m], blank], axis=1),
                jnp.concatenate([corner.astype(BF), fulls[2 * m + 1]], axis=1),
            ],
            axis=0,
        )
        for m, corner in enumerate(corners)
    ]


def tap_masks(doc, length):
    pos = lax.broadcasted_iota(jnp.int32, (length, 1), 0)
    return [
        jnp.broadcast_to((pos - (CONV - 1) + i >= doc).astype(F32), (length, HD)) for i in range(CONV - 1)
    ]


def conv_rows(ext, taps, kept, length):
    total = ext[RIM : RIM + length] * taps[CONV - 1 : CONV]
    for i in range(CONV - 1):
        first = RIM - (CONV - 1) + i
        total = total + ext[first : first + length] * taps[i : i + 1] * kept[i]
    return total


def masks(doc, length):
    ri, ci = iotas(length, length)
    same = (doc <= ci) & (ri >= ci)
    return same.astype(F32), (same & (ri > ci)).astype(F32)


def ends(doc, length):
    last = doc[length - 1 : length]
    pos = lax.broadcasted_iota(jnp.int32, (length, 1), 0)
    return (pos >= last).astype(F32), (last < 0).astype(F32), (doc < 0).astype(F32)


def row_starts(n):
    return (0, n, 2 * n, 3 * n, 3 * n + split_at(n))


def row_copies(srcs, dst, sem):
    starts = row_starts(srcs[0].shape[0])
    return [
        pltpu.make_async_copy(src, dst.at[pl.ds(starts[i], src.shape[0])], sem.at[i])
        for i, src in enumerate(srcs)
    ]


def front_kernel(groups, *refs):
    idx_ref, xs, ws = refs[0], refs[1:6], refs[6 : 6 + 2 * groups]
    (
        beta_ref, taps_ref, doc_ref, qo, ko, vo, t_ref, u0_ref, wo_ref, m_ref, b_ref, p_ref, rate_ref,
        all_ref, w_ref, x_sem, w_sem,
    ) = refs[6 + 2 * groups :]
    length = doc_ref.shape[1]
    half = ws[0].shape[0]
    step = pl.program_id(0)

    @pl.when(step == 0)
    def _():
        copies = row_copies(xs, all_ref, x_sem)
        for cc in range(2):
            for s in range(groups):
                at = (cc * groups + (idx_ref[2] + groups - s) % groups) * half
                copies.append(
                    pltpu.make_async_copy(
                        ws[cc * groups + s],
                        w_ref.at[pl.ds(pl.multiple_of(at, 128), half)],
                        w_sem.at[cc * groups + s],
                    )
                )
        for copy in copies:
            copy.start()
        for copy in copies:
            copy.wait()

    rows = length + RIM
    here = pl.ds(pl.multiple_of(step * rows, 16), rows)
    doc = doc_ref[0]
    same, strict = masks(doc, length)
    tail, keep, carried = ends(doc, length)
    eye = (iotas(HD, HD)[0] == iotas(HD, HD)[1]).astype(F32)

    for i in range(3 * DT // 256):
        cols = slice(i * 256, (i + 1) * 256)
        p_ref[0, :, cols] = dot(all_ref[here], w_ref[:, cols]).astype(BF)

    own = pl.ds(pl.multiple_of(step * rows + RIM, 16), length)
    rates = jax.nn.sigmoid(dot(all_ref[own], beta_ref[...]))
    rate_ref[0] = rates
    kept = tap_masks(doc, length)
    wide = (length, HD)
    tail, carried = jnp.broadcast_to(tail, wide), jnp.broadcast_to(carried, wide)
    head_rates = [jnp.broadcast_to(rates[:, h : h + 1], wide) for h in range(HT)]
    lanes = [slice(h * HD, (h + 1) * HD) for h in range(HT)]
    mats = []
    for h in range(HT):
        acts = []
        for part in range(3):
            cols = slice(part * DT + h * HD, part * DT + (h + 1) * HD)
            mixed = conv_rows(p_ref[0, :, cols].astype(F32), taps_ref[part, :, lanes[h]], kept, length)
            acts.append(mixed * jax.nn.sigmoid(mixed))
        qa, ka, va = acts
        q = (qa * (lax.rsqrt(jnp.sum(qa * qa, axis=-1, keepdims=True) + EPS) * SCALE)).astype(BF)
        k = (ka * lax.rsqrt(jnp.sum(ka * ka, axis=-1, keepdims=True) + EPS)).astype(BF)
        qo[0, :, lanes[h]] = q
        ko[0, :, lanes[h]] = k
        vo[0, :, lanes[h]] = va.astype(BF)
        mats.append(dot(k, k, NT) * (strict * rates[:, h : h + 1]))
    invs = unit_lower_inverses(mats)
    for h in range(HT):
        inv, rate = invs[h], head_rates[h]
        kf = ko[0, :, lanes[h]].astype(F32)
        u0 = dot(inv, (vo[0, :, lanes[h]].astype(F32) * rate).astype(BF))
        w = dot(inv, (kf * (rate * carried)).astype(BF)).astype(BF)
        kl = (kf * tail).astype(BF)
        m_ref[0, h] = (eye * keep - dot(kl, w, TN)).astype(BF)
        b_ref[0, h] = dot(kl, u0.astype(BF), TN)
        t_ref[0, h] = inv
        u0_ref[0, :, lanes[h]] = u0
        wo_ref[0, :, lanes[h]] = w


def out_kernel(gain_ref, q_ref, k_ref, u0_ref, w_ref, s_ref, doc_ref, n_ref, o_ref, u_ref):
    length = doc_ref.shape[1]
    doc = doc_ref[0]
    same, _ = masks(doc, length)
    carried = (doc < 0).astype(F32)
    gain = gain_ref[...]
    for h in range(HT):
        lanes = slice(h * HD, (h + 1) * HD)
        q, k, state = q_ref[0, :, lanes], k_ref[0, :, lanes], s_ref[0, h]
        u = (u0_ref[0, :, lanes] - dot(w_ref[0, :, lanes], state)).astype(BF)
        scores = (dot(q, k, NT) * same).astype(BF)
        o = dot(scores, u) + dot(q, state) * carried
        r = lax.rsqrt(jnp.mean(o * o, axis=-1, keepdims=True) + EPS)
        n_ref[0, :, lanes] = (o * r * gain).astype(BF)
        o_ref[0, :, lanes] = o
        u_ref[0, :, lanes] = u


def back_kernel(
    gain_ref, dn_ref, o_ref, q_ref, k_ref, t_ref, rate_ref, doc_ref, g_ref, y_ref, z_ref, l_ref, hg_ref
):
    length = doc_ref.shape[1]
    doc = doc_ref[0]
    same, _ = masks(doc, length)
    tail, _, carried = ends(doc, length)
    gain = gain_ref[...]

    @pl.when(pl.program_id(0) == 0)
    def _():
        hg_ref[...] = jnp.zeros_like(hg_ref)

    total = jnp.zeros((1, HD), F32)
    for h in range(HT):
        lanes = slice(h * HD, (h + 1) * HD)
        o, dy = o_ref[0, :, lanes], dn_ref[0, :, lanes].astype(F32)
        r = lax.rsqrt(jnp.mean(o * o, axis=-1, keepdims=True) + EPS)
        total = total + jnp.sum(o * r * dy, axis=0, keepdims=True)
        gy = gain * dy
        gf = r * gy - o * (r * r * r * jnp.mean(o * gy, axis=-1, keepdims=True))
        g = gf.astype(BF)
        q, k = q_ref[0, :, lanes], k_ref[0, :, lanes]
        inv = t_ref[0, h]
        scores = (dot(q, k, NT) * same).astype(BF)
        kf = k.astype(F32)
        y = dot(inv, dot(scores, g, TN).astype(BF), TN)
        z_ref[0, :, lanes] = dot(inv, (kf * tail).astype(BF), TN).astype(BF)
        rate = rate_ref[0, :, h : h + 1]
        l_ref[0, h] = dot((q.astype(F32) * carried).astype(BF), g, TN) - dot(
            (kf * (rate * carried)).astype(BF), y.astype(BF), TN
        )
        g_ref[0, :, lanes] = g
        y_ref[0, :, lanes] = y
    hg_ref[0:1] += total


def unit_back(act, dy, scale):
    r = lax.rsqrt(jnp.sum(act * act, axis=-1, keepdims=True) + EPS)
    inner = jnp.sum(act * dy, axis=-1, keepdims=True)
    return (r * scale) * dy - act * (r * r * r * scale * inner)


def grad_kernel(
    taps_ref, w_ref, beta_ref, p_ref, doc_ref, rate_ref, q_ref, k_ref, v_ref, s_ref, u_ref, g_ref, y_ref,
    z_ref, a_ref, gp_ref, gl_ref, in_ref, cg_ref,
):
    length = doc_ref.shape[1]
    doc = doc_ref[0]
    same, strict = masks(doc, length)
    tail, _, carried = ends(doc, length)

    @pl.when(pl.program_id(0) == 0)
    def _():
        cg_ref[...] = jnp.zeros_like(cg_ref)

    logits = []
    kept = tap_masks(doc, length)
    tail, carried = jnp.broadcast_to(tail, (length, HD)), jnp.broadcast_to(carried, (length, HD))
    for h in range(HT):
        lanes = slice(h * HD, (h + 1) * HD)
        q, k, v = q_ref[0, :, lanes], k_ref[0, :, lanes], v_ref[0, :, lanes]
        state, u, g, adj = s_ref[0, h], u_ref[0, :, lanes], g_ref[0, :, lanes], a_ref[0, h]
        rate = rate_ref[0, :, h : h + 1]
        yf = y_ref[0, :, lanes] + dot(z_ref[0, :, lanes], adj)
        y = yf.astype(BF)
        dv = rate * yf
        d1 = dot(y, u, NT) * strict
        gram = dot(k, k, NT)
        e = v.astype(F32) - dot(k, state) * carried
        drate = jnp.sum(yf * e, axis=-1, keepdims=True) - jnp.sum(d1 * gram, axis=-1, keepdims=True)
        dgram = (d1 * (-rate)).astype(BF)
        dscore = (dot(g, u, NT) * same).astype(BF)
        dq = dot(dscore, k) + dot(g, state, NT) * carried
        dk = dot(dscore, q, TN) + dot(dgram, k) + dot(dgram, k, TN)
        dk = dk - dot(y, state, NT) * (rate * carried) + dot(u, adj, NT) * tail
        logits.append(drate * rate * (1.0 - rate))
        for part, grad in enumerate((dq, dk, dv)):
            cols = slice(part * DT + h * HD, part * DT + (h + 1) * HD)
            ext = p_ref[0, :, cols].astype(F32)
            taps = taps_ref[part, :, lanes]
            mixed = conv_rows(ext, taps, kept, length)
            s = jax.nn.sigmoid(mixed)
            if part < 2:
                grad = unit_back(mixed * s, grad, SCALE if part == 0 else 1.0)
            gm = grad * (s * (1.0 + mixed * (1.0 - s)))
            total = jnp.zeros((length + RIM, HD), F32)
            for i in range(CONV):
                gv = gm * kept[i] if i < CONV - 1 else gm
                first = RIM - (CONV - 1) + i
                cg_ref[part, i : i + 1, lanes] += jnp.sum(
                    gv * ext[first : first + length], axis=0, keepdims=True
                )
                gv = gv * taps[i : i + 1]
                pads = [jnp.zeros((first, HD), F32), gv]
                if RIM - first > 0:
                    pads.append(jnp.zeros((RIM - first, HD), F32))
                total = total + jnp.concatenate(pads, axis=0)
            gp_ref[0, :, cols] = total.astype(BF)
    lane = lax.broadcasted_iota(jnp.int32, (length, HD), 1)
    wide = jnp.zeros((length, HD), F32)
    for h in range(HT):
        wide = jnp.where(lane == h, logits[h], wide)
    gl_ref[0, :RIM] = jnp.zeros((RIM, HD), BF)
    gl_ref[0, RIM:] = wide.astype(BF)

    for i in range(D // 256):
        span = slice(i * 256, (i + 1) * 256)
        total = dot(gp_ref[0], w_ref[span], NT) + dot(gl_ref[0], beta_ref[span], NT)
        in_ref[0, :, span] = total.astype(BF)


def to_rel(x, c, groups):
    half = D // groups // 2
    out = []
    for cc in range(2):
        for i in range(groups):
            at = i * 2 * half
            one, two = x[:, at : at + half], x[:, at + half : at + 2 * half]
            out.append(jnp.where(c == 0, one, two) if cc == 0 else jnp.where(c == 0, two, one))
    return jnp.concatenate(out, axis=1)


def from_rel(x, c, groups):
    half = D // groups // 2
    out = []
    for i in range(groups):
        one, two = x[:, i * half : (i + 1) * half], x[:, (groups + i) * half : (groups + i + 1) * half]
        out += [jnp.where(c == 0, one, two), jnp.where(c == 0, two, one)]
    return jnp.concatenate(out, axis=1)


def norm_kernel(groups, idx_ref, rim_ref, x_ref, gain_ref, n_ref):
    c = idx_ref[0]
    for src, span in ((rim_ref, slice(0, RIM)), (x_ref, slice(RIM, RIM + x_ref.shape[0]))):
        x = src[...].astype(F32)
        r = lax.rsqrt(jnp.mean(x * x, axis=-1, keepdims=True) + EPS)
        n_ref[span] = to_rel(x * r * gain_ref[...], c, groups).astype(BF)


def mid_kernel(groups, idx_ref, n0, n1, n2, n3, w_ref, x_ref, gain_ref, mid_ref, n_ref):
    c = idx_ref[0]
    heads = (n0, n1, n2, n3)

    for i in range(D // 256):
        span = slice(i * 256, (i + 1) * 256)
        total = x_ref[:, span].astype(F32)
        for j in range(TP):
            total = total + dot(heads[j][...], w_ref[j * DT : (j + 1) * DT, span])
        mid_ref[:, span] = total

    x = mid_ref[...]
    r = lax.rsqrt(jnp.mean(x * x, axis=-1, keepdims=True) + EPS)
    n_ref[...] = to_rel(x * r * gain_ref[...], c, groups).astype(BF)


def norm_back_rows(groups, c, parts, x, gain):
    dy = parts[0].astype(F32)
    for part in parts[1:]:
        dy = dy + part.astype(F32)
    dy = from_rel(dy, c, groups)
    r = lax.rsqrt(jnp.mean(x * x, axis=-1, keepdims=True) + EPS)
    gy = gain * dy
    dx = r * gy - x * (r * r * r * jnp.mean(x * gy, axis=-1, keepdims=True))
    return dx, jnp.sum(x * r * dy, axis=0, keepdims=True)


def mid_back_kernel(
    groups, idx_ref, p0, p1, p2, x_ref, cot_ref, gain_ref, w_ref, gm_ref, away_ref, mine_ref, d0, d1, d2, d3,
    gg_ref, br_ref,
):
    parts = [p[...] for p in (p0, p1, p2)]
    dx, gain_part = norm_back_rows(groups, idx_ref[0], parts, x_ref[...], gain_ref[...])
    grad = cot_ref[...].astype(F32) + dx
    gm_ref[...] = grad
    br_ref[...] = grad.astype(BF)
    gg_ref[...] = gain_part
    col = D // 8
    for j in range(TP):
        for cc, ref in ((1, away_ref), (0, mine_ref)):
            at = (jnp.bitwise_xor(idx_ref[1], j) * 2 + jnp.bitwise_xor(idx_ref[0], cc)) * col
            ref[:, j * col : (j + 1) * col] = br_ref[:, pl.ds(pl.multiple_of(at, 128), col)]
    for j, d_ref in enumerate((d0, d1, d2, d3)):
        for i in range(DT // 256):
            at = i * 256
            d_ref[:, at : at + 256] = dot(br_ref[...], w_ref[j * DT + at : j * DT + at + 256], NT).astype(BF)


def in_back_kernel(groups, idx_ref, p0, p1, p2, x_ref, base_ref, gain_ref, out_ref, gg_ref):
    parts = [p[...] for p in (p0, p1, p2)]
    dx, gain_part = norm_back_rows(groups, idx_ref[0], parts, x_ref[...].astype(F32), gain_ref[...])
    out_ref[...] = base_ref[...] + dx
    gg_ref[...] = gain_part


def ffn_kernel(*refs):
    idx_ref, xs, cs, gus, downs = refs[0], refs[1:6], refs[6:11], refs[11:13], refs[13:21]
    hid_ref, gg_ref, part_ref, away_ref, mine_ref, x_ref, d_ref, c_ref, w_ref = refs[22:31]
    x_sem, c_sem, w_sem, d_sem = refs[31:]
    length = hid_ref.shape[1]
    c, t = idx_ref[0], idx_ref[1]
    step = pl.program_id(0)
    depth = gus[0].shape[0]
    col = downs[0].shape[1]

    def x_copies():
        return row_copies(xs, x_ref, x_sem)

    def c_copies():
        return row_copies(cs, c_ref, c_sem)

    def w_copies():
        return [
            pltpu.make_async_copy(gus[i], w_ref.at[pl.ds(i * depth, depth)], w_sem.at[i]) for i in range(2)
        ]

    def d_copies():
        out = []
        for cc in range(2):
            for j in range(TP):
                at = (jnp.bitwise_xor(t, j) * 2 + jnp.bitwise_xor(c, cc)) * col
                n = cc * TP + j
                out.append(
                    pltpu.make_async_copy(
                        downs[n], d_ref.at[:, pl.ds(pl.multiple_of(at, 128), col)], d_sem.at[n]
                    )
                )
        return out

    @pl.when(step == 0)
    def _():
        first = w_copies() + x_copies()
        for copy in first + c_copies() + d_copies():
            copy.start()
        for copy in first:
            copy.wait()

    here = pl.ds(pl.multiple_of(step * length, 16), length)

    def hidden_tile(at, width):
        cols = pl.ds(at, width)
        ups = pl.ds(FT + at, width)
        x = x_ref[here]
        gate, up = dot(x, w_ref[:, cols]), dot(x, w_ref[:, ups])
        grad = dot(c_ref[here], d_ref[cols], NT)
        sg = jax.nn.sigmoid(gate)
        act = gate * sg
        hid_ref[0, :, cols] = (act * up).astype(BF)
        gg_ref[0, :, cols] = (grad * up * (sg * (1.0 + gate * (1.0 - sg)))).astype(BF)
        gg_ref[0, :, ups] = (grad * act).astype(BF)

    @pl.when(step == 0)
    def _():
        for copy in c_copies() + d_copies():
            copy.wait()

    tiles = FT // 256

    for i in range(tiles):
        hidden_tile(i * 256, 256)

    if FT % 256:
        hidden_tile(tiles * 256, FT % 256)

    for i in range(D // 256):
        span = slice(i * 256, (i + 1) * 256)
        part_ref[0, :, span] = dot(gg_ref[0], w_ref[span], NT).astype(BF)

    for j in range(TP):
        for cc, ref in ((1, away_ref), (0, mine_ref)):
            at = (jnp.bitwise_xor(t, j) * 2 + jnp.bitwise_xor(c, cc)) * col
            ref[0, :, j * col : (j + 1) * col] = c_ref[here, pl.ds(pl.multiple_of(at, 128), col)]


def whole_call(kernel, idx, ins, outs, us=5, scratch=()):
    return pl.pallas_call(
        kernel,
        in_specs=[pl.BlockSpec(memory_space=pltpu.SMEM)]
        + [pl.BlockSpec(memory_space=pltpu.VMEM)] * len(ins),
        out_specs=[pl.BlockSpec(memory_space=pltpu.VMEM)] * len(outs),
        out_shape=[jax.ShapeDtypeStruct(s, d) for s, d in outs],
        scratch_shapes=list(scratch),
        compiler_params=pltpu.CompilerParams(vmem_limit_bytes=VMEM),
        cost_estimate=cost(us),
    )(idx, *ins)


def assemble(idx, pieces, plan, shape, us=5):
    count = len(plan([0, 0, 0]))

    def kernel(idx_ref, *refs):
        srcs, out, sem = refs[: len(pieces)], refs[-2], refs[-1]
        copies = [
            pltpu.make_async_copy(srcs[p].at[src], out.at[dst], sem.at[n])
            for n, (p, src, dst) in enumerate(plan(idx_ref))
        ]
        for copy in copies:
            copy.start()
        for copy in copies:
            copy.wait()

    dtype = pieces[0].dtype
    return pl.pallas_call(
        kernel,
        in_specs=[pl.BlockSpec(memory_space=pltpu.SMEM)] + [pl.BlockSpec(memory_space=pl.ANY)] * len(pieces),
        out_specs=pl.BlockSpec(memory_space=pltpu.VMEM),
        out_shape=jax.ShapeDtypeStruct(shape, dtype),
        scratch_shapes=[pltpu.SemaphoreType.DMA((count,))],
        compiler_params=pltpu.CompilerParams(vmem_limit_bytes=VMEM),
        cost_estimate=cost(us),
    )(idx, *pieces)


def split_at(rows):
    unit = 16
    while unit < 128 and rows % (2 * unit) == 0:
        unit *= 2
    return (rows // unit + 1) // 2 * unit if unit >= 64 and rows // unit > 8 else rows // 32 * 16


def chunk_of(rows, cap):
    best = 16
    for q in range(16, cap + 1, 16):
        if rows % q == 0:
            best = q
    return best


def join_kernel(groups, idx_ref, g0, g1, g2, g3, out_ref):
    t = idx_ref[1]
    got = (g0, g1, g2, g3)
    shard, ff_shard = D // groups, FF // groups
    for i in range(groups):
        span = slice(FT + i * shard, FT + (i + 1) * shard)
        total = got[0][span].astype(F32)
        for x in got[1:]:
            total = total + x[span].astype(F32)
        out_ref[i, ff_shard:] = total.astype(BF)
    per = groups // TP
    for j in range(TP):
        chip = jnp.bitwise_xor(t, j)
        for i in range(per):
            out_ref[chip * per + i, :ff_shard] = got[j][i * ff_shard : (i + 1) * ff_shard]


def spread_first(x):
    return [x, plane_swap(x, 1), plane_swap(x, 2)]


def spread_pieces(first):
    x, a, b = first
    h = split_at(x.shape[0])
    mine = [x, a, b, plane_swap(a[:h], 2), plane_swap(b[h:], 1)]
    return mine + [core_swap(p) for p in mine]


def spread_out(idx, first, parts, heights=None):
    pieces = first if len(first) == 10 else spread_pieces(first)
    rows, cols = pieces[0].shape
    h = split_at(rows)
    width = cols // parts if parts else cols
    outs = []
    start = 0
    for height in heights or (rows,):
        edges = [start, start + height] + ([h] if start < h < start + height else [])
        q = 16
        for n in range(16, (64 if parts else 256) + 1, 16):
            if all((e - start) % n == 0 for e in edges) and start % n == 0 and h % n == 0:
                q = n
        outs.append(spread_part(idx, pieces, parts, width, start, height, h, q))
        start += height
    return outs


def gather_eight(x):
    n = lax.axis_size("replica")
    blocks = [list(range(i, i + 8)) for i in range(0, n, 8)]
    return lax.all_gather(x, "replica", axis=0, axis_index_groups=blocks if n > 8 else None)


def spread_abs(x, parts, start, height):
    _, rows, cols = x.shape
    width = cols // parts if parts else cols
    q = 16
    for n in range(16, (64 if parts else 128) + 1, 16):
        if height % n == 0 and start % n == 0:
            q = n
    base = start // q

    def kernel(x_ref, out):
        for r in range(8):
            chip, core = r // 2, r % 2
            if parts:
                for p in range(parts):
                    at = (p * TP + chip) * width
                    out[core, :, at : at + width] = x_ref[r, :, p * width : (p + 1) * width].astype(F32)
            else:
                out[:, r * width : (r + 1) * width] = x_ref[r].astype(F32)

    if parts:
        shape, out_spec = (2, height, TP * cols), pl.BlockSpec((2, q, TP * cols), lambda i: (0, i, 0))
    else:
        shape, out_spec = (height, 8 * cols), pl.BlockSpec((q, 8 * cols), lambda i: (i, 0))
    out = pl.pallas_call(
        kernel,
        grid=(height // q,),
        in_specs=[pl.BlockSpec((8, q, cols), lambda i: (0, i + base, 0))],
        out_specs=out_spec,
        out_shape=jax.ShapeDtypeStruct(shape, F32),
        compiler_params=pltpu.CompilerParams(vmem_limit_bytes=VMEM),
        cost_estimate=cost(height * cols * 16e-6),
    )(x)
    return out.reshape(-1, out.shape[-1])


def spread_part(idx, pieces, parts, width, start, height, h, q):
    cols = pieces[0].shape[1]
    rows = pieces[0].shape[0]
    cut, base = h // q, start // q

    def kernel(idx_ref, *refs):
        srcs, out = refs[:-1], refs[-1]
        c, t = idx_ref[0], idx_ref[1]
        i = pl.program_id(0) + base
        for cc in range(2):
            core = jnp.bitwise_xor(c, cc)

            def put(j, value):
                chip = jnp.bitwise_xor(t, j)
                if parts:
                    for p in range(parts):
                        at = pl.multiple_of((p * TP + chip) * width, 128)
                        out[core, :, pl.ds(at, width)] = value[:, p * width : (p + 1) * width].astype(F32)
                else:
                    at = pl.multiple_of((chip * 2 + core) * width, 128)
                    out[:, pl.ds(at, width)] = value.astype(F32)

            for j in range(3):
                put(j, srcs[5 * cc + j][...])

            @pl.when(i < cut)
            def _():
                put(3, srcs[5 * cc + 3][...])

            @pl.when(i >= cut)
            def _():
                put(3, srcs[5 * cc + 4][...])

    most = (rows - h) // q - 1
    full = pl.BlockSpec((q, cols), lambda i: (i + base, 0))
    low = pl.BlockSpec((q, cols), lambda i: (jnp.minimum(i + base, cut - 1), 0))
    high = pl.BlockSpec((q, cols), lambda i: (jnp.clip(i + base - cut, 0, most), 0))
    if parts:
        shape, out_spec = (2, height, TP * cols), pl.BlockSpec((2, q, TP * cols), lambda i: (0, i, 0))
    else:
        shape, out_spec = (height, 8 * cols), pl.BlockSpec((q, 8 * cols), lambda i: (i, 0))
    out = pl.pallas_call(
        kernel,
        grid=(height // q,),
        in_specs=[pl.BlockSpec(memory_space=pltpu.SMEM)] + [full, full, full, low, high] * 2,
        out_specs=out_spec,
        out_shape=jax.ShapeDtypeStruct(shape, F32),
        compiler_params=pltpu.CompilerParams(vmem_limit_bytes=VMEM),
        cost_estimate=cost(0.05),
    )(idx, *pieces)
    return out.reshape(-1, out.shape[-1])


def cost(us):
    return pl.CostEstimate(flops=int(us * 1.1e9), bytes_accessed=0, transcendentals=0)


def block(shape, fixed=False):
    zeros = (0,) * len(shape)
    if fixed:
        return pl.BlockSpec(tuple(shape), lambda i: zeros, pipeline_mode=pl.Buffered(1))
    return pl.BlockSpec((1,) + tuple(shape[1:]), lambda i: (i,) + zeros[1:])


def call(kernel, ins, fixed_ins, outs, fixed_outs=(), us=10, extra=(), scratch=(), held_outs=()):
    count = ins[-1].shape[0]
    out_specs = []
    for i, (shape, _) in enumerate(outs):
        zeros = (0,) * len(shape)
        if i in held_outs:
            spec = pl.BlockSpec(shape, lambda i, z=zeros: z, pipeline_mode=pl.Buffered(1))
        elif i in fixed_outs:
            spec = pl.BlockSpec(shape, lambda i, z=zeros: z)
        else:
            spec = block(shape)
        out_specs.append(spec)
    lead = [pl.BlockSpec(memory_space=pltpu.SMEM)] + [pl.BlockSpec(memory_space=pl.ANY)] * (len(extra) - 1)
    return pl.pallas_call(
        kernel,
        grid=(count,),
        in_specs=(lead if extra else []) + [block(x.shape, i in fixed_ins) for i, x in enumerate(ins)],
        out_specs=out_specs,
        out_shape=[jax.ShapeDtypeStruct(s, d) for s, d in outs],
        scratch_shapes=list(scratch),
        compiler_params=pltpu.CompilerParams(vmem_limit_bytes=VMEM),
        cost_estimate=cost(us),
    )(*extra, *ins)


def mm(a, b, dims=((1,), (0,))):
    return lax.dot_general(a, b, (dims, ((), ())), preferred_element_type=F32)


def body(
    tokens,
    cotangent,
    doc_start,
    norm_gain,
    qkv_weight,
    conv_weight,
    beta_weight,
    head_gain,
    out_weight,
    ffn_gain,
    gate_up_weight,
    down_weight,
):
    groups = lax.axis_size("group")
    r = lax.axis_index("replica") % 8
    g = lax.axis_index("group")
    c, t = r % 2, r // 2
    idx = jnp.stack([c, t, g]).astype(jnp.int32)
    _, length, _ = tokens.shape
    seqs = TP
    ext_len = length + RIM
    shard = D // groups
    half = shard // 2
    ff_shard = FF // groups
    col = D // 8
    tokens = tokens.reshape(length, D)
    cot = cotangent.reshape(length, D)

    def z_pieces(x):
        return [x] + [z_turn(x, s) for s in range(1, groups)]

    def z_abs(x):
        pieces = z_pieces(x)
        return place([((g - s) % groups, piece) for s, piece in enumerate(pieces)], groups)

    def rel(x):
        x = x.reshape(x.shape[:-1] + (groups, 2, half))
        x = jnp.where(c == 0, x, jnp.flip(x, -2))
        return jnp.swapaxes(x, -3, -2).reshape(x.shape[:-3] + (D,))

    def unrel(x):
        x = jnp.swapaxes(x.reshape(x.shape[:-1] + (2, groups, half)), -3, -2)
        x = jnp.where(c == 0, x, jnp.flip(x, -2))
        return x.reshape(x.shape[:-3] + (D,))

    small = jnp.concatenate(
        [
            beta_weight.T,
            jnp.swapaxes(conv_weight.reshape(3, shard, CONV), 1, 2).reshape(3 * CONV, shard),
            ffn_gain.reshape(1, shard),
            norm_gain.reshape(1, shard),
            jnp.zeros((2, shard), BF),
        ],
        axis=0,
    )
    rim = z_shift(tokens[length - RIM :], 1)
    small = z_abs(small)
    gain_in = small[:, HEADS + 3 * CONV + 1].reshape(1, D).astype(F32)
    gain_mid = small[:, HEADS + 3 * CONV].reshape(1, D).astype(F32)
    beta_full = jnp.swapaxes(small[:, :HEADS], 0, 1).reshape(HEADS, D)
    beta_t = jnp.pad(rel(lax.dynamic_slice(beta_full, (t * HT, 0), (HT, D))).T, ((0, 0), (0, HD - HT)))
    conv_full = small[:, HEADS : HEADS + 3 * CONV].reshape(groups * 3, CONV, shard)
    conv_full = jnp.swapaxes(conv_full, 0, 1).reshape(CONV, 3, TP, DT)
    taps = jnp.swapaxes(pick(conv_full, t, 2), 0, 1).astype(F32)
    gain_head = head_gain.astype(F32).reshape(1, HD)
    doc_rel = doc_start.reshape(1, length) - g * length
    docs = jnp.concatenate(
        [doc_rel] + [plane_swap(doc_rel, j) for j in (1, 2, 3)], axis=0
    ).reshape(seqs, length, 1)
    cot_x, cot_y = plane_swap(cot, 1), plane_swap(cot, 2)
    qkv_weight, small, rim = lax.optimization_barrier((qkv_weight, small, rim))

    (normed_ext,) = whole_call(
        functools.partial(norm_kernel, groups), idx, [rim, tokens, gain_in], [((ext_len, D), BF)]
    )
    normed_pieces = plane_copies(normed_ext)

    piece = jnp.concatenate(
        [lax.dynamic_slice(qkv_weight, (c * half, j * D + t * DT), (half, DT)) for j in range(3)], axis=1
    )
    qkv_pieces = z_pieces(piece)
    qkv_late = qkv_pieces
    qkv_pieces = qkv_pieces + [core_swap(p) for p in qkv_pieces]

    h = split_at(length)
    cot_pieces = [cot, cot_x, cot_y, plane_swap(cot_x[:h], 2), plane_swap(cot_y[h:], 1)]

    piece = jnp.concatenate(
        [
            lax.dynamic_slice(out_weight, (0, r * col), (shard, col)),
            lax.dynamic_slice(down_weight, (0, r * col), (ff_shard, col)),
        ],
        axis=0,
    )
    both = lax.all_gather(after(piece, *qkv_late), "group", axis=0)

    normed_pieces[0] = after(normed_pieces[0], *cot_pieces[:3])

    wide = (seqs, length, DT)
    square = (seqs, HT, HD, HD)
    (
        queries, key_rows, value_rows, inverse, u0, w, move, free, projected, rates, normed_all, qkv,
    ) = call(
        functools.partial(front_kernel, groups),
        [beta_t, taps, docs],
        (0, 1),
        [
            (wide, BF),
            (wide, BF),
            (wide, BF),
            ((seqs, HT, length, length), BF),
            (wide, F32),
            (wide, BF),
            (square, BF),
            (square, F32),
            ((seqs, ext_len, 3 * DT), BF),
            ((seqs, length, HD), F32),
            ((seqs * ext_len, D), BF),
            ((D, 3 * DT), BF),
        ],
        us=40,
        extra=[idx, *normed_pieces, *qkv_pieces],
        scratch=[pltpu.SemaphoreType.DMA((5,)), pltpu.SemaphoreType.DMA((2 * groups,))],
        held_outs=(10, 11),
    )
    piece = jnp.concatenate(
        [
            lax.dynamic_slice(gate_up_weight, (c * half, j * FF + t * FT), (half, FT))
            for j in range(2)
        ],
        axis=1,
    )
    gate_up = lax.all_gather(after(piece, free), "group", axis=0, tiled=True)

    state = jnp.zeros(square, BF)
    for hop in range(groups - 1):
        leaving = jnp.einsum("shij,shjk->shik", move, state, preferred_element_type=F32) + free
        if hop == groups - 2:
            leaving = after(leaving, *downs, *outs)
        state = z_shift(leaving.astype(BF), 1)
        if hop == 0:
            both = after(both, free)
            part = both[:, shard:].reshape(TP, FT, col)
            downs = plane_trade([pick(part, t ^ j) for j in range(TP)])
            outs = both[:, :shard].reshape(D, col)
            outs = plane_copies(outs)
    outs = outs + [core_swap(p) for p in outs]
    downs = downs + [core_swap(p) for p in downs]
    normed, head_out, update = call(
        out_kernel,
        [gain_head, queries, key_rows, u0, w, state, docs],
        (0,),
        [(wide, BF), (wide, F32), (wide, BF)],
        us=6,
    )

    def plan(ref):
        moves = []
        for cc in range(2):
            for j in range(TP):
                at = ((ref[1] ^ j) * 2 + (ref[0] ^ cc)) * col
                for b in range(TP):
                    n, first = (j, b) if j < 3 else ((3, b) if b < 2 else (4, b - 2))
                    moves.append(
                        (
                            5 * cc + n,
                            pl.ds(first * DT, DT),
                            (
                                pl.ds(pl.multiple_of((ref[1] ^ b) * DT, DT), DT),
                                pl.ds(pl.multiple_of(at, 128), col),
                            ),
                        )
                    )
        return moves

    out_w = assemble(idx, outs, plan, (D, D))

    heads = plane_trade([normed[j] for j in range(TP)])
    middle, normed_mid = whole_call(
        functools.partial(mid_kernel, groups),
        idx,
        heads + [out_w, tokens, gain_mid],
        [((length, D), F32), ((length, D), BF)],
        us=10,
    )
    mid_pieces = plane_copies(normed_mid)
    gate_ups = [gate_up, core_swap(after(gate_up, mid_pieces[1], mid_pieces[2]))]

    hidden, grad_gate_up, mid_part, cot_away, cot_mine, mid_all, down = call(
        ffn_kernel,
        [docs],
        (),
        [
            ((seqs, length, FT), BF),
            ((seqs, length, 2 * FT), BF),
            ((seqs, length, D), BF),
            ((seqs, length, D // 2), BF),
            ((seqs, length, D // 2), BF),
            ((seqs * length, D), BF),
            ((FT, D), BF),
        ],
        us=45,
        extra=[idx, *mid_pieces, *cot_pieces, *gate_ups, *downs],
        scratch=[pltpu.VMEM((seqs * length, D), BF), pltpu.VMEM((D, 2 * FT), BF)]
        + [pltpu.SemaphoreType.DMA((n,)) for n in (5, 5, 2, 8)],
        held_outs=(5, 6),
    )
    hidden = hidden.reshape(-1, FT)
    grad_gate_up = grad_gate_up.reshape(-1, 2 * FT)
    def two_halves(left, right):
        away = mm(left[:, groups * half :], right, TN).astype(BF)
        mine = mm(left[:, : groups * half], right, TN)
        return (mine + core_swap(away).astype(F32)).astype(BF).reshape(groups, half, -1)

    def two_columns(left, away, mine):
        away = mm(left, away, TN).astype(BF)
        mine = mm(left, mine, TN)
        return (mine + core_swap(away).astype(F32)).astype(BF)

    def z_sum(x, *others):
        total = pick(x, g).astype(F32)
        for s in range(1, groups):
            total = total + after(z_turn(pick(x, (g + s) % groups), s), *others).astype(F32)
        return total

    parts = plane_parts([mid_part[j] for j in range(TP)])
    gate_sums = [two_halves(mid_all, grad_gate_up[:, i * FT : (i + 1) * FT]) for i in range(2)]
    down_sum = two_columns(hidden, cot_away.reshape(-1, D // 2), cot_mine.reshape(-1, D // 2))
    first_sum = far_sum(lax.psum_scatter(gate_sums[0], "group", scatter_dimension=0)).astype(BF)
    parts, second_sum, down_sum = lax.optimization_barrier((parts, gate_sums[1], down_sum))
    second_sum = far_sum(lax.psum_scatter(second_sum, "group", scatter_dimension=0)).astype(BF)
    grad_middle, branch_away, branch_mine, *dheads, ffn_gain_part = whole_call(
        functools.partial(mid_back_kernel, groups),
        idx,
        parts + [middle.reshape(length, D), cot, gain_mid, out_w],
        [((length, D), F32)]
        + [((length, D // 2), BF)] * 2
        + [((length, DT), BF)] * TP
        + [((1, D), F32)],
        us=13,
        scratch=[pltpu.VMEM((length, D), BF)],
    )
    dnormed = jnp.stack(plane_trade(dheads))

    normed_abs = jnp.swapaxes(
        place([(t ^ j, heads[j]) for j in range(TP)], TP), 0, 1
    ).reshape(length, D)
    out_sum = two_columns(normed_abs, branch_away, branch_mine)
    both = [
        jnp.concatenate([x[:, j * col : (j + 1) * col] for x in (down_sum, out_sum)], axis=0)
        for j in range(TP)
    ]
    dnormed = after(dnormed, first_sum, *both)
    both = plane_trade(both)

    grad_out, y0, z, local, head_part = call(
        back_kernel,
        [gain_head, dnormed, head_out, queries, key_rows, inverse, rates, docs],
        (0,),
        [(wide, BF), (wide, F32), (wide, BF), (square, F32), ((8, HD), F32)],
        (4,),
        us=12,
    )

    out_part = mm(hidden, down).astype(BF).reshape(TP, length, D)

    later = jnp.zeros(square, BF)
    for hop in range(groups - 1):
        leaving = jnp.einsum("shji,shjk->shik", move, later, preferred_element_type=F32) + local
        if hop == 1:
            leaving = after(leaving, out_part)
        later = z_shift(leaving.astype(BF), -1)

    (both_sum,) = whole_call(
        functools.partial(join_kernel, groups), idx, both, [((groups, shard + ff_shard, col), BF)]
    )
    later = after(later, both_sum, second_sum)
    gate_sum = jnp.concatenate([first_sum, second_sum], axis=1)
    both_sum = lax.psum_scatter(both_sum, "group", scatter_dimension=0)
    gate_pieces = spread_first(gate_sum)
    grad_proj, grad_logit, in_part, conv_part = call(
        grad_kernel,
        [
            taps, qkv, beta_t, projected, docs, rates, queries, key_rows, value_rows, state, update, grad_out,
            y0, z, later,
        ],
        (0, 1, 2),
        [
            ((seqs, ext_len, 3 * DT), BF),
            ((seqs, ext_len, HD), BF),
            ((seqs, ext_len, D), BF),
            ((3, CONV, DT), F32),
        ],
        (3,),
        us=44,
    )
    qkv_sum = two_halves(normed_all, grad_proj.reshape(-1, 3 * DT))
    gate_pieces = spread_pieces([after(p, qkv_sum) for p in gate_pieces])
    rim = z_shift(in_part[:, :RIM], -1)
    in_part = after(in_part[:, RIM:], qkv_sum)
    qkv_sum = z_sum(qkv_sum)
    ends_in = (in_part[:, length - RIM :].astype(F32) + rim.astype(F32)).astype(BF)
    in_part = jnp.concatenate([in_part[:, : length - RIM], ends_in], axis=1)
    parts = plane_parts([in_part[j] for j in range(TP)])
    parts[0] = after(parts[0], qkv_sum)
    input_grad, norm_gain_part = whole_call(
        functools.partial(in_back_kernel, groups),
        idx,
        parts + [tokens, grad_middle, gain_in],
        [((length, D), F32), ((1, D), F32)],
        us=0.05,
    )
    output = (middle + plane_sum([out_part[j] for j in range(TP)])).astype(BF)

    beta_part = mm(grad_logit.reshape(-1, HD), normed_all, TN)[:HT]
    beta_all = lax.dynamic_update_slice(jnp.zeros((HEADS, D), F32), unrel(beta_part), (t * HT, 0))
    conv_all = lax.dynamic_update_slice(
        jnp.zeros((CONV, 3, TP, DT), F32), jnp.swapaxes(conv_part, 0, 1)[:, :, None], (0, 0, t, 0)
    )
    conv_all = jnp.swapaxes(conv_all.reshape(CONV, groups * 3, shard), 0, 1)
    pack = jnp.concatenate(
        [
            jnp.swapaxes(beta_all.reshape(HEADS, groups, shard), 0, 1),
            conv_all.reshape(groups, 3 * CONV, shard),
            norm_gain_part.reshape(groups, 1, shard),
            ffn_gain_part.reshape(groups, 1, shard),
            jnp.broadcast_to(jnp.pad(head_part[:1], ((0, 0), (0, shard - HD))), (groups, 1, shard)),
            jnp.zeros((groups, 1, shard), F32),
        ],
        axis=1,
    )
    pack = pack + core_swap(pack)
    pack = pack + plane_swap(pack, 1)
    pack = pack + plane_swap(pack, 2)

    (gate_up_grad,) = spread_out(idx, gate_pieces, 2)

    total = far_sum(z_sum(after(pack, qkv_sum)))
    both_pieces = [after(p, qkv_sum) for p in spread_first(far_sum(both_sum).astype(BF))]
    qkv_pieces = [after(p, gate_up_grad, output) for p in spread_first(far_sum(qkv_sum).astype(BF))]
    qkv_pieces = spread_pieces(qkv_pieces)
    down_grad, out_grad = spread_out(idx, both_pieces, 0, (ff_shard, shard))
    qkv_pieces[0] = after(qkv_pieces[0], total, out_grad, down_grad)
    (qkv_grad,) = spread_out(idx, qkv_pieces, 3)
    beta_grad = total[:HEADS].T
    conv_grad = jnp.swapaxes(total[HEADS : HEADS + 3 * CONV].reshape(3, CONV, shard), 1, 2)
    at = HEADS + 3 * CONV
    return (
        output.reshape(1, length, D),
        input_grad.reshape(1, length, D),
        total[at],
        qkv_grad,
        conv_grad.reshape(-1, CONV),
        beta_grad,
        total[at + 2, :HD],
        out_grad,
        total[at + 1],
        gate_up_grad,
        down_grad,
    )


def solution(mesh):
    rows = P("replica", "group", None)
    shard = P("group", None)
    return jax.shard_map(
        body,
        mesh=mesh,
        in_specs=(
            rows, rows, P("replica", "group"), P("group"), shard, shard, shard, P(), shard, P("group"), shard, shard,
        ),
        out_specs=(
            rows, rows, P("group"), shard, shard, shard, P(), shard, P("group"), shard, shard,
        ),
        check_vma=False,
    )
```

```python
import functools

import jax
import jax.numpy as jnp
from jax import lax
from jax.experimental import pallas as pl
from jax.experimental.pallas import tpu as pltpu
from jax.sharding import PartitionSpec as P

D = 2048
HEADS = 16
HD = 128
FF = 5632
CONV = 4
EPS = 1e-06
RIM = 16
TP = 4
HT = HEADS // TP
DT = D // TP
FT = FF // TP
SCALE = HD**-0.5
VMEM = 56 * 1024 * 1024

BF = jnp.bfloat16
F32 = jnp.float32


def swap(x, bits):
    n = lax.axis_size("replica")
    return lax.ppermute(x, "replica", [(i, i ^ bits) for i in range(n)])


def plane_swap(x, j):
    return swap(x, 2 * j)


def core_swap(x):
    return swap(x, 1)


def far_sum(x):
    x = x.astype(F32)
    bits = 8
    while bits < lax.axis_size("replica"):
        x = x + swap(x.astype(BF), bits).astype(F32)
        bits *= 2
    return x


def z_shift(x, by):
    n = lax.axis_size("group")
    return lax.ppermute(x, "group", [(i, i + by) for i in range(n) if 0 <= i + by < n])


def z_turn(x, by):
    n = lax.axis_size("group")
    return lax.ppermute(x, "group", [(i, (i + by) % n) for i in range(n)])


def plane_copies(x):
    a, b = plane_swap(x, 1), plane_swap(x, 2)
    h = split_at(x.shape[0])
    return [x, a, b, plane_swap(a[:h], 2), plane_swap(b[h:], 1)]


def plane_parts(parts):
    own, x, y, d = parts
    h = split_at(own.shape[0])
    via_x, via_y = plane_swap(d[:h], 1), plane_swap(d[h:], 2)
    y = jnp.concatenate([(y[:h].astype(F32) + via_x.astype(F32)).astype(BF), y[h:]], axis=0)
    x = jnp.concatenate([x[:h], (x[h:].astype(F32) + via_y.astype(F32)).astype(BF)], axis=0)
    return [own, plane_swap(x, 1), plane_swap(y, 2)]


def plane_sum(parts):
    own, x, y = plane_parts([p.astype(BF) for p in parts])
    return parts[0].astype(F32) + x.astype(F32) + y.astype(F32)


def after(x, *others):
    return lax.optimization_barrier((x, *others))[0]


def plane_trade(parts):
    return [parts[0]] + [plane_swap(parts[j], j) for j in (1, 2, 3)]


def place(pieces, count, axis=0):
    shape = list(pieces[0][1].shape)
    shape.insert(axis, count)
    buf = jnp.zeros(shape, pieces[0][1].dtype)
    for index, piece in pieces:
        buf = lax.dynamic_update_index_in_dim(buf, piece, index, axis)
    return buf


def pick(x, index, axis=0):
    return lax.dynamic_index_in_dim(x, index, axis, keepdims=False)


def dot(a, b, dims=((1,), (0,))):
    return lax.dot_general(a, b, (dims, ((), ())), preferred_element_type=F32)


NT = ((1,), (1,))
TN = ((0,), (0,))


def iotas(rows, cols):
    return (
        lax.broadcasted_iota(jnp.int32, (rows, cols), 0),
        lax.broadcasted_iota(jnp.int32, (rows, cols), 1),
    )


def unit_lower_inverses(mats):
    n = mats[0].shape[0]
    base, tile = 16, 128
    ri, ci = iotas(n, n)
    lane = lax.broadcasted_iota(jnp.int32, (base, tile), 1) % base
    rows = lax.broadcasted_iota(jnp.int32, (base, tile), 0)
    picks = [lane == j for j in range(base)]
    rt, ct = iotas(tile, tile)
    same = (rt // base) == (ct // base)
    ones = same.astype(BF)
    zero = jnp.zeros((), BF)
    lows = [a.astype(BF) for a in mats]
    spans = [slice(at, at + tile) for at in range(0, n, tile)]
    blocks = [(m, span) for m in range(len(mats)) for span in spans]
    wides = []
    for m, span in blocks:
        part = jnp.where(same, mats[m][span, span], 0.0)
        compact = jnp.sum(part.reshape(tile // base, base, tile), axis=0).astype(BF)
        spread = jnp.concatenate([jnp.where(p, compact, zero) for p in picks], axis=0)
        wides.append(dot(spread, ones))
    xs = [(lane == rows).astype(F32)] * len(blocks)
    for j in range(base - 1):
        xs = [x - w[j * base : (j + 1) * base] * x[j : j + 1] for x, w in zip(xs, wides)]
    fulls = [jnp.where(same, jnp.concatenate([x] * (tile // base), axis=0), 0.0) for x in xs]
    size = base
    while size < tile:
        part = (
            ((rt // (2 * size)) == (ct // (2 * size)))
            & ((rt // size) % 2 == 1)
            & ((ct // size) % 2 == 0)
        )
        halves = [full.astype(BF) for full in fulls]
        inner = [
            dot(jnp.where(part, lows[m][span, span], zero), h).astype(BF)
            for (m, span), h in zip(blocks, halves)
        ]
        fulls = [full - dot(h, i) for full, h, i in zip(fulls, halves, inner)]
        size *= 2
    fulls = [full.astype(BF) for full in fulls]
    if n == tile:
        return fulls
    inner = [dot(low[tile:, :tile], fulls[2 * m]).astype(BF) for m, low in enumerate(lows)]
    corners = [-dot(fulls[2 * m + 1], i) for m, i in enumerate(inner)]
    blank = jnp.zeros((tile, tile), BF)
    return [
        jnp.concatenate(
            [
                jnp.concatenate([fulls[2 * m], blank], axis=1),
                jnp.concatenate([corner.astype(BF), fulls[2 * m + 1]], axis=1),
            ],
            axis=0,
        )
        for m, corner in enumerate(corners)
    ]


def tap_masks(doc, length):
    pos = lax.broadcasted_iota(jnp.int32, (length, 1), 0)
    return [
        jnp.broadcast_to((pos - (CONV - 1) + i >= doc).astype(F32), (length, HD)) for i in range(CONV - 1)
    ]


def conv_rows(ext, taps, kept, length):
    total = ext[RIM : RIM + length] * taps[CONV - 1 : CONV]
    for i in range(CONV - 1):
        first = RIM - (CONV - 1) + i
        total = total + ext[first : first + length] * taps[i : i + 1] * kept[i]
    return total


def masks(doc, length):
    ri, ci = iotas(length, length)
    same = (doc <= ci) & (ri >= ci)
    return same.astype(F32), (same & (ri > ci)).astype(F32)


def ends(doc, length):
    last = doc[length - 1 : length]
    pos = lax.broadcasted_iota(jnp.int32, (length, 1), 0)
    return (pos >= last).astype(F32), (last < 0).astype(F32), (doc < 0).astype(F32)


def row_starts(n):
    return (0, n, 2 * n, 3 * n, 3 * n + split_at(n))


def row_copies(srcs, dst, sem):
    starts = row_starts(srcs[0].shape[0])
    return [
        pltpu.make_async_copy(src, dst.at[pl.ds(starts[i], src.shape[0])], sem.at[i])
        for i, src in enumerate(srcs)
    ]


def front_kernel(groups, *refs):
    idx_ref, xs, ws = refs[0], refs[1:6], refs[6 : 6 + 2 * groups]
    (
        beta_ref, taps_ref, doc_ref, qo, ko, vo, t_ref, u0_ref, wo_ref, m_ref, b_ref, p_ref, rate_ref,
        all_ref, w_ref, x_sem, w_sem,
    ) = refs[6 + 2 * groups :]
    length = doc_ref.shape[1]
    half = ws[0].shape[0]
    step = pl.program_id(0)

    @pl.when(step == 0)
    def _():
        copies = row_copies(xs, all_ref, x_sem)
        for cc in range(2):
            for s in range(groups):
                at = (cc * groups + (idx_ref[2] + groups - s) % groups) * half
                copies.append(
                    pltpu.make_async_copy(
                        ws[cc * groups + s],
                        w_ref.at[pl.ds(pl.multiple_of(at, 128), half)],
                        w_sem.at[cc * groups + s],
                    )
                )
        for copy in copies:
            copy.start()
        for copy in copies:
            copy.wait()

    rows = length + RIM
    here = pl.ds(pl.multiple_of(step * rows, 16), rows)
    doc = doc_ref[0]
    same, strict = masks(doc, length)
    tail, keep, carried = ends(doc, length)
    eye = (iotas(HD, HD)[0] == iotas(HD, HD)[1]).astype(F32)

    for i in range(3 * DT // 256):
        cols = slice(i * 256, (i + 1) * 256)
        p_ref[0, :, cols] = dot(all_ref[here], w_ref[:, cols]).astype(BF)

    own = pl.ds(pl.multiple_of(step * rows + RIM, 16), length)
    rates = jax.nn.sigmoid(dot(all_ref[own], beta_ref[...]))
    rate_ref[0] = rates
    kept = tap_masks(doc, length)
    wide = (length, HD)
    tail, carried = jnp.broadcast_to(tail, wide), jnp.broadcast_to(carried, wide)
    head_rates = [jnp.broadcast_to(rates[:, h : h + 1], wide) for h in range(HT)]
    lanes = [slice(h * HD, (h + 1) * HD) for h in range(HT)]
    mats = []
    for h in range(HT):
        acts = []
        for part in range(3):
            cols = slice(part * DT + h * HD, part * DT + (h + 1) * HD)
            mixed = conv_rows(p_ref[0, :, cols].astype(F32), taps_ref[part, :, lanes[h]], kept, length)
            acts.append(mixed * jax.nn.sigmoid(mixed))
        qa, ka, va = acts
        q = (qa * (lax.rsqrt(jnp.sum(qa * qa, axis=-1, keepdims=True) + EPS) * SCALE)).astype(BF)
        k = (ka * lax.rsqrt(jnp.sum(ka * ka, axis=-1, keepdims=True) + EPS)).astype(BF)
        qo[0, :, lanes[h]] = q
        ko[0, :, lanes[h]] = k
        vo[0, :, lanes[h]] = va.astype(BF)
        mats.append(dot(k, k, NT) * (strict * rates[:, h : h + 1]))
    invs = unit_lower_inverses(mats)
    for h in range(HT):
        inv, rate = invs[h], head_rates[h]
        kf = ko[0, :, lanes[h]].astype(F32)
        u0 = dot(inv, (vo[0, :, lanes[h]].astype(F32) * rate).astype(BF))
        w = dot(inv, (kf * (rate * carried)).astype(BF)).astype(BF)
        kl = (kf * tail).astype(BF)
        m_ref[0, h] = (eye * keep - dot(kl, w, TN)).astype(BF)
        b_ref[0, h] = dot(kl, u0.astype(BF), TN)
        t_ref[0, h] = inv
        u0_ref[0, :, lanes[h]] = u0
        wo_ref[0, :, lanes[h]] = w


def out_kernel(gain_ref, q_ref, k_ref, u0_ref, w_ref, s_ref, doc_ref, n_ref, o_ref, u_ref):
    length = doc_ref.shape[1]
    doc = doc_ref[0]
    same, _ = masks(doc, length)
    carried = (doc < 0).astype(F32)
    gain = gain_ref[...]
    for h in range(HT):
        lanes = slice(h * HD, (h + 1) * HD)
        q, k, state = q_ref[0, :, lanes], k_ref[0, :, lanes], s_ref[0, h]
        u = (u0_ref[0, :, lanes] - dot(w_ref[0, :, lanes], state)).astype(BF)
        scores = (dot(q, k, NT) * same).astype(BF)
        o = dot(scores, u) + dot(q, state) * carried
        r = lax.rsqrt(jnp.mean(o * o, axis=-1, keepdims=True) + EPS)
        n_ref[0, :, lanes] = (o * r * gain).astype(BF)
        o_ref[0, :, lanes] = o
        u_ref[0, :, lanes] = u


def back_kernel(
    gain_ref, dn_ref, o_ref, q_ref, k_ref, t_ref, rate_ref, doc_ref, g_ref, y_ref, z_ref, l_ref, hg_ref
):
    length = doc_ref.shape[1]
    doc = doc_ref[0]
    same, _ = masks(doc, length)
    tail, _, carried = ends(doc, length)
    gain = gain_ref[...]

    @pl.when(pl.program_id(0) == 0)
    def _():
        hg_ref[...] = jnp.zeros_like(hg_ref)

    total = jnp.zeros((1, HD), F32)
    for h in range(HT):
        lanes = slice(h * HD, (h + 1) * HD)
        o, dy = o_ref[0, :, lanes], dn_ref[0, :, lanes].astype(F32)
        r = lax.rsqrt(jnp.mean(o * o, axis=-1, keepdims=True) + EPS)
        total = total + jnp.sum(o * r * dy, axis=0, keepdims=True)
        gy = gain * dy
        gf = r * gy - o * (r * r * r * jnp.mean(o * gy, axis=-1, keepdims=True))
        g = gf.astype(BF)
        q, k = q_ref[0, :, lanes], k_ref[0, :, lanes]
        inv = t_ref[0, h]
        scores = (dot(q, k, NT) * same).astype(BF)
        kf = k.astype(F32)
        y = dot(inv, dot(scores, g, TN).astype(BF), TN)
        z_ref[0, :, lanes] = dot(inv, (kf * tail).astype(BF), TN).astype(BF)
        rate = rate_ref[0, :, h : h + 1]
        l_ref[0, h] = dot((q.astype(F32) * carried).astype(BF), g, TN) - dot(
            (kf * (rate * carried)).astype(BF), y.astype(BF), TN
        )
        g_ref[0, :, lanes] = g
        y_ref[0, :, lanes] = y
    hg_ref[0:1] += total


def unit_back(act, dy, scale):
    r = lax.rsqrt(jnp.sum(act * act, axis=-1, keepdims=True) + EPS)
    inner = jnp.sum(act * dy, axis=-1, keepdims=True)
    return (r * scale) * dy - act * (r * r * r * scale * inner)


def grad_kernel(
    taps_ref, w_ref, beta_ref, p_ref, doc_ref, rate_ref, q_ref, k_ref, v_ref, s_ref, u_ref, g_ref, y_ref,
    z_ref, a_ref, gp_ref, gl_ref, in_ref, cg_ref,
):
    length = doc_ref.shape[1]
    doc = doc_ref[0]
    same, strict = masks(doc, length)
    tail, _, carried = ends(doc, length)

    @pl.when(pl.program_id(0) == 0)
    def _():
        cg_ref[...] = jnp.zeros_like(cg_ref)

    logits = []
    kept = tap_masks(doc, length)
    tail, carried = jnp.broadcast_to(tail, (length, HD)), jnp.broadcast_to(carried, (length, HD))
    for h in range(HT):
        lanes = slice(h * HD, (h + 1) * HD)
        q, k, v = q_ref[0, :, lanes], k_ref[0, :, lanes], v_ref[0, :, lanes]
        state, u, g, adj = s_ref[0, h], u_ref[0, :, lanes], g_ref[0, :, lanes], a_ref[0, h]
        rate = rate_ref[0, :, h : h + 1]
        yf = y_ref[0, :, lanes] + dot(z_ref[0, :, lanes], adj)
        y = yf.astype(BF)
        dv = rate * yf
        d1 = dot(y, u, NT) * strict
        gram = dot(k, k, NT)
        e = v.astype(F32) - dot(k, state) * carried
        drate = jnp.sum(yf * e, axis=-1, keepdims=True) - jnp.sum(d1 * gram, axis=-1, keepdims=True)
        dgram = (d1 * (-rate)).astype(BF)
        dscore = (dot(g, u, NT) * same).astype(BF)
        dq = dot(dscore, k) + dot(g, state, NT) * carried
        dk = dot(dscore, q, TN) + dot(dgram, k) + dot(dgram, k, TN)
        dk = dk - dot(y, state, NT) * (rate * carried) + dot(u, adj, NT) * tail
        logits.append(drate * rate * (1.0 - rate))
        for part, grad in enumerate((dq, dk, dv)):
            cols = slice(part * DT + h * HD, part * DT + (h + 1) * HD)
            ext = p_ref[0, :, cols].astype(F32)
            taps = taps_ref[part, :, lanes]
            mixed = conv_rows(ext, taps, kept, length)
            s = jax.nn.sigmoid(mixed)
            if part < 2:
                grad = unit_back(mixed * s, grad, SCALE if part == 0 else 1.0)
            gm = grad * (s * (1.0 + mixed * (1.0 - s)))
            total = jnp.zeros((length + RIM, HD), F32)
            for i in range(CONV):
                gv = gm * kept[i] if i < CONV - 1 else gm
                first = RIM - (CONV - 1) + i
                cg_ref[part, i : i + 1, lanes] += jnp.sum(
                    gv * ext[first : first + length], axis=0, keepdims=True
                )
                gv = gv * taps[i : i + 1]
                pads = [jnp.zeros((first, HD), F32), gv]
                if RIM - first > 0:
                    pads.append(jnp.zeros((RIM - first, HD), F32))
                total = total + jnp.concatenate(pads, axis=0)
            gp_ref[0, :, cols] = total.astype(BF)
    lane = lax.broadcasted_iota(jnp.int32, (length, HD), 1)
    wide = jnp.zeros((length, HD), F32)
    for h in range(HT):
        wide = jnp.where(lane == h, logits[h], wide)
    gl_ref[0, :RIM] = jnp.zeros((RIM, HD), BF)
    gl_ref[0, RIM:] = wide.astype(BF)

    for i in range(D // 256):
        span = slice(i * 256, (i + 1) * 256)
        total = dot(gp_ref[0], w_ref[span], NT) + dot(gl_ref[0], beta_ref[span], NT)
        in_ref[0, :, span] = total.astype(BF)


def to_rel(x, c, groups):
    half = D // groups // 2
    out = []
    for cc in range(2):
        for i in range(groups):
            at = i * 2 * half
            one, two = x[:, at : at + half], x[:, at + half : at + 2 * half]
            out.append(jnp.where(c == 0, one, two) if cc == 0 else jnp.where(c == 0, two, one))
    return jnp.concatenate(out, axis=1)


def from_rel(x, c, groups):
    half = D // groups // 2
    out = []
    for i in range(groups):
        one, two = x[:, i * half : (i + 1) * half], x[:, (groups + i) * half : (groups + i + 1) * half]
        out += [jnp.where(c == 0, one, two), jnp.where(c == 0, two, one)]
    return jnp.concatenate(out, axis=1)


def norm_kernel(groups, idx_ref, rim_ref, x_ref, gain_ref, n_ref):
    c = idx_ref[0]
    for src, span in ((rim_ref, slice(0, RIM)), (x_ref, slice(RIM, RIM + x_ref.shape[0]))):
        x = src[...].astype(F32)
        r = lax.rsqrt(jnp.mean(x * x, axis=-1, keepdims=True) + EPS)
        n_ref[span] = to_rel(x * r * gain_ref[...], c, groups).astype(BF)


def mid_kernel(groups, idx_ref, n0, n1, n2, n3, w_ref, x_ref, gain_ref, mid_ref, n_ref):
    c = idx_ref[0]
    heads = (n0, n1, n2, n3)

    for i in range(D // 256):
        span = slice(i * 256, (i + 1) * 256)
        total = x_ref[:, span].astype(F32)
        for j in range(TP):
            total = total + dot(heads[j][...], w_ref[j * DT : (j + 1) * DT, span])
        mid_ref[:, span] = total

    x = mid_ref[...]
    r = lax.rsqrt(jnp.mean(x * x, axis=-1, keepdims=True) + EPS)
    n_ref[...] = to_rel(x * r * gain_ref[...], c, groups).astype(BF)


def norm_back_rows(groups, c, parts, x, gain):
    dy = parts[0].astype(F32)
    for part in parts[1:]:
        dy = dy + part.astype(F32)
    dy = from_rel(dy, c, groups)
    r = lax.rsqrt(jnp.mean(x * x, axis=-1, keepdims=True) + EPS)
    gy = gain * dy
    dx = r * gy - x * (r * r * r * jnp.mean(x * gy, axis=-1, keepdims=True))
    return dx, jnp.sum(x * r * dy, axis=0, keepdims=True)


def mid_back_kernel(
    groups, idx_ref, p0, p1, p2, x_ref, cot_ref, gain_ref, w_ref, gm_ref, away_ref, mine_ref, d0, d1, d2, d3,
    gg_ref, br_ref,
):
    parts = [p[...] for p in (p0, p1, p2)]
    dx, gain_part = norm_back_rows(groups, idx_ref[0], parts, x_ref[...], gain_ref[...])
    grad = cot_ref[...].astype(F32) + dx
    gm_ref[...] = grad
    br_ref[...] = grad.astype(BF)
    gg_ref[...] = gain_part
    col = D // 8
    for j in range(TP):
        for cc, ref in ((1, away_ref), (0, mine_ref)):
            at = (jnp.bitwise_xor(idx_ref[1], j) * 2 + jnp.bitwise_xor(idx_ref[0], cc)) * col
            ref[:, j * col : (j + 1) * col] = br_ref[:, pl.ds(pl.multiple_of(at, 128), col)]
    for j, d_ref in enumerate((d0, d1, d2, d3)):
        for i in range(DT // 256):
            at = i * 256
            d_ref[:, at : at + 256] = dot(br_ref[...], w_ref[j * DT + at : j * DT + at + 256], NT).astype(BF)


def in_back_kernel(groups, idx_ref, p0, p1, p2, x_ref, base_ref, gain_ref, out_ref, gg_ref):
    parts = [p[...] for p in (p0, p1, p2)]
    dx, gain_part = norm_back_rows(groups, idx_ref[0], parts, x_ref[...].astype(F32), gain_ref[...])
    out_ref[...] = base_ref[...] + dx
    gg_ref[...] = gain_part


def ffn_kernel(*refs):
    idx_ref, xs, cs, gus, downs = refs[0], refs[1:6], refs[6:11], refs[11:13], refs[13:21]
    hid_ref, gg_ref, part_ref, away_ref, mine_ref, x_ref, d_ref, c_ref, w_ref = refs[22:31]
    x_sem, c_sem, w_sem, d_sem = refs[31:]
    length = hid_ref.shape[1]
    c, t = idx_ref[0], idx_ref[1]
    step = pl.program_id(0)
    depth = gus[0].shape[0]
    col = downs[0].shape[1]

    def x_copies():
        return row_copies(xs, x_ref, x_sem)

    def c_copies():
        return row_copies(cs, c_ref, c_sem)

    def w_copies():
        return [
            pltpu.make_async_copy(gus[i], w_ref.at[pl.ds(i * depth, depth)], w_sem.at[i]) for i in range(2)
        ]

    def d_copies():
        out = []
        for cc in range(2):
            for j in range(TP):
                at = (jnp.bitwise_xor(t, j) * 2 + jnp.bitwise_xor(c, cc)) * col
                n = cc * TP + j
                out.append(
                    pltpu.make_async_copy(
                        downs[n], d_ref.at[:, pl.ds(pl.multiple_of(at, 128), col)], d_sem.at[n]
                    )
                )
        return out

    @pl.when(step == 0)
    def _():
        first = w_copies() + x_copies()
        for copy in first + c_copies() + d_copies():
            copy.start()
        for copy in first:
            copy.wait()

    here = pl.ds(pl.multiple_of(step * length, 16), length)

    def hidden_tile(at, width):
        cols = pl.ds(at, width)
        ups = pl.ds(FT + at, width)
        x = x_ref[here]
        gate, up = dot(x, w_ref[:, cols]), dot(x, w_ref[:, ups])
        grad = dot(c_ref[here], d_ref[cols], NT)
        sg = jax.nn.sigmoid(gate)
        act = gate * sg
        hid_ref[0, :, cols] = (act * up).astype(BF)
        gg_ref[0, :, cols] = (grad * up * (sg * (1.0 + gate * (1.0 - sg)))).astype(BF)
        gg_ref[0, :, ups] = (grad * act).astype(BF)

    @pl.when(step == 0)
    def _():
        for copy in c_copies() + d_copies():
            copy.wait()

    tiles = FT // 256

    for i in range(tiles):
        hidden_tile(i * 256, 256)

    if FT % 256:
        hidden_tile(tiles * 256, FT % 256)

    for i in range(D // 256):
        span = slice(i * 256, (i + 1) * 256)
        part_ref[0, :, span] = dot(gg_ref[0], w_ref[span], NT).astype(BF)

    for j in range(TP):
        for cc, ref in ((1, away_ref), (0, mine_ref)):
            at = (jnp.bitwise_xor(t, j) * 2 + jnp.bitwise_xor(c, cc)) * col
            ref[0, :, j * col : (j + 1) * col] = c_ref[here, pl.ds(pl.multiple_of(at, 128), col)]


def whole_call(kernel, idx, ins, outs, us=5, scratch=()):
    return pl.pallas_call(
        kernel,
        in_specs=[pl.BlockSpec(memory_space=pltpu.SMEM)]
        + [pl.BlockSpec(memory_space=pltpu.VMEM)] * len(ins),
        out_specs=[pl.BlockSpec(memory_space=pltpu.VMEM)] * len(outs),
        out_shape=[jax.ShapeDtypeStruct(s, d) for s, d in outs],
        scratch_shapes=list(scratch),
        compiler_params=pltpu.CompilerParams(vmem_limit_bytes=VMEM),
        cost_estimate=cost(us),
    )(idx, *ins)


def assemble(idx, pieces, plan, shape, us=5):
    count = len(plan([0, 0, 0]))

    def kernel(idx_ref, *refs):
        srcs, out, sem = refs[: len(pieces)], refs[-2], refs[-1]
        copies = [
            pltpu.make_async_copy(srcs[p].at[src], out.at[dst], sem.at[n])
            for n, (p, src, dst) in enumerate(plan(idx_ref))
        ]
        for copy in copies:
            copy.start()
        for copy in copies:
            copy.wait()

    dtype = pieces[0].dtype
    return pl.pallas_call(
        kernel,
        in_specs=[pl.BlockSpec(memory_space=pltpu.SMEM)] + [pl.BlockSpec(memory_space=pl.ANY)] * len(pieces),
        out_specs=pl.BlockSpec(memory_space=pltpu.VMEM),
        out_shape=jax.ShapeDtypeStruct(shape, dtype),
        scratch_shapes=[pltpu.SemaphoreType.DMA((count,))],
        compiler_params=pltpu.CompilerParams(vmem_limit_bytes=VMEM),
        cost_estimate=cost(us),
    )(idx, *pieces)


def split_at(rows):
    unit = 16
    while unit < 128 and rows % (2 * unit) == 0:
        unit *= 2
    return (rows // unit + 1) // 2 * unit if unit >= 64 and rows // unit > 8 else rows // 32 * 16


def chunk_of(rows, cap):
    best = 16
    for q in range(16, cap + 1, 16):
        if rows % q == 0:
            best = q
    return best


def join_kernel(groups, idx_ref, g0, g1, g2, g3, out_ref):
    t = idx_ref[1]
    got = (g0, g1, g2, g3)
    shard, ff_shard = D // groups, FF // groups
    for i in range(groups):
        span = slice(FT + i * shard, FT + (i + 1) * shard)
        total = got[0][span].astype(F32)
        for x in got[1:]:
            total = total + x[span].astype(F32)
        out_ref[i, ff_shard:] = total.astype(BF)
    per = groups // TP
    for j in range(TP):
        chip = jnp.bitwise_xor(t, j)
        for i in range(per):
            out_ref[chip * per + i, :ff_shard] = got[j][i * ff_shard : (i + 1) * ff_shard]


def spread_first(x):
    return [x, plane_swap(x, 1), plane_swap(x, 2)]


def spread_pieces(first):
    x, a, b = first
    h = split_at(x.shape[0])
    mine = [x, a, b, plane_swap(a[:h], 2), plane_swap(b[h:], 1)]
    return mine + [core_swap(p) for p in mine]


def spread_out(idx, first, parts, heights=None):
    pieces = first if len(first) == 10 else spread_pieces(first)
    rows, cols = pieces[0].shape
    h = split_at(rows)
    width = cols // parts if parts else cols
    outs = []
    start = 0
    for height in heights or (rows,):
        edges = [start, start + height] + ([h] if start < h < start + height else [])
        q = 16
        for n in range(16, (64 if parts else 256) + 1, 16):
            if all((e - start) % n == 0 for e in edges) and start % n == 0 and h % n == 0:
                q = n
        outs.append(spread_part(idx, pieces, parts, width, start, height, h, q))
        start += height
    return outs


def gather_eight(x):
    n = lax.axis_size("replica")
    blocks = [list(range(i, i + 8)) for i in range(0, n, 8)]
    return lax.all_gather(x, "replica", axis=0, axis_index_groups=blocks if n > 8 else None)


def spread_abs(x, parts, start, height):
    _, rows, cols = x.shape
    width = cols // parts if parts else cols
    q = 16
    for n in range(16, (64 if parts else 128) + 1, 16):
        if height % n == 0 and start % n == 0:
            q = n
    base = start // q

    def kernel(x_ref, out):
        for r in range(8):
            chip, core = r // 2, r % 2
            if parts:
                for p in range(parts):
                    at = (p * TP + chip) * width
                    out[core, :, at : at + width] = x_ref[r, :, p * width : (p + 1) * width].astype(F32)
            else:
                out[:, r * width : (r + 1) * width] = x_ref[r].astype(F32)

    if parts:
        shape, out_spec = (2, height, TP * cols), pl.BlockSpec((2, q, TP * cols), lambda i: (0, i, 0))
    else:
        shape, out_spec = (height, 8 * cols), pl.BlockSpec((q, 8 * cols), lambda i: (i, 0))
    out = pl.pallas_call(
        kernel,
        grid=(height // q,),
        in_specs=[pl.BlockSpec((8, q, cols), lambda i: (0, i + base, 0))],
        out_specs=out_spec,
        out_shape=jax.ShapeDtypeStruct(shape, F32),
        compiler_params=pltpu.CompilerParams(vmem_limit_bytes=VMEM),
        cost_estimate=cost(height * cols * 16e-6),
    )(x)
    return out.reshape(-1, out.shape[-1])


def spread_part(idx, pieces, parts, width, start, height, h, q):
    cols = pieces[0].shape[1]
    rows = pieces[0].shape[0]
    cut, base = h // q, start // q

    def kernel(idx_ref, *refs):
        srcs, out = refs[:-1], refs[-1]
        c, t = idx_ref[0], idx_ref[1]
        i = pl.program_id(0) + base
        for cc in range(2):
            core = jnp.bitwise_xor(c, cc)

            def put(j, value):
                chip = jnp.bitwise_xor(t, j)
                if parts:
                    for p in range(parts):
                        at = pl.multiple_of((p * TP + chip) * width, 128)
                        out[core, :, pl.ds(at, width)] = value[:, p * width : (p + 1) * width].astype(F32)
                else:
                    at = pl.multiple_of((chip * 2 + core) * width, 128)
                    out[:, pl.ds(at, width)] = value.astype(F32)

            for j in range(3):
                put(j, srcs[5 * cc + j][...])

            @pl.when(i < cut)
            def _():
                put(3, srcs[5 * cc + 3][...])

            @pl.when(i >= cut)
            def _():
                put(3, srcs[5 * cc + 4][...])

    most = (rows - h) // q - 1
    full = pl.BlockSpec((q, cols), lambda i: (i + base, 0))
    low = pl.BlockSpec((q, cols), lambda i: (jnp.minimum(i + base, cut - 1), 0))
    high = pl.BlockSpec((q, cols), lambda i: (jnp.clip(i + base - cut, 0, most), 0))
    if parts:
        shape, out_spec = (2, height, TP * cols), pl.BlockSpec((2, q, TP * cols), lambda i: (0, i, 0))
    else:
        shape, out_spec = (height, 8 * cols), pl.BlockSpec((q, 8 * cols), lambda i: (i, 0))
    out = pl.pallas_call(
        kernel,
        grid=(height // q,),
        in_specs=[pl.BlockSpec(memory_space=pltpu.SMEM)] + [full, full, full, low, high] * 2,
        out_specs=out_spec,
        out_shape=jax.ShapeDtypeStruct(shape, F32),
        compiler_params=pltpu.CompilerParams(vmem_limit_bytes=VMEM),
        cost_estimate=cost(0.05),
    )(idx, *pieces)
    return out.reshape(-1, out.shape[-1])


def cost(us):
    return pl.CostEstimate(flops=int(us * 1.1e9), bytes_accessed=0, transcendentals=0)


def block(shape, fixed=False):
    zeros = (0,) * len(shape)
    if fixed:
        return pl.BlockSpec(tuple(shape), lambda i: zeros, pipeline_mode=pl.Buffered(1))
    return pl.BlockSpec((1,) + tuple(shape[1:]), lambda i: (i,) + zeros[1:])


def call(kernel, ins, fixed_ins, outs, fixed_outs=(), us=10, extra=(), scratch=(), held_outs=()):
    count = ins[-1].shape[0]
    out_specs = []
    for i, (shape, _) in enumerate(outs):
        zeros = (0,) * len(shape)
        if i in held_outs:
            spec = pl.BlockSpec(shape, lambda i, z=zeros: z, pipeline_mode=pl.Buffered(1))
        elif i in fixed_outs:
            spec = pl.BlockSpec(shape, lambda i, z=zeros: z)
        else:
            spec = block(shape)
        out_specs.append(spec)
    lead = [pl.BlockSpec(memory_space=pltpu.SMEM)] + [pl.BlockSpec(memory_space=pl.ANY)] * (len(extra) - 1)
    return pl.pallas_call(
        kernel,
        grid=(count,),
        in_specs=(lead if extra else []) + [block(x.shape, i in fixed_ins) for i, x in enumerate(ins)],
        out_specs=out_specs,
        out_shape=[jax.ShapeDtypeStruct(s, d) for s, d in outs],
        scratch_shapes=list(scratch),
        compiler_params=pltpu.CompilerParams(vmem_limit_bytes=VMEM),
        cost_estimate=cost(us),
    )(*extra, *ins)


def mm(a, b, dims=((1,), (0,))):
    return lax.dot_general(a, b, (dims, ((), ())), preferred_element_type=F32)


def body(
    tokens,
    cotangent,
    doc_start,
    norm_gain,
    qkv_weight,
    conv_weight,
    beta_weight,
    head_gain,
    out_weight,
    ffn_gain,
    gate_up_weight,
    down_weight,
):
    groups = lax.axis_size("group")
    r = lax.axis_index("replica") % 8
    g = lax.axis_index("group")
    c, t = r % 2, r // 2
    idx = jnp.stack([c, t, g]).astype(jnp.int32)
    _, length, _ = tokens.shape
    seqs = TP
    ext_len = length + RIM
    shard = D // groups
    half = shard // 2
    ff_shard = FF // groups
    col = D // 8
    tokens = tokens.reshape(length, D)
    cot = cotangent.reshape(length, D)

    def z_pieces(x):
        return [x] + [z_turn(x, s) for s in range(1, groups)]

    def z_abs(x):
        pieces = z_pieces(x)
        return place([((g - s) % groups, piece) for s, piece in enumerate(pieces)], groups)

    def rel(x):
        x = x.reshape(x.shape[:-1] + (groups, 2, half))
        x = jnp.where(c == 0, x, jnp.flip(x, -2))
        return jnp.swapaxes(x, -3, -2).reshape(x.shape[:-3] + (D,))

    def unrel(x):
        x = jnp.swapaxes(x.reshape(x.shape[:-1] + (2, groups, half)), -3, -2)
        x = jnp.where(c == 0, x, jnp.flip(x, -2))
        return x.reshape(x.shape[:-3] + (D,))

    small = jnp.concatenate(
        [
            beta_weight.T,
            jnp.swapaxes(conv_weight.reshape(3, shard, CONV), 1, 2).reshape(3 * CONV, shard),
            ffn_gain.reshape(1, shard),
            norm_gain.reshape(1, shard),
            jnp.zeros((2, shard), BF),
        ],
        axis=0,
    )
    rim = z_shift(tokens[length - RIM :], 1)
    small = z_abs(small)
    gain_in = small[:, HEADS + 3 * CONV + 1].reshape(1, D).astype(F32)
    gain_mid = small[:, HEADS + 3 * CONV].reshape(1, D).astype(F32)
    beta_full = jnp.swapaxes(small[:, :HEADS], 0, 1).reshape(HEADS, D)
    beta_t = jnp.pad(rel(lax.dynamic_slice(beta_full, (t * HT, 0), (HT, D))).T, ((0, 0), (0, HD - HT)))
    conv_full = small[:, HEADS : HEADS + 3 * CONV].reshape(groups * 3, CONV, shard)
    conv_full = jnp.swapaxes(conv_full, 0, 1).reshape(CONV, 3, TP, DT)
    taps = jnp.swapaxes(pick(conv_full, t, 2), 0, 1).astype(F32)
    gain_head = head_gain.astype(F32).reshape(1, HD)
    doc_rel = doc_start.reshape(1, length) - g * length
    docs = jnp.concatenate(
        [doc_rel] + [plane_swap(doc_rel, j) for j in (1, 2, 3)], axis=0
    ).reshape(seqs, length, 1)
    cot_x, cot_y = plane_swap(cot, 1), plane_swap(cot, 2)
    qkv_weight, small, rim = lax.optimization_barrier((qkv_weight, small, rim))

    (normed_ext,) = whole_call(
        functools.partial(norm_kernel, groups), idx, [rim, tokens, gain_in], [((ext_len, D), BF)]
    )
    normed_pieces = plane_copies(normed_ext)

    piece = jnp.concatenate(
        [lax.dynamic_slice(qkv_weight, (c * half, j * D + t * DT), (half, DT)) for j in range(3)], axis=1
    )
    qkv_pieces = z_pieces(piece)
    qkv_late = qkv_pieces
    qkv_pieces = qkv_pieces + [core_swap(p) for p in qkv_pieces]

    h = split_at(length)
    cot_pieces = [cot, cot_x, cot_y, plane_swap(cot_x[:h], 2), plane_swap(cot_y[h:], 1)]

    piece = jnp.concatenate(
        [
            lax.dynamic_slice(out_weight, (0, r * col), (shard, col)),
            lax.dynamic_slice(down_weight, (0, r * col), (ff_shard, col)),
        ],
        axis=0,
    )
    both = lax.all_gather(after(piece, *qkv_late), "group", axis=0)

    normed_pieces[0] = after(normed_pieces[0], *cot_pieces[:3])

    wide = (seqs, length, DT)
    square = (seqs, HT, HD, HD)
    (
        queries, key_rows, value_rows, inverse, u0, w, move, free, projected, rates, normed_all, qkv,
    ) = call(
        functools.partial(front_kernel, groups),
        [beta_t, taps, docs],
        (0, 1),
        [
            (wide, BF),
            (wide, BF),
            (wide, BF),
            ((seqs, HT, length, length), BF),
            (wide, F32),
            (wide, BF),
            (square, BF),
            (square, F32),
            ((seqs, ext_len, 3 * DT), BF),
            ((seqs, length, HD), F32),
            ((seqs * ext_len, D), BF),
            ((D, 3 * DT), BF),
        ],
        us=40,
        extra=[idx, *normed_pieces, *qkv_pieces],
        scratch=[pltpu.SemaphoreType.DMA((5,)), pltpu.SemaphoreType.DMA((2 * groups,))],
        held_outs=(10, 11),
    )
    piece = jnp.concatenate(
        [
            lax.dynamic_slice(gate_up_weight, (c * half, j * FF + t * FT), (half, FT))
            for j in range(2)
        ],
        axis=1,
    )
    gate_up = lax.all_gather(after(piece, free), "group", axis=0, tiled=True)

    state = jnp.zeros(square, BF)
    for hop in range(groups - 1):
        leaving = jnp.einsum("shij,shjk->shik", move, state, preferred_element_type=F32) + free
        if hop == groups - 2:
            leaving = after(leaving, *downs, *outs)
        state = z_shift(leaving.astype(BF), 1)
        if hop == 0:
            both = after(both, free)
            part = both[:, shard:].reshape(TP, FT, col)
            downs = plane_trade([pick(part, t ^ j) for j in range(TP)])
            outs = both[:, :shard].reshape(D, col)
            outs = plane_copies(outs)
    outs = outs + [core_swap(p) for p in outs]
    downs = downs + [core_swap(p) for p in downs]
    normed, head_out, update = call(
        out_kernel,
        [gain_head, queries, key_rows, u0, w, state, docs],
        (0,),
        [(wide, BF), (wide, F32), (wide, BF)],
        us=6,
    )

    def plan(ref):
        moves = []
        for cc in range(2):
            for j in range(TP):
                at = ((ref[1] ^ j) * 2 + (ref[0] ^ cc)) * col
                for b in range(TP):
                    n, first = (j, b) if j < 3 else ((3, b) if b < 2 else (4, b - 2))
                    moves.append(
                        (
                            5 * cc + n,
                            pl.ds(first * DT, DT),
                            (
                                pl.ds(pl.multiple_of((ref[1] ^ b) * DT, DT), DT),
                                pl.ds(pl.multiple_of(at, 128), col),
                            ),
                        )
                    )
        return moves

    out_w = assemble(idx, outs, plan, (D, D))

    heads = plane_trade([normed[j] for j in range(TP)])
    middle, normed_mid = whole_call(
        functools.partial(mid_kernel, groups),
        idx,
        heads + [out_w, tokens, gain_mid],
        [((length, D), F32), ((length, D), BF)],
        us=10,
    )
    mid_pieces = plane_copies(normed_mid)
    gate_ups = [gate_up, core_swap(after(gate_up, mid_pieces[1], mid_pieces[2]))]

    hidden, grad_gate_up, mid_part, cot_away, cot_mine, mid_all, down = call(
        ffn_kernel,
        [docs],
        (),
        [
            ((seqs, length, FT), BF),
            ((seqs, length, 2 * FT), BF),
            ((seqs, length, D), BF),
            ((seqs, length, D // 2), BF),
            ((seqs, length, D // 2), BF),
            ((seqs * length, D), BF),
            ((FT, D), BF),
        ],
        us=45,
        extra=[idx, *mid_pieces, *cot_pieces, *gate_ups, *downs],
        scratch=[pltpu.VMEM((seqs * length, D), BF), pltpu.VMEM((D, 2 * FT), BF)]
        + [pltpu.SemaphoreType.DMA((n,)) for n in (5, 5, 2, 8)],
        held_outs=(5, 6),
    )
    hidden = hidden.reshape(-1, FT)
    grad_gate_up = grad_gate_up.reshape(-1, 2 * FT)
    def two_halves(left, right):
        away = mm(left[:, groups * half :], right, TN).astype(BF)
        mine = mm(left[:, : groups * half], right, TN)
        return (mine + core_swap(away).astype(F32)).astype(BF).reshape(groups, half, -1)

    def two_columns(left, away, mine):
        away = mm(left, away, TN).astype(BF)
        mine = mm(left, mine, TN)
        return (mine + core_swap(away).astype(F32)).astype(BF)

    def z_sum(x, *others):
        total = pick(x, g).astype(F32)
        for s in range(1, groups):
            total = total + after(z_turn(pick(x, (g + s) % groups), s), *others).astype(F32)
        return total

    parts = plane_parts([mid_part[j] for j in range(TP)])
    gate_sums = [two_halves(mid_all, grad_gate_up[:, i * FT : (i + 1) * FT]) for i in range(2)]
    down_sum = two_columns(hidden, cot_away.reshape(-1, D // 2), cot_mine.reshape(-1, D // 2))
    first_sum = far_sum(lax.psum_scatter(gate_sums[0], "group", scatter_dimension=0)).astype(BF)
    parts, second_sum, down_sum = lax.optimization_barrier((parts, gate_sums[1], down_sum))
    second_sum = far_sum(lax.psum_scatter(second_sum, "group", scatter_dimension=0)).astype(BF)
    grad_middle, branch_away, branch_mine, *dheads, ffn_gain_part = whole_call(
        functools.partial(mid_back_kernel, groups),
        idx,
        parts + [middle.reshape(length, D), cot, gain_mid, out_w],
        [((length, D), F32)]
        + [((length, D // 2), BF)] * 2
        + [((length, DT), BF)] * TP
        + [((1, D), F32)],
        us=13,
        scratch=[pltpu.VMEM((length, D), BF)],
    )
    dnormed = jnp.stack(plane_trade(dheads))

    normed_abs = jnp.swapaxes(
        place([(t ^ j, heads[j]) for j in range(TP)], TP), 0, 1
    ).reshape(length, D)
    out_sum = two_columns(normed_abs, branch_away, branch_mine)
    both = [
        jnp.concatenate([x[:, j * col : (j + 1) * col] for x in (down_sum, out_sum)], axis=0)
        for j in range(TP)
    ]
    dnormed = after(dnormed, first_sum, *both)
    both = plane_trade(both)

    grad_out, y0, z, local, head_part = call(
        back_kernel,
        [gain_head, dnormed, head_out, queries, key_rows, inverse, rates, docs],
        (0,),
        [(wide, BF), (wide, F32), (wide, BF), (square, F32), ((8, HD), F32)],
        (4,),
        us=12,
    )


    later = jnp.zeros(square, BF)
    for hop in range(groups - 1):
        leaving = jnp.einsum("shji,shjk->shik", move, later, preferred_element_type=F32) + local
        later = z_shift(leaving.astype(BF), -1)

    (both_sum,) = whole_call(
        functools.partial(join_kernel, groups), idx, both, [((groups, shard + ff_shard, col), BF)]
    )
    later = after(later, both_sum, second_sum)
    gate_sum = jnp.concatenate([first_sum, second_sum], axis=1)
    both_sum = lax.psum_scatter(both_sum, "group", scatter_dimension=0)
    gate_pieces = spread_first(gate_sum)
    grad_proj, grad_logit, in_part, conv_part = call(
        grad_kernel,
        [
            taps, qkv, beta_t, projected, docs, rates, queries, key_rows, value_rows, state, update, grad_out,
            y0, z, later,
        ],
        (0, 1, 2),
        [
            ((seqs, ext_len, 3 * DT), BF),
            ((seqs, ext_len, HD), BF),
            ((seqs, ext_len, D), BF),
            ((3, CONV, DT), F32),
        ],
        (3,),
        us=44,
    )
    qkv_sum = two_halves(normed_all, grad_proj.reshape(-1, 3 * DT))
    qkv_mine = qkv_sum
    gate_pieces = spread_pieces([after(p, qkv_sum) for p in gate_pieces])
    rim = z_shift(in_part[:, :RIM], -1)
    in_part = after(in_part[:, RIM:], qkv_sum)
    qkv_sum = z_sum(qkv_sum)
    ends_in = (in_part[:, length - RIM :].astype(F32) + rim.astype(F32)).astype(BF)
    in_part = jnp.concatenate([in_part[:, : length - RIM], ends_in], axis=1)
    parts = plane_parts([in_part[j] for j in range(TP)])
    parts[0] = after(parts[0], qkv_sum)
    input_grad, norm_gain_part = whole_call(
        functools.partial(in_back_kernel, groups),
        idx,
        parts + [tokens, grad_middle, gain_in],
        [((length, D), F32), ((1, D), F32)],
        us=0.05,
    )
    out_part = mm(after(hidden, qkv_mine), down).astype(BF).reshape(TP, length, D)
    output = (middle + plane_sum([out_part[j] for j in range(TP)])).astype(BF)

    beta_part = mm(grad_logit.reshape(-1, HD), normed_all, TN)[:HT]
    beta_all = lax.dynamic_update_slice(jnp.zeros((HEADS, D), F32), unrel(beta_part), (t * HT, 0))
    conv_all = lax.dynamic_update_slice(
        jnp.zeros((CONV, 3, TP, DT), F32), jnp.swapaxes(conv_part, 0, 1)[:, :, None], (0, 0, t, 0)
    )
    conv_all = jnp.swapaxes(conv_all.reshape(CONV, groups * 3, shard), 0, 1)
    pack = jnp.concatenate(
        [
            jnp.swapaxes(beta_all.reshape(HEADS, groups, shard), 0, 1),
            conv_all.reshape(groups, 3 * CONV, shard),
            norm_gain_part.reshape(groups, 1, shard),
            ffn_gain_part.reshape(groups, 1, shard),
            jnp.broadcast_to(jnp.pad(head_part[:1], ((0, 0), (0, shard - HD))), (groups, 1, shard)),
            jnp.zeros((groups, 1, shard), F32),
        ],
        axis=1,
    )
    pack = pack + core_swap(pack)
    pack = pack + plane_swap(pack, 1)
    pack = pack + plane_swap(pack, 2)

    (gate_up_grad,) = spread_out(idx, gate_pieces, 2)

    total = far_sum(z_sum(after(pack, qkv_sum)))
    both_pieces = [after(p, qkv_sum) for p in spread_first(far_sum(both_sum).astype(BF))]
    qkv_pieces = [after(p, gate_up_grad, output) for p in spread_first(far_sum(qkv_sum).astype(BF))]
    qkv_pieces = spread_pieces(qkv_pieces)
    down_grad, out_grad = spread_out(idx, both_pieces, 0, (ff_shard, shard))
    qkv_pieces[0] = after(qkv_pieces[0], total, out_grad, down_grad)
    (qkv_grad,) = spread_out(idx, qkv_pieces, 3)
    beta_grad = total[:HEADS].T
    conv_grad = jnp.swapaxes(total[HEADS : HEADS + 3 * CONV].reshape(3, CONV, shard), 1, 2)
    at = HEADS + 3 * CONV
    return (
        output.reshape(1, length, D),
        input_grad.reshape(1, length, D),
        total[at],
        qkv_grad,
        conv_grad.reshape(-1, CONV),
        beta_grad,
        total[at + 2, :HD],
        out_grad,
        total[at + 1],
        gate_up_grad,
        down_grad,
    )


def solution(mesh):
    rows = P("replica", "group", None)
    shard = P("group", None)
    return jax.shard_map(
        body,
        mesh=mesh,
        in_specs=(
            rows, rows, P("replica", "group"), P("group"), shard, shard, shard, P(), shard, P("group"), shard, shard,
        ),
        out_specs=(
            rows, rows, P("group"), shard, shard, shard, P(), shard, P("group"), shard, shard,
        ),
        check_vma=False,
    )
```

```python
import functools

import jax
import jax.numpy as jnp
from jax import lax
from jax.experimental import pallas as pl
from jax.experimental.pallas import tpu as pltpu
from jax.sharding import PartitionSpec as P

D = 2048
HEADS = 16
HD = 128
FF = 5632
CONV = 4
EPS = 1e-06
RIM = 16
TP = 4
HT = HEADS // TP
DT = D // TP
FT = FF // TP
SCALE = HD**-0.5
VMEM = 56 * 1024 * 1024

BF = jnp.bfloat16
F32 = jnp.float32


def swap(x, bits):
    n = lax.axis_size("replica")
    return lax.ppermute(x, "replica", [(i, i ^ bits) for i in range(n)])


def plane_swap(x, j):
    return swap(x, 2 * j)


def core_swap(x):
    return swap(x, 1)


def far_sum(x):
    x = x.astype(F32)
    bits = 8
    while bits < lax.axis_size("replica"):
        x = x + swap(x.astype(BF), bits).astype(F32)
        bits *= 2
    return x


def z_shift(x, by):
    n = lax.axis_size("group")
    return lax.ppermute(x, "group", [(i, i + by) for i in range(n) if 0 <= i + by < n])


def z_turn(x, by):
    n = lax.axis_size("group")
    return lax.ppermute(x, "group", [(i, (i + by) % n) for i in range(n)])


def plane_copies(x):
    a, b = plane_swap(x, 1), plane_swap(x, 2)
    h = split_at(x.shape[0])
    return [x, a, b, plane_swap(a[:h], 2), plane_swap(b[h:], 1)]


def plane_parts(parts):
    own, x, y, d = parts
    h = split_at(own.shape[0])
    via_x, via_y = plane_swap(d[:h], 1), plane_swap(d[h:], 2)
    y = jnp.concatenate([(y[:h].astype(F32) + via_x.astype(F32)).astype(BF), y[h:]], axis=0)
    x = jnp.concatenate([x[:h], (x[h:].astype(F32) + via_y.astype(F32)).astype(BF)], axis=0)
    return [own, plane_swap(x, 1), plane_swap(y, 2)]


def plane_sum(parts):
    own, x, y = plane_parts([p.astype(BF) for p in parts])
    return parts[0].astype(F32) + x.astype(F32) + y.astype(F32)


def after(x, *others):
    return lax.optimization_barrier((x, *others))[0]


def plane_trade(parts):
    return [parts[0]] + [plane_swap(parts[j], j) for j in (1, 2, 3)]


def place(pieces, count, axis=0):
    shape = list(pieces[0][1].shape)
    shape.insert(axis, count)
    buf = jnp.zeros(shape, pieces[0][1].dtype)
    for index, piece in pieces:
        buf = lax.dynamic_update_index_in_dim(buf, piece, index, axis)
    return buf


def pick(x, index, axis=0):
    return lax.dynamic_index_in_dim(x, index, axis, keepdims=False)


def dot(a, b, dims=((1,), (0,))):
    return lax.dot_general(a, b, (dims, ((), ())), preferred_element_type=F32)


NT = ((1,), (1,))
TN = ((0,), (0,))


def iotas(rows, cols):
    return (
        lax.broadcasted_iota(jnp.int32, (rows, cols), 0),
        lax.broadcasted_iota(jnp.int32, (rows, cols), 1),
    )


def unit_lower_inverses(mats):
    n = mats[0].shape[0]
    base, tile = 16, 128
    ri, ci = iotas(n, n)
    lane = lax.broadcasted_iota(jnp.int32, (base, tile), 1) % base
    rows = lax.broadcasted_iota(jnp.int32, (base, tile), 0)
    picks = [lane == j for j in range(base)]
    rt, ct = iotas(tile, tile)
    same = (rt // base) == (ct // base)
    ones = same.astype(BF)
    zero = jnp.zeros((), BF)
    lows = [a.astype(BF) for a in mats]
    spans = [slice(at, at + tile) for at in range(0, n, tile)]
    blocks = [(m, span) for m in range(len(mats)) for span in spans]
    wides = []
    for m, span in blocks:
        part = jnp.where(same, mats[m][span, span], 0.0)
        compact = jnp.sum(part.reshape(tile // base, base, tile), axis=0).astype(BF)
        spread = jnp.concatenate([jnp.where(p, compact, zero) for p in picks], axis=0)
        wides.append(dot(spread, ones))
    xs = [(lane == rows).astype(F32)] * len(blocks)
    for j in range(base - 1):
        xs = [x - w[j * base : (j + 1) * base] * x[j : j + 1] for x, w in zip(xs, wides)]
    fulls = [jnp.where(same, jnp.concatenate([x] * (tile // base), axis=0), 0.0) for x in xs]
    size = base
    while size < tile:
        part = (
            ((rt // (2 * size)) == (ct // (2 * size)))
            & ((rt // size) % 2 == 1)
            & ((ct // size) % 2 == 0)
        )
        halves = [full.astype(BF) for full in fulls]
        inner = [
            dot(jnp.where(part, lows[m][span, span], zero), h).astype(BF)
            for (m, span), h in zip(blocks, halves)
        ]
        fulls = [full - dot(h, i) for full, h, i in zip(fulls, halves, inner)]
        size *= 2
    fulls = [full.astype(BF) for full in fulls]
    if n == tile:
        return fulls
    inner = [dot(low[tile:, :tile], fulls[2 * m]).astype(BF) for m, low in enumerate(lows)]
    corners = [-dot(fulls[2 * m + 1], i) for m, i in enumerate(inner)]
    blank = jnp.zeros((tile, tile), BF)
    return [
        jnp.concatenate(
            [
                jnp.concatenate([fulls[2 * m], blank], axis=1),
                jnp.concatenate([corner.astype(BF), fulls[2 * m + 1]], axis=1),
            ],
            axis=0,
        )
        for m, corner in enumerate(corners)
    ]


def tap_masks(doc, length):
    pos = lax.broadcasted_iota(jnp.int32, (length, 1), 0)
    return [
        jnp.broadcast_to((pos - (CONV - 1) + i >= doc).astype(F32), (length, HD)) for i in range(CONV - 1)
    ]


def conv_rows(ext, taps, kept, length):
    total = ext[RIM : RIM + length] * taps[CONV - 1 : CONV]
    for i in range(CONV - 1):
        first = RIM - (CONV - 1) + i
        total = total + ext[first : first + length] * taps[i : i + 1] * kept[i]
    return total


def masks(doc, length):
    ri, ci = iotas(length, length)
    same = (doc <= ci) & (ri >= ci)
    return same.astype(F32), (same & (ri > ci)).astype(F32)


def ends(doc, length):
    last = doc[length - 1 : length]
    pos = lax.broadcasted_iota(jnp.int32, (length, 1), 0)
    return (pos >= last).astype(F32), (last < 0).astype(F32), (doc < 0).astype(F32)


def row_starts(n):
    return (0, n, 2 * n, 3 * n, 3 * n + split_at(n))


def row_copies(srcs, dst, sem):
    starts = row_starts(srcs[0].shape[0])
    return [
        pltpu.make_async_copy(src, dst.at[pl.ds(starts[i], src.shape[0])], sem.at[i])
        for i, src in enumerate(srcs)
    ]


def front_kernel(groups, *refs):
    idx_ref, xs, ws = refs[0], refs[1:6], refs[6 : 6 + 2 * groups]
    (
        beta_ref, taps_ref, doc_ref, qo, ko, vo, t_ref, u0_ref, wo_ref, m_ref, b_ref, p_ref, rate_ref,
        all_ref, w_ref, x_sem, w_sem,
    ) = refs[6 + 2 * groups :]
    length = doc_ref.shape[1]
    half = ws[0].shape[0]
    step = pl.program_id(0)

    @pl.when(step == 0)
    def _():
        copies = row_copies(xs, all_ref, x_sem)
        for cc in range(2):
            for s in range(groups):
                at = (cc * groups + (idx_ref[2] + groups - s) % groups) * half
                copies.append(
                    pltpu.make_async_copy(
                        ws[cc * groups + s],
                        w_ref.at[pl.ds(pl.multiple_of(at, 128), half)],
                        w_sem.at[cc * groups + s],
                    )
                )
        for copy in copies:
            copy.start()
        for copy in copies:
            copy.wait()

    rows = length + RIM
    here = pl.ds(pl.multiple_of(step * rows, 16), rows)
    doc = doc_ref[0]
    same, strict = masks(doc, length)
    tail, keep, carried = ends(doc, length)
    eye = (iotas(HD, HD)[0] == iotas(HD, HD)[1]).astype(F32)

    for i in range(3 * DT // 256):
        cols = slice(i * 256, (i + 1) * 256)
        p_ref[0, :, cols] = dot(all_ref[here], w_ref[:, cols]).astype(BF)

    own = pl.ds(pl.multiple_of(step * rows + RIM, 16), length)
    rates = jax.nn.sigmoid(dot(all_ref[own], beta_ref[...]))
    rate_ref[0] = rates
    kept = tap_masks(doc, length)
    wide = (length, HD)
    tail, carried = jnp.broadcast_to(tail, wide), jnp.broadcast_to(carried, wide)
    head_rates = [jnp.broadcast_to(rates[:, h : h + 1], wide) for h in range(HT)]
    lanes = [slice(h * HD, (h + 1) * HD) for h in range(HT)]
    mats = []
    for h in range(HT):
        acts = []
        for part in range(3):
            cols = slice(part * DT + h * HD, part * DT + (h + 1) * HD)
            mixed = conv_rows(p_ref[0, :, cols].astype(F32), taps_ref[part, :, lanes[h]], kept, length)
            acts.append(mixed * jax.nn.sigmoid(mixed))
        qa, ka, va = acts
        q = (qa * (lax.rsqrt(jnp.sum(qa * qa, axis=-1, keepdims=True) + EPS) * SCALE)).astype(BF)
        k = (ka * lax.rsqrt(jnp.sum(ka * ka, axis=-1, keepdims=True) + EPS)).astype(BF)
        qo[0, :, lanes[h]] = q
        ko[0, :, lanes[h]] = k
        vo[0, :, lanes[h]] = va.astype(BF)
        mats.append(dot(k, k, NT) * (strict * rates[:, h : h + 1]))
    invs = unit_lower_inverses(mats)
    for h in range(HT):
        inv, rate = invs[h], head_rates[h]
        kf = ko[0, :, lanes[h]].astype(F32)
        u0 = dot(inv, (vo[0, :, lanes[h]].astype(F32) * rate).astype(BF))
        w = dot(inv, (kf * (rate * carried)).astype(BF)).astype(BF)
        kl = (kf * tail).astype(BF)
        m_ref[0, h] = (eye * keep - dot(kl, w, TN)).astype(BF)
        b_ref[0, h] = dot(kl, u0.astype(BF), TN)
        t_ref[0, h] = inv
        u0_ref[0, :, lanes[h]] = u0
        wo_ref[0, :, lanes[h]] = w


def out_kernel(gain_ref, q_ref, k_ref, u0_ref, w_ref, s_ref, doc_ref, n_ref, o_ref, u_ref):
    length = doc_ref.shape[1]
    doc = doc_ref[0]
    same, _ = masks(doc, length)
    carried = (doc < 0).astype(F32)
    gain = gain_ref[...]
    for h in range(HT):
        lanes = slice(h * HD, (h + 1) * HD)
        q, k, state = q_ref[0, :, lanes], k_ref[0, :, lanes], s_ref[0, h]
        u = (u0_ref[0, :, lanes] - dot(w_ref[0, :, lanes], state)).astype(BF)
        scores = (dot(q, k, NT) * same).astype(BF)
        o = dot(scores, u) + dot(q, state) * carried
        r = lax.rsqrt(jnp.mean(o * o, axis=-1, keepdims=True) + EPS)
        n_ref[0, :, lanes] = (o * r * gain).astype(BF)
        o_ref[0, :, lanes] = o
        u_ref[0, :, lanes] = u


def back_kernel(
    gain_ref, dn_ref, o_ref, q_ref, k_ref, t_ref, rate_ref, doc_ref, g_ref, y_ref, z_ref, l_ref, hg_ref
):
    length = doc_ref.shape[1]
    doc = doc_ref[0]
    same, _ = masks(doc, length)
    tail, _, carried = ends(doc, length)
    gain = gain_ref[...]

    @pl.when(pl.program_id(0) == 0)
    def _():
        hg_ref[...] = jnp.zeros_like(hg_ref)

    total = jnp.zeros((1, HD), F32)
    for h in range(HT):
        lanes = slice(h * HD, (h + 1) * HD)
        o, dy = o_ref[0, :, lanes], dn_ref[0, :, lanes].astype(F32)
        r = lax.rsqrt(jnp.mean(o * o, axis=-1, keepdims=True) + EPS)
        total = total + jnp.sum(o * r * dy, axis=0, keepdims=True)
        gy = gain * dy
        gf = r * gy - o * (r * r * r * jnp.mean(o * gy, axis=-1, keepdims=True))
        g = gf.astype(BF)
        q, k = q_ref[0, :, lanes], k_ref[0, :, lanes]
        inv = t_ref[0, h]
        scores = (dot(q, k, NT) * same).astype(BF)
        kf = k.astype(F32)
        y = dot(inv, dot(scores, g, TN).astype(BF), TN)
        z_ref[0, :, lanes] = dot(inv, (kf * tail).astype(BF), TN).astype(BF)
        rate = rate_ref[0, :, h : h + 1]
        l_ref[0, h] = dot((q.astype(F32) * carried).astype(BF), g, TN) - dot(
            (kf * (rate * carried)).astype(BF), y.astype(BF), TN
        )
        g_ref[0, :, lanes] = g
        y_ref[0, :, lanes] = y
    hg_ref[0:1] += total


def unit_back(act, dy, scale):
    r = lax.rsqrt(jnp.sum(act * act, axis=-1, keepdims=True) + EPS)
    inner = jnp.sum(act * dy, axis=-1, keepdims=True)
    return (r * scale) * dy - act * (r * r * r * scale * inner)


def grad_kernel(
    taps_ref, w_ref, beta_ref, p_ref, doc_ref, rate_ref, q_ref, k_ref, v_ref, s_ref, u_ref, g_ref, y_ref,
    z_ref, a_ref, gp_ref, gl_ref, in_ref, cg_ref,
):
    length = doc_ref.shape[1]
    doc = doc_ref[0]
    same, strict = masks(doc, length)
    tail, _, carried = ends(doc, length)

    @pl.when(pl.program_id(0) == 0)
    def _():
        cg_ref[...] = jnp.zeros_like(cg_ref)

    logits = []
    kept = tap_masks(doc, length)
    tail, carried = jnp.broadcast_to(tail, (length, HD)), jnp.broadcast_to(carried, (length, HD))
    for h in range(HT):
        lanes = slice(h * HD, (h + 1) * HD)
        q, k, v = q_ref[0, :, lanes], k_ref[0, :, lanes], v_ref[0, :, lanes]
        state, u, g, adj = s_ref[0, h], u_ref[0, :, lanes], g_ref[0, :, lanes], a_ref[0, h]
        rate = rate_ref[0, :, h : h + 1]
        yf = y_ref[0, :, lanes] + dot(z_ref[0, :, lanes], adj)
        y = yf.astype(BF)
        dv = rate * yf
        d1 = dot(y, u, NT) * strict
        gram = dot(k, k, NT)
        e = v.astype(F32) - dot(k, state) * carried
        drate = jnp.sum(yf * e, axis=-1, keepdims=True) - jnp.sum(d1 * gram, axis=-1, keepdims=True)
        dgram = (d1 * (-rate)).astype(BF)
        dscore = (dot(g, u, NT) * same).astype(BF)
        dq = dot(dscore, k) + dot(g, state, NT) * carried
        dk = dot(dscore, q, TN) + dot(dgram, k) + dot(dgram, k, TN)
        dk = dk - dot(y, state, NT) * (rate * carried) + dot(u, adj, NT) * tail
        logits.append(drate * rate * (1.0 - rate))
        for part, grad in enumerate((dq, dk, dv)):
            cols = slice(part * DT + h * HD, part * DT + (h + 1) * HD)
            ext = p_ref[0, :, cols].astype(F32)
            taps = taps_ref[part, :, lanes]
            mixed = conv_rows(ext, taps, kept, length)
            s = jax.nn.sigmoid(mixed)
            if part < 2:
                grad = unit_back(mixed * s, grad, SCALE if part == 0 else 1.0)
            gm = grad * (s * (1.0 + mixed * (1.0 - s)))
            total = jnp.zeros((length + RIM, HD), F32)
            for i in range(CONV):
                gv = gm * kept[i] if i < CONV - 1 else gm
                first = RIM - (CONV - 1) + i
                cg_ref[part, i : i + 1, lanes] += jnp.sum(
                    gv * ext[first : first + length], axis=0, keepdims=True
                )
                gv = gv * taps[i : i + 1]
                pads = [jnp.zeros((first, HD), F32), gv]
                if RIM - first > 0:
                    pads.append(jnp.zeros((RIM - first, HD), F32))
                total = total + jnp.concatenate(pads, axis=0)
            gp_ref[0, :, cols] = total.astype(BF)
    lane = lax.broadcasted_iota(jnp.int32, (length, HD), 1)
    wide = jnp.zeros((length, HD), F32)
    for h in range(HT):
        wide = jnp.where(lane == h, logits[h], wide)
    gl_ref[0, :RIM] = jnp.zeros((RIM, HD), BF)
    gl_ref[0, RIM:] = wide.astype(BF)

    for i in range(D // 256):
        span = slice(i * 256, (i + 1) * 256)
        total = dot(gp_ref[0], w_ref[span], NT) + dot(gl_ref[0], beta_ref[span], NT)
        in_ref[0, :, span] = total.astype(BF)


def to_rel(x, c, groups):
    half = D // groups // 2
    out = []
    for cc in range(2):
        for i in range(groups):
            at = i * 2 * half
            one, two = x[:, at : at + half], x[:, at + half : at + 2 * half]
            out.append(jnp.where(c == 0, one, two) if cc == 0 else jnp.where(c == 0, two, one))
    return jnp.concatenate(out, axis=1)


def from_rel(x, c, groups):
    half = D // groups // 2
    out = []
    for i in range(groups):
        one, two = x[:, i * half : (i + 1) * half], x[:, (groups + i) * half : (groups + i + 1) * half]
        out += [jnp.where(c == 0, one, two), jnp.where(c == 0, two, one)]
    return jnp.concatenate(out, axis=1)


def norm_kernel(groups, idx_ref, rim_ref, x_ref, gain_ref, n_ref):
    c = idx_ref[0]
    for src, span in ((rim_ref, slice(0, RIM)), (x_ref, slice(RIM, RIM + x_ref.shape[0]))):
        x = src[...].astype(F32)
        r = lax.rsqrt(jnp.mean(x * x, axis=-1, keepdims=True) + EPS)
        n_ref[span] = to_rel(x * r * gain_ref[...], c, groups).astype(BF)


def mid_kernel(groups, idx_ref, n0, n1, n2, n3, w_ref, x_ref, gain_ref, mid_ref, n_ref):
    c = idx_ref[0]
    heads = (n0, n1, n2, n3)

    for i in range(D // 256):
        span = slice(i * 256, (i + 1) * 256)
        total = x_ref[:, span].astype(F32)
        for j in range(TP):
            total = total + dot(heads[j][...], w_ref[j * DT : (j + 1) * DT, span])
        mid_ref[:, span] = total

    x = mid_ref[...]
    r = lax.rsqrt(jnp.mean(x * x, axis=-1, keepdims=True) + EPS)
    n_ref[...] = to_rel(x * r * gain_ref[...], c, groups).astype(BF)


def norm_back_rows(groups, c, parts, x, gain):
    dy = parts[0].astype(F32)
    for part in parts[1:]:
        dy = dy + part.astype(F32)
    dy = from_rel(dy, c, groups)
    r = lax.rsqrt(jnp.mean(x * x, axis=-1, keepdims=True) + EPS)
    gy = gain * dy
    dx = r * gy - x * (r * r * r * jnp.mean(x * gy, axis=-1, keepdims=True))
    return dx, jnp.sum(x * r * dy, axis=0, keepdims=True)


def mid_back_kernel(
    groups, idx_ref, p0, p1, p2, x_ref, cot_ref, gain_ref, w_ref, gm_ref, away_ref, mine_ref, d0, d1, d2, d3,
    gg_ref, br_ref,
):
    parts = [p[...] for p in (p0, p1, p2)]
    dx, gain_part = norm_back_rows(groups, idx_ref[0], parts, x_ref[...], gain_ref[...])
    grad = cot_ref[...].astype(F32) + dx
    gm_ref[...] = grad
    br_ref[...] = grad.astype(BF)
    gg_ref[...] = gain_part
    col = D // 8
    for j in range(TP):
        for cc, ref in ((1, away_ref), (0, mine_ref)):
            at = (jnp.bitwise_xor(idx_ref[1], j) * 2 + jnp.bitwise_xor(idx_ref[0], cc)) * col
            ref[:, j * col : (j + 1) * col] = br_ref[:, pl.ds(pl.multiple_of(at, 128), col)]
    for j, d_ref in enumerate((d0, d1, d2, d3)):
        for i in range(DT // 256):
            at = i * 256
            d_ref[:, at : at + 256] = dot(br_ref[...], w_ref[j * DT + at : j * DT + at + 256], NT).astype(BF)


def in_back_kernel(groups, idx_ref, p0, p1, p2, x_ref, base_ref, gain_ref, out_ref, gg_ref):
    parts = [p[...] for p in (p0, p1, p2)]
    dx, gain_part = norm_back_rows(groups, idx_ref[0], parts, x_ref[...].astype(F32), gain_ref[...])
    out_ref[...] = base_ref[...] + dx
    gg_ref[...] = gain_part


def ffn_kernel(*refs):
    idx_ref, xs, cs, gus, downs = refs[0], refs[1:6], refs[6:11], refs[11:13], refs[13:21]
    hid_ref, gg_ref, part_ref, away_ref, mine_ref, x_ref, d_ref, c_ref, w_ref = refs[22:31]
    x_sem, c_sem, w_sem, d_sem = refs[31:]
    length = hid_ref.shape[1]
    c, t = idx_ref[0], idx_ref[1]
    step = pl.program_id(0)
    depth = gus[0].shape[0]
    col = downs[0].shape[1]

    def x_copies():
        return row_copies(xs, x_ref, x_sem)

    def c_copies():
        return row_copies(cs, c_ref, c_sem)

    def w_copies():
        return [
            pltpu.make_async_copy(gus[i], w_ref.at[pl.ds(i * depth, depth)], w_sem.at[i]) for i in range(2)
        ]

    def d_copies():
        out = []
        for cc in range(2):
            for j in range(TP):
                at = (jnp.bitwise_xor(t, j) * 2 + jnp.bitwise_xor(c, cc)) * col
                n = cc * TP + j
                out.append(
                    pltpu.make_async_copy(
                        downs[n], d_ref.at[:, pl.ds(pl.multiple_of(at, 128), col)], d_sem.at[n]
                    )
                )
        return out

    @pl.when(step == 0)
    def _():
        first = w_copies() + x_copies()
        for copy in first + c_copies() + d_copies():
            copy.start()
        for copy in first:
            copy.wait()

    here = pl.ds(pl.multiple_of(step * length, 16), length)

    def hidden_tile(at, width):
        cols = pl.ds(at, width)
        ups = pl.ds(FT + at, width)
        x = x_ref[here]
        gate, up = dot(x, w_ref[:, cols]), dot(x, w_ref[:, ups])
        grad = dot(c_ref[here], d_ref[cols], NT)
        sg = jax.nn.sigmoid(gate)
        act = gate * sg
        hid_ref[0, :, cols] = (act * up).astype(BF)
        gg_ref[0, :, cols] = (grad * up * (sg * (1.0 + gate * (1.0 - sg)))).astype(BF)
        gg_ref[0, :, ups] = (grad * act).astype(BF)

    @pl.when(step == 0)
    def _():
        for copy in c_copies() + d_copies():
            copy.wait()

    tiles = FT // 256

    for i in range(tiles):
        hidden_tile(i * 256, 256)

    if FT % 256:
        hidden_tile(tiles * 256, FT % 256)

    for i in range(D // 256):
        span = slice(i * 256, (i + 1) * 256)
        part_ref[0, :, span] = dot(gg_ref[0], w_ref[span], NT).astype(BF)

    for j in range(TP):
        for cc, ref in ((1, away_ref), (0, mine_ref)):
            at = (jnp.bitwise_xor(t, j) * 2 + jnp.bitwise_xor(c, cc)) * col
            ref[0, :, j * col : (j + 1) * col] = c_ref[here, pl.ds(pl.multiple_of(at, 128), col)]


def whole_call(kernel, idx, ins, outs, us=5, scratch=()):
    return pl.pallas_call(
        kernel,
        in_specs=[pl.BlockSpec(memory_space=pltpu.SMEM)]
        + [pl.BlockSpec(memory_space=pltpu.VMEM)] * len(ins),
        out_specs=[pl.BlockSpec(memory_space=pltpu.VMEM)] * len(outs),
        out_shape=[jax.ShapeDtypeStruct(s, d) for s, d in outs],
        scratch_shapes=list(scratch),
        compiler_params=pltpu.CompilerParams(vmem_limit_bytes=VMEM),
        cost_estimate=cost(us),
    )(idx, *ins)


def assemble(idx, pieces, plan, shape, us=5):
    count = len(plan([0, 0, 0]))

    def kernel(idx_ref, *refs):
        srcs, out, sem = refs[: len(pieces)], refs[-2], refs[-1]
        copies = [
            pltpu.make_async_copy(srcs[p].at[src], out.at[dst], sem.at[n])
            for n, (p, src, dst) in enumerate(plan(idx_ref))
        ]
        for copy in copies:
            copy.start()
        for copy in copies:
            copy.wait()

    dtype = pieces[0].dtype
    return pl.pallas_call(
        kernel,
        in_specs=[pl.BlockSpec(memory_space=pltpu.SMEM)] + [pl.BlockSpec(memory_space=pl.ANY)] * len(pieces),
        out_specs=pl.BlockSpec(memory_space=pltpu.VMEM),
        out_shape=jax.ShapeDtypeStruct(shape, dtype),
        scratch_shapes=[pltpu.SemaphoreType.DMA((count,))],
        compiler_params=pltpu.CompilerParams(vmem_limit_bytes=VMEM),
        cost_estimate=cost(us),
    )(idx, *pieces)


def split_at(rows):
    unit = 16
    while unit < 128 and rows % (2 * unit) == 0:
        unit *= 2
    return (rows // unit + 1) // 2 * unit if unit >= 64 and rows // unit > 8 else rows // 32 * 16


def chunk_of(rows, cap):
    best = 16
    for q in range(16, cap + 1, 16):
        if rows % q == 0:
            best = q
    return best


def join_kernel(groups, idx_ref, g0, g1, g2, g3, out_ref):
    t = idx_ref[1]
    got = (g0, g1, g2, g3)
    shard, ff_shard = D // groups, FF // groups
    for i in range(groups):
        span = slice(FT + i * shard, FT + (i + 1) * shard)
        total = got[0][span].astype(F32)
        for x in got[1:]:
            total = total + x[span].astype(F32)
        out_ref[i, ff_shard:] = total.astype(BF)
    per = groups // TP
    for j in range(TP):
        chip = jnp.bitwise_xor(t, j)
        for i in range(per):
            out_ref[chip * per + i, :ff_shard] = got[j][i * ff_shard : (i + 1) * ff_shard]


def spread_first(x):
    return [x, plane_swap(x, 1), plane_swap(x, 2)]


def spread_pieces(first):
    x, a, b = first
    h = split_at(x.shape[0])
    mine = [x, a, b, plane_swap(a[:h], 2), plane_swap(b[h:], 1)]
    return mine + [core_swap(p) for p in mine]


def spread_out(idx, first, parts, heights=None):
    pieces = first if len(first) == 10 else spread_pieces(first)
    rows, cols = pieces[0].shape
    h = split_at(rows)
    width = cols // parts if parts else cols
    outs = []
    start = 0
    for height in heights or (rows,):
        edges = [start, start + height] + ([h] if start < h < start + height else [])
        q = 16
        for n in range(16, (64 if parts else 256) + 1, 16):
            if all((e - start) % n == 0 for e in edges) and start % n == 0 and h % n == 0:
                q = n
        outs.append(spread_part(idx, pieces, parts, width, start, height, h, q))
        start += height
    return outs


def gather_eight(x):
    n = lax.axis_size("replica")
    blocks = [list(range(i, i + 8)) for i in range(0, n, 8)]
    return lax.all_gather(x, "replica", axis=0, axis_index_groups=blocks if n > 8 else None)


def spread_abs(x, parts, start, height):
    _, rows, cols = x.shape
    width = cols // parts if parts else cols
    q = 16
    for n in range(16, (64 if parts else 128) + 1, 16):
        if height % n == 0 and start % n == 0:
            q = n
    base = start // q

    def kernel(x_ref, out):
        for r in range(8):
            chip, core = r // 2, r % 2
            if parts:
                for p in range(parts):
                    at = (p * TP + chip) * width
                    out[core, :, at : at + width] = x_ref[r, :, p * width : (p + 1) * width].astype(F32)
            else:
                out[:, r * width : (r + 1) * width] = x_ref[r].astype(F32)

    if parts:
        shape, out_spec = (2, height, TP * cols), pl.BlockSpec((2, q, TP * cols), lambda i: (0, i, 0))
    else:
        shape, out_spec = (height, 8 * cols), pl.BlockSpec((q, 8 * cols), lambda i: (i, 0))
    out = pl.pallas_call(
        kernel,
        grid=(height // q,),
        in_specs=[pl.BlockSpec((8, q, cols), lambda i: (0, i + base, 0))],
        out_specs=out_spec,
        out_shape=jax.ShapeDtypeStruct(shape, F32),
        compiler_params=pltpu.CompilerParams(vmem_limit_bytes=VMEM),
        cost_estimate=cost(height * cols * 16e-6),
    )(x)
    return out.reshape(-1, out.shape[-1])


def spread_part(idx, pieces, parts, width, start, height, h, q):
    cols = pieces[0].shape[1]
    rows = pieces[0].shape[0]
    cut, base = h // q, start // q

    def kernel(idx_ref, *refs):
        srcs, out = refs[:-1], refs[-1]
        c, t = idx_ref[0], idx_ref[1]
        i = pl.program_id(0) + base
        for cc in range(2):
            core = jnp.bitwise_xor(c, cc)

            def put(j, value):
                chip = jnp.bitwise_xor(t, j)
                if parts:
                    for p in range(parts):
                        at = pl.multiple_of((p * TP + chip) * width, 128)
                        out[core, :, pl.ds(at, width)] = value[:, p * width : (p + 1) * width].astype(F32)
                else:
                    at = pl.multiple_of((chip * 2 + core) * width, 128)
                    out[:, pl.ds(at, width)] = value.astype(F32)

            for j in range(3):
                put(j, srcs[5 * cc + j][...])

            @pl.when(i < cut)
            def _():
                put(3, srcs[5 * cc + 3][...])

            @pl.when(i >= cut)
            def _():
                put(3, srcs[5 * cc + 4][...])

    most = (rows - h) // q - 1
    full = pl.BlockSpec((q, cols), lambda i: (i + base, 0))
    low = pl.BlockSpec((q, cols), lambda i: (jnp.minimum(i + base, cut - 1), 0))
    high = pl.BlockSpec((q, cols), lambda i: (jnp.clip(i + base - cut, 0, most), 0))
    if parts:
        shape, out_spec = (2, height, TP * cols), pl.BlockSpec((2, q, TP * cols), lambda i: (0, i, 0))
    else:
        shape, out_spec = (height, 8 * cols), pl.BlockSpec((q, 8 * cols), lambda i: (i, 0))
    out = pl.pallas_call(
        kernel,
        grid=(height // q,),
        in_specs=[pl.BlockSpec(memory_space=pltpu.SMEM)] + [full, full, full, low, high] * 2,
        out_specs=out_spec,
        out_shape=jax.ShapeDtypeStruct(shape, F32),
        compiler_params=pltpu.CompilerParams(vmem_limit_bytes=VMEM),
        cost_estimate=cost(0.05),
    )(idx, *pieces)
    return out.reshape(-1, out.shape[-1])


def cost(us):
    return pl.CostEstimate(flops=int(us * 2.2e9), bytes_accessed=0, transcendentals=0)


def block(shape, fixed=False):
    zeros = (0,) * len(shape)
    if fixed:
        return pl.BlockSpec(tuple(shape), lambda i: zeros, pipeline_mode=pl.Buffered(1))
    return pl.BlockSpec((1,) + tuple(shape[1:]), lambda i: (i,) + zeros[1:])


def call(kernel, ins, fixed_ins, outs, fixed_outs=(), us=10, extra=(), scratch=(), held_outs=()):
    count = ins[-1].shape[0]
    out_specs = []
    for i, (shape, _) in enumerate(outs):
        zeros = (0,) * len(shape)
        if i in held_outs:
            spec = pl.BlockSpec(shape, lambda i, z=zeros: z, pipeline_mode=pl.Buffered(1))
        elif i in fixed_outs:
            spec = pl.BlockSpec(shape, lambda i, z=zeros: z)
        else:
            spec = block(shape)
        out_specs.append(spec)
    lead = [pl.BlockSpec(memory_space=pltpu.SMEM)] + [pl.BlockSpec(memory_space=pl.ANY)] * (len(extra) - 1)
    return pl.pallas_call(
        kernel,
        grid=(count,),
        in_specs=(lead if extra else []) + [block(x.shape, i in fixed_ins) for i, x in enumerate(ins)],
        out_specs=out_specs,
        out_shape=[jax.ShapeDtypeStruct(s, d) for s, d in outs],
        scratch_shapes=list(scratch),
        compiler_params=pltpu.CompilerParams(vmem_limit_bytes=VMEM),
        cost_estimate=cost(us),
    )(*extra, *ins)


def mm(a, b, dims=((1,), (0,))):
    return lax.dot_general(a, b, (dims, ((), ())), preferred_element_type=F32)


def body(
    tokens,
    cotangent,
    doc_start,
    norm_gain,
    qkv_weight,
    conv_weight,
    beta_weight,
    head_gain,
    out_weight,
    ffn_gain,
    gate_up_weight,
    down_weight,
):
    groups = lax.axis_size("group")
    r = lax.axis_index("replica") % 8
    g = lax.axis_index("group")
    c, t = r % 2, r // 2
    idx = jnp.stack([c, t, g]).astype(jnp.int32)
    _, length, _ = tokens.shape
    seqs = TP
    ext_len = length + RIM
    shard = D // groups
    half = shard // 2
    ff_shard = FF // groups
    col = D // 8
    tokens = tokens.reshape(length, D)
    cot = cotangent.reshape(length, D)

    def z_pieces(x):
        return [x] + [z_turn(x, s) for s in range(1, groups)]

    def z_abs(x):
        pieces = z_pieces(x)
        return place([((g - s) % groups, piece) for s, piece in enumerate(pieces)], groups)

    def rel(x):
        x = x.reshape(x.shape[:-1] + (groups, 2, half))
        x = jnp.where(c == 0, x, jnp.flip(x, -2))
        return jnp.swapaxes(x, -3, -2).reshape(x.shape[:-3] + (D,))

    def unrel(x):
        x = jnp.swapaxes(x.reshape(x.shape[:-1] + (2, groups, half)), -3, -2)
        x = jnp.where(c == 0, x, jnp.flip(x, -2))
        return x.reshape(x.shape[:-3] + (D,))

    small = jnp.concatenate(
        [
            beta_weight.T,
            jnp.swapaxes(conv_weight.reshape(3, shard, CONV), 1, 2).reshape(3 * CONV, shard),
            ffn_gain.reshape(1, shard),
            norm_gain.reshape(1, shard),
            jnp.zeros((2, shard), BF),
        ],
        axis=0,
    )
    rim = z_shift(tokens[length - RIM :], 1)
    small = z_abs(small)
    gain_in = small[:, HEADS + 3 * CONV + 1].reshape(1, D).astype(F32)
    gain_mid = small[:, HEADS + 3 * CONV].reshape(1, D).astype(F32)
    beta_full = jnp.swapaxes(small[:, :HEADS], 0, 1).reshape(HEADS, D)
    beta_t = jnp.pad(rel(lax.dynamic_slice(beta_full, (t * HT, 0), (HT, D))).T, ((0, 0), (0, HD - HT)))
    conv_full = small[:, HEADS : HEADS + 3 * CONV].reshape(groups * 3, CONV, shard)
    conv_full = jnp.swapaxes(conv_full, 0, 1).reshape(CONV, 3, TP, DT)
    taps = jnp.swapaxes(pick(conv_full, t, 2), 0, 1).astype(F32)
    gain_head = head_gain.astype(F32).reshape(1, HD)
    doc_rel = doc_start.reshape(1, length) - g * length
    docs = jnp.concatenate(
        [doc_rel] + [plane_swap(doc_rel, j) for j in (1, 2, 3)], axis=0
    ).reshape(seqs, length, 1)
    cot_x, cot_y = plane_swap(cot, 1), plane_swap(cot, 2)
    qkv_weight, small, rim = lax.optimization_barrier((qkv_weight, small, rim))

    (normed_ext,) = whole_call(
        functools.partial(norm_kernel, groups), idx, [rim, tokens, gain_in], [((ext_len, D), BF)]
    )
    normed_pieces = plane_copies(normed_ext)

    piece = jnp.concatenate(
        [lax.dynamic_slice(qkv_weight, (c * half, j * D + t * DT), (half, DT)) for j in range(3)], axis=1
    )
    qkv_pieces = z_pieces(piece)
    qkv_late = qkv_pieces
    qkv_pieces = qkv_pieces + [core_swap(p) for p in qkv_pieces]

    h = split_at(length)
    cot_pieces = [cot, cot_x, cot_y, plane_swap(cot_x[:h], 2), plane_swap(cot_y[h:], 1)]

    piece = jnp.concatenate(
        [
            lax.dynamic_slice(out_weight, (0, r * col), (shard, col)),
            lax.dynamic_slice(down_weight, (0, r * col), (ff_shard, col)),
        ],
        axis=0,
    )
    both = lax.all_gather(after(piece, *qkv_late), "group", axis=0)

    normed_pieces[0] = after(normed_pieces[0], *cot_pieces[:3])

    wide = (seqs, length, DT)
    square = (seqs, HT, HD, HD)
    (
        queries, key_rows, value_rows, inverse, u0, w, move, free, projected, rates, normed_all, qkv,
    ) = call(
        functools.partial(front_kernel, groups),
        [beta_t, taps, docs],
        (0, 1),
        [
            (wide, BF),
            (wide, BF),
            (wide, BF),
            ((seqs, HT, length, length), BF),
            (wide, F32),
            (wide, BF),
            (square, BF),
            (square, F32),
            ((seqs, ext_len, 3 * DT), BF),
            ((seqs, length, HD), F32),
            ((seqs * ext_len, D), BF),
            ((D, 3 * DT), BF),
        ],
        us=40,
        extra=[idx, *normed_pieces, *qkv_pieces],
        scratch=[pltpu.SemaphoreType.DMA((5,)), pltpu.SemaphoreType.DMA((2 * groups,))],
        held_outs=(10, 11),
    )
    piece = jnp.concatenate(
        [
            lax.dynamic_slice(gate_up_weight, (c * half, j * FF + t * FT), (half, FT))
            for j in range(2)
        ],
        axis=1,
    )
    gate_up = lax.all_gather(after(piece, free), "group", axis=0, tiled=True)

    state = jnp.zeros(square, BF)
    for hop in range(groups - 1):
        leaving = jnp.einsum("shij,shjk->shik", move, state, preferred_element_type=F32) + free
        if hop == groups - 2:
            leaving = after(leaving, *downs, *outs)
        state = z_shift(leaving.astype(BF), 1)
        if hop == 0:
            both = after(both, free)
            part = both[:, shard:].reshape(TP, FT, col)
            downs = plane_trade([pick(part, t ^ j) for j in range(TP)])
            outs = both[:, :shard].reshape(D, col)
            outs = plane_copies(outs)
    outs = outs + [core_swap(p) for p in outs]
    downs = downs + [core_swap(p) for p in downs]
    normed, head_out, update = call(
        out_kernel,
        [gain_head, queries, key_rows, u0, w, state, docs],
        (0,),
        [(wide, BF), (wide, F32), (wide, BF)],
        us=6,
    )

    def plan(ref):
        moves = []
        for cc in range(2):
            for j in range(TP):
                at = ((ref[1] ^ j) * 2 + (ref[0] ^ cc)) * col
                for b in range(TP):
                    n, first = (j, b) if j < 3 else ((3, b) if b < 2 else (4, b - 2))
                    moves.append(
                        (
                            5 * cc + n,
                            pl.ds(first * DT, DT),
                            (
                                pl.ds(pl.multiple_of((ref[1] ^ b) * DT, DT), DT),
                                pl.ds(pl.multiple_of(at, 128), col),
                            ),
                        )
                    )
        return moves

    out_w = assemble(idx, outs, plan, (D, D))

    heads = plane_trade([normed[j] for j in range(TP)])
    middle, normed_mid = whole_call(
        functools.partial(mid_kernel, groups),
        idx,
        heads + [out_w, tokens, gain_mid],
        [((length, D), F32), ((length, D), BF)],
        us=10,
    )
    mid_pieces = plane_copies(normed_mid)
    gate_ups = [gate_up, core_swap(after(gate_up, mid_pieces[1], mid_pieces[2]))]

    hidden, grad_gate_up, mid_part, cot_away, cot_mine, mid_all, down = call(
        ffn_kernel,
        [docs],
        (),
        [
            ((seqs, length, FT), BF),
            ((seqs, length, 2 * FT), BF),
            ((seqs, length, D), BF),
            ((seqs, length, D // 2), BF),
            ((seqs, length, D // 2), BF),
            ((seqs * length, D), BF),
            ((FT, D), BF),
        ],
        us=45,
        extra=[idx, *mid_pieces, *cot_pieces, *gate_ups, *downs],
        scratch=[pltpu.VMEM((seqs * length, D), BF), pltpu.VMEM((D, 2 * FT), BF)]
        + [pltpu.SemaphoreType.DMA((n,)) for n in (5, 5, 2, 8)],
        held_outs=(5, 6),
    )
    hidden = hidden.reshape(-1, FT)
    grad_gate_up = grad_gate_up.reshape(-1, 2 * FT)
    def two_halves(left, right):
        away = mm(left[:, groups * half :], right, TN).astype(BF)
        mine = mm(left[:, : groups * half], right, TN)
        return (mine + core_swap(away).astype(F32)).astype(BF).reshape(groups, half, -1)

    def two_columns(left, away, mine):
        away = mm(left, away, TN).astype(BF)
        mine = mm(left, mine, TN)
        return (mine + core_swap(away).astype(F32)).astype(BF)

    def z_sum(x, *others):
        total = pick(x, g).astype(F32)
        for s in range(1, groups):
            total = total + after(z_turn(pick(x, (g + s) % groups), s), *others).astype(F32)
        return total

    parts = plane_parts([mid_part[j] for j in range(TP)])
    gate_sums = [two_halves(mid_all, grad_gate_up[:, i * FT : (i + 1) * FT]) for i in range(2)]
    down_sum = two_columns(hidden, cot_away.reshape(-1, D // 2), cot_mine.reshape(-1, D // 2))
    first_sum = far_sum(lax.psum_scatter(gate_sums[0], "group", scatter_dimension=0)).astype(BF)
    parts, second_sum, down_sum = lax.optimization_barrier((parts, gate_sums[1], down_sum))
    second_sum = far_sum(lax.psum_scatter(second_sum, "group", scatter_dimension=0)).astype(BF)
    grad_middle, branch_away, branch_mine, *dheads, ffn_gain_part = whole_call(
        functools.partial(mid_back_kernel, groups),
        idx,
        parts + [middle.reshape(length, D), cot, gain_mid, out_w],
        [((length, D), F32)]
        + [((length, D // 2), BF)] * 2
        + [((length, DT), BF)] * TP
        + [((1, D), F32)],
        us=13,
        scratch=[pltpu.VMEM((length, D), BF)],
    )
    dnormed = jnp.stack(plane_trade(dheads))

    normed_abs = jnp.swapaxes(
        place([(t ^ j, heads[j]) for j in range(TP)], TP), 0, 1
    ).reshape(length, D)
    out_sum = two_columns(normed_abs, branch_away, branch_mine)
    both = [
        jnp.concatenate([x[:, j * col : (j + 1) * col] for x in (down_sum, out_sum)], axis=0)
        for j in range(TP)
    ]
    dnormed = after(dnormed, first_sum, *both)
    both = plane_trade(both)

    grad_out, y0, z, local, head_part = call(
        back_kernel,
        [gain_head, dnormed, head_out, queries, key_rows, inverse, rates, docs],
        (0,),
        [(wide, BF), (wide, F32), (wide, BF), (square, F32), ((8, HD), F32)],
        (4,),
        us=12,
    )


    later = jnp.zeros(square, BF)
    for hop in range(groups - 1):
        leaving = jnp.einsum("shji,shjk->shik", move, later, preferred_element_type=F32) + local
        later = z_shift(leaving.astype(BF), -1)

    (both_sum,) = whole_call(
        functools.partial(join_kernel, groups), idx, both, [((groups, shard + ff_shard, col), BF)]
    )
    later = after(later, both_sum, second_sum)
    gate_sum = jnp.concatenate([first_sum, second_sum], axis=1)
    both_sum = lax.psum_scatter(both_sum, "group", scatter_dimension=0)
    gate_pieces = spread_first(gate_sum)
    grad_proj, grad_logit, in_part, conv_part = call(
        grad_kernel,
        [
            taps, qkv, beta_t, projected, docs, rates, queries, key_rows, value_rows, state, update, grad_out,
            y0, z, later,
        ],
        (0, 1, 2),
        [
            ((seqs, ext_len, 3 * DT), BF),
            ((seqs, ext_len, HD), BF),
            ((seqs, ext_len, D), BF),
            ((3, CONV, DT), F32),
        ],
        (3,),
        us=44,
    )
    qkv_sum = two_halves(normed_all, grad_proj.reshape(-1, 3 * DT))
    qkv_mine = qkv_sum
    gate_pieces = spread_pieces([after(p, qkv_sum) for p in gate_pieces])
    rim = z_shift(in_part[:, :RIM], -1)
    in_part = after(in_part[:, RIM:], qkv_sum)
    qkv_sum = z_sum(qkv_sum)
    ends_in = (in_part[:, length - RIM :].astype(F32) + rim.astype(F32)).astype(BF)
    in_part = jnp.concatenate([in_part[:, : length - RIM], ends_in], axis=1)
    parts = plane_parts([in_part[j] for j in range(TP)])
    parts[0] = after(parts[0], qkv_sum)
    input_grad, norm_gain_part = whole_call(
        functools.partial(in_back_kernel, groups),
        idx,
        parts + [tokens, grad_middle, gain_in],
        [((length, D), F32), ((1, D), F32)],
        us=0.05,
    )
    out_part = mm(after(hidden, qkv_mine), down).astype(BF).reshape(TP, length, D)
    output = (middle + plane_sum([out_part[j] for j in range(TP)])).astype(BF)

    beta_part = mm(grad_logit.reshape(-1, HD), normed_all, TN)[:HT]
    beta_all = lax.dynamic_update_slice(jnp.zeros((HEADS, D), F32), unrel(beta_part), (t * HT, 0))
    conv_all = lax.dynamic_update_slice(
        jnp.zeros((CONV, 3, TP, DT), F32), jnp.swapaxes(conv_part, 0, 1)[:, :, None], (0, 0, t, 0)
    )
    conv_all = jnp.swapaxes(conv_all.reshape(CONV, groups * 3, shard), 0, 1)
    pack = jnp.concatenate(
        [
            jnp.swapaxes(beta_all.reshape(HEADS, groups, shard), 0, 1),
            conv_all.reshape(groups, 3 * CONV, shard),
            norm_gain_part.reshape(groups, 1, shard),
            ffn_gain_part.reshape(groups, 1, shard),
            jnp.broadcast_to(jnp.pad(head_part[:1], ((0, 0), (0, shard - HD))), (groups, 1, shard)),
            jnp.zeros((groups, 1, shard), F32),
        ],
        axis=1,
    )
    pack = pack + core_swap(pack)
    pack = pack + plane_swap(pack, 1)
    pack = pack + plane_swap(pack, 2)

    (gate_up_grad,) = spread_out(idx, gate_pieces, 2)

    total = far_sum(z_sum(after(pack, qkv_sum)))
    both_pieces = [after(p, qkv_sum) for p in spread_first(far_sum(both_sum).astype(BF))]
    qkv_pieces = [after(p, gate_up_grad, output) for p in spread_first(far_sum(qkv_sum).astype(BF))]
    qkv_pieces = spread_pieces(qkv_pieces)
    down_grad, out_grad = spread_out(idx, both_pieces, 0, (ff_shard, shard))
    qkv_pieces[0] = after(qkv_pieces[0], total, out_grad, down_grad)
    (qkv_grad,) = spread_out(idx, qkv_pieces, 3)
    beta_grad = total[:HEADS].T
    conv_grad = jnp.swapaxes(total[HEADS : HEADS + 3 * CONV].reshape(3, CONV, shard), 1, 2)
    at = HEADS + 3 * CONV
    return (
        output.reshape(1, length, D),
        input_grad.reshape(1, length, D),
        total[at],
        qkv_grad,
        conv_grad.reshape(-1, CONV),
        beta_grad,
        total[at + 2, :HD],
        out_grad,
        total[at + 1],
        gate_up_grad,
        down_grad,
    )


def solution(mesh):
    rows = P("replica", "group", None)
    shard = P("group", None)
    return jax.shard_map(
        body,
        mesh=mesh,
        in_specs=(
            rows, rows, P("replica", "group"), P("group"), shard, shard, shard, P(), shard, P("group"), shard, shard,
        ),
        out_specs=(
            rows, rows, P("group"), shard, shard, shard, P(), shard, P("group"), shard, shard,
        ),
        check_vma=False,
    )
```
